512 devices in a mesh: seq: 128 (over x, z, y_hi), dp: 4 (over y_lo, core).
Axes of the slice: x: 4, y: 8 (y_hi: 4, y_lo: 2; y = y_hi * 2 + y_lo), z: 8, core: 2. Of those that a mesh axis runs over, the one named last changes fastest.
Arguments:
- queries: bfloat16 [768, 32768], P('dp', 'seq'), may hold values from -9.5 to 9.5
- keys: bfloat16 [768, 32768], P('dp', 'seq'), may hold values from -4.5 to 4.5
- values: bfloat16 [768, 32768], P('dp', 'seq'), may hold values from -6 to 6
- grad_out: bfloat16 [768, 32768], P('dp', 'seq'), may hold values from -24 to 24
- out_weight: bfloat16 [768, 768], P('dp'), may hold values from -0.21875 to 0.21875
- offsets: int32 [12], P('dp'), may hold values from 0 to 127
Outputs:
- grad_queries: bfloat16 [768, 32768], P('dp', 'seq')
- grad_keys: bfloat16 [768, 32768], P('dp', 'seq')
- grad_values: bfloat16 [768, 32768], P('dp', 'seq')
- grad_weight: float32 [768, 768], P('dp')
The draws below stay inside these ranges and needn't reach their ends.
All inputs are finite; a program needn't handle non-finite values.
Results may differ from the reference program's by a relative error of at most 0.012.
The reference program's roundings to bfloat16 on the way count: a program that leaves them out, or rounds other values in their place, can miss the bound.
Values may be sent and summed in bfloat16 or wider, within the bound.
No kernel may reach another device: no remote copies, remote signals or barrier semaphores. Data moves between devices by JAX's collectives and lax.ppermute only.
A program may use at most 64 MiB of HBM per device.

```python
import jax
import jax.numpy as jnp
from jax import lax

HEADS = 12
HEAD_DIM = 64
TOK_DEV = 256
SEG_A = 256
RB = 2
RC = 16
RE = 128
TOKENS = 32768


def head_shifts(key):
    base_key = jax.random.fold_in(key, 11)
    first_key, second_key, third_key = jax.random.split(base_key, 3)
    drawn = jax.random.randint(first_key, (HEADS,), 0, RE)
    low_head = jax.random.randint(second_key, (), 0, HEADS)
    high_head = (low_head + 1 + jax.random.randint(third_key, (), 0, HEADS - 1)) % HEADS
    head_ids = jnp.arange(HEADS)
    drawn = jnp.where(head_ids == low_head, 0, drawn)
    return jnp.where(head_ids == high_head, RE - 1, drawn).astype(jnp.int32)


def draw_offsets(key, part):
    return head_shifts(key)


def draw_queries(key, part):
    key = jax.random.fold_in(key, 3)
    drawn_key = jax.random.fold_in(key, 0)
    entries = 1.5 * jax.random.truncated_normal(drawn_key, -4.0, 4.0, (TOKENS, HEADS * HEAD_DIM), jnp.float32)
    return entries.T.astype(jnp.bfloat16)


def draw_keys(key, part):
    key = jax.random.fold_in(key, 5)
    entries = jax.random.truncated_normal(key, -4.0, 4.0, (TOKENS, HEADS * HEAD_DIM), jnp.float32)
    return entries.T.astype(jnp.bfloat16)


def levels(key, dims, cuts, low, top_value):
    def one(dim, blocks):
        heights = jax.random.uniform(jax.random.fold_in(jax.random.fold_in(key, 6), dim), (blocks,), jnp.float32, low / len(cuts), top_value / len(cuts))
        return jnp.repeat(jnp.exp(heights), dims[dim] // blocks).reshape((-1,) + (1,) * (len(dims) - dim - 1))

    gain = one(*cuts[0])
    for cut in cuts[1:]:
        gain = gain * one(*cut)
    return gain


def gaussian(own_key, dims, deviation, limit, cuts=(), held_as=jnp.bfloat16):
    result = deviation * jax.random.normal(own_key, dims, jnp.float32)
    if cuts:
        result = result * levels(own_key, dims, cuts, -0.22, 0.18)
    return jnp.clip(result, -limit, limit).astype(held_as)


def setup_inputs(seed: int = 0) -> dict:
    seeds = jax.random.split(jax.random.key(seed), 7)
    queries = draw_queries(jax.random.fold_in(seeds[6], 71), 0)
    keys = draw_keys(jax.random.fold_in(seeds[6], 71), 0)
    values = gaussian(seeds[2], (HEADS * HEAD_DIM, TOKENS), 1.0, 6.0, ((0, 4), (1, 128)))
    grad_out = gaussian(seeds[3], (HEADS * HEAD_DIM, TOKENS), 4.0, 24.0, ((0, 4), (1, 128)))
    out_weight = gaussian(seeds[4], (HEADS * HEAD_DIM, HEADS * HEAD_DIM), (HEADS * HEAD_DIM) ** -0.5, 0.21875, ((0, 4),))
    offsets = draw_offsets(jax.random.fold_in(seeds[6], 71), 0)
    return dict(queries=queries, keys=keys, values=values, grad_out=grad_out, out_weight=out_weight, offsets=offsets)


WEIGHT_SCALE = 0.03125


def select_rows(source, seg_width, stride, shift):
    seg_count = source.shape[0] // seg_width
    shaped = source.reshape((seg_count, seg_width // stride, stride) + source.shape[1:])
    return lax.dynamic_index_in_dim(shaped, (shift % stride).astype(jnp.int32), 2, keepdims=False)


def spread_rows(picked, stride, shift):
    shape = picked.shape[:2] + (stride,) + picked.shape[2:]
    empty = jnp.zeros(shape, picked.dtype)
    placed = lax.dynamic_update_slice_in_dim(empty, jnp.expand_dims(picked, 2), (shift % stride).astype(jnp.int32), 2)
    return placed.reshape((shape[0] * shape[1] * stride,) + picked.shape[2:])


def head_pass(packed):
    query_head, key_head, value_head, dout_head, shift = packed
    layout = ((SEG_A, 1), (TOK_DEV, RB), (2 * TOK_DEV, RC), (TOKENS, RE))
    score_scale = HEAD_DIM ** -0.5
    picked = []
    for seg_width, stride in layout:
        level = tuple(select_rows(source, seg_width, stride, shift).astype(jnp.float32) for source in (query_head, key_head, value_head, dout_head))
        scores = jnp.einsum('sqd,skd->sqk', level[0], level[1]) * score_scale
        row_max = jnp.max(scores, axis=-1)
        log_mass = row_max + jnp.log(jnp.sum(jnp.exp(scores - row_max[..., None]), axis=-1))
        picked.append((seg_width, stride, level, scores, log_mass))
    base_stat = picked[0][4].reshape(-1)
    peak_stat = base_stat
    for seg_width, stride, level, scores, log_mass in picked[1:]:
        lifted = log_mass - select_rows(base_stat, seg_width, stride, shift)
        peak_stat = jnp.maximum(peak_stat, base_stat + spread_rows(lifted, stride, shift))
    total_mass = jnp.zeros((TOKENS,), jnp.float32)
    for seg_width, stride, level, scores, log_mass in picked:
        total_mass = total_mass + spread_rows(jnp.exp(log_mass - select_rows(peak_stat, seg_width, stride, shift)), stride, shift)
    normalizer = peak_stat + jnp.log(total_mass)
    attended = jnp.zeros((TOKENS, HEAD_DIM), jnp.float32)
    prob_sets = []
    for seg_width, stride, level, scores, log_mass in picked:
        probs = jnp.exp(scores - select_rows(normalizer, seg_width, stride, shift)[..., None])
        probs_low = lax.optimization_barrier(probs.astype(jnp.bfloat16)).astype(jnp.float32)
        prob_sets.append((probs, probs_low))
        attended = attended + spread_rows(jnp.einsum('sqk,skd->sqd', probs_low, level[2]), stride, shift)
    delta_stat = jnp.sum(dout_head.astype(jnp.float32) * attended, axis=-1)
    grad_query = jnp.zeros((TOKENS, HEAD_DIM), jnp.float32)
    grad_key = jnp.zeros((TOKENS, HEAD_DIM), jnp.float32)
    grad_value = jnp.zeros((TOKENS, HEAD_DIM), jnp.float32)
    for (seg_width, stride, level, scores, log_mass), (probs, probs_low) in zip(picked, prob_sets):
        row_delta = select_rows(delta_stat, seg_width, stride, shift)[..., None]
        grad_probs = jnp.einsum('sqd,skd->sqk', level[3], level[2])
        grad_scores = lax.optimization_barrier((probs * (grad_probs - row_delta)).astype(jnp.bfloat16)).astype(jnp.float32)
        grad_query = grad_query + spread_rows(jnp.einsum('sqk,skd->sqd', grad_scores, level[1]), stride, shift)
        grad_key = grad_key + spread_rows(jnp.einsum('sqk,sqd->skd', grad_scores, level[0]), stride, shift)
        grad_value = grad_value + spread_rows(jnp.einsum('sqk,sqd->skd', probs_low, level[3]), stride, shift)
    return ((grad_query * score_scale).astype(jnp.bfloat16), (grad_key * score_scale).astype(jnp.bfloat16),
            grad_value.astype(jnp.bfloat16), attended.astype(jnp.bfloat16))


def by_head(source):
    return source.reshape(HEADS, HEAD_DIM, TOKENS).transpose(0, 2, 1)


def by_feature(source):
    return source.transpose(0, 2, 1).reshape(HEADS * HEAD_DIM, TOKENS)


def reference(queries, keys, values, grad_out, out_weight, offsets):
    dout = lax.optimization_barrier(jnp.dot(out_weight, grad_out, preferred_element_type=jnp.float32).astype(jnp.bfloat16))
    results = lax.map(head_pass, (by_head(queries), by_head(keys), by_head(values), by_head(dout), offsets))
    grad_queries = by_feature(results[0])
    grad_keys = by_feature(results[1])
    grad_values = by_feature(results[2])
    attended_low = by_feature(results[3])
    grad_weight = jnp.dot(attended_low, grad_out.T, preferred_element_type=jnp.float32) * WEIGHT_SCALE
    return grad_queries, grad_keys, grad_values, grad_weight
```

```python
import jax
import jax.numpy as jnp
from jax import lax
from jax.sharding import PartitionSpec as P

HEAD_DIM = 64
SEG_A = 256
RB = 2
RC = 16
RE = 128


WEIGHT_SCALE = 0.03125


def swapped(value, axis, distance):
    return lax.ppermute(value, axis, [(i, i ^ 1 << distance) for i in range(lax.axis_size(axis))])


def exchange(pieces, axis):
    return lax.all_to_all(pieces, axis, 0, 0, tiled=True)


def gather_direct(value, axis):
    pieces = jnp.broadcast_to(value.reshape(1, -1), (lax.axis_size(axis), value.size))
    return exchange(pieces, axis)


def pick_rows(source, seg_width, stride, shifts):
    seg_count = source.shape[0] // seg_width
    shaped = source.reshape((seg_count, seg_width // stride, stride) + source.shape[1:])
    if stride == 1:
        return shaped[:, :, 0]
    chooser = jnp.arange(stride)[:, None] == (shifts % stride)[None, :]
    chooser = chooser.reshape((1, 1, stride, shifts.shape[0]) + (1,) * (source.ndim - 2)).astype(
        source.dtype
    )
    return jnp.sum(shaped * chooser, axis=2)


def spread_rows(picked, stride, shifts):
    if stride == 1:
        return picked.reshape((-1,) + picked.shape[2:])
    chooser = jnp.arange(stride)[:, None] == (shifts % stride)[None, :]
    chooser = chooser.reshape((1, 1, stride, shifts.shape[0]) + (1,) * (picked.ndim - 3)).astype(
        picked.dtype
    )
    placed = jnp.expand_dims(picked, 2) * chooser
    return placed.reshape((-1,) + picked.shape[2:])


def local(queries, keys, values, grad_out, out_weight, offsets):
    row_count = queries.shape[1]
    heads_here = offsets.shape[0]
    score_scale = HEAD_DIM ** (-0.5)
    full_grad = lax.all_gather(grad_out, "dp", axis=0, tiled=True)
    dout_flat = jnp.dot(out_weight, full_grad, preferred_element_type=jnp.float32).astype(
        jnp.bfloat16
    )
    head_shape = (row_count, heads_here, HEAD_DIM)
    sources = tuple(
        (jnp.transpose(source).reshape(head_shape) for source in (queries, keys, values, dout_flat))
    )
    layout = ((SEG_A, 1), (row_count, RB), (row_count, RC), (row_count, RE))
    selected = [
        tuple((pick_rows(source, seg_width, stride, offsets) for source in sources))
        for seg_width, stride in layout
    ]
    near_query, near_key, near_value, near_dout = selected[2]
    partner_key, partner_value = swapped((near_key[0], near_value[0]), "seq", 0)
    pair_keys = jnp.concatenate([near_key, partner_key[None]], axis=1)
    pair_values = jnp.concatenate([near_value, partner_value[None]], axis=1)
    far_query, far_key, far_value, far_dout = selected[3]
    far_count = far_key.shape[1]
    far_pairs = gather_direct(jnp.stack([far_key[0], far_value[0]]), "seq")
    far_pairs = far_pairs.reshape((-1, 2, far_count, heads_here, HEAD_DIM))
    all_key = far_pairs[:, 0].reshape((-1, heads_here, HEAD_DIM))
    all_value = far_pairs[:, 1].reshape((-1, heads_here, HEAD_DIM))
    levels = (
        selected[0],
        selected[1],
        (near_query, pair_keys, pair_values, near_dout),
        (far_query, all_key[None], all_value[None], far_dout),
    )
    score_sets = []
    log_masses = []
    for level_query, level_key, level_value, level_dout in levels:
        scores = (
            jnp.einsum(
                "sqhd,skhd->shqk", level_query, level_key, preferred_element_type=jnp.float32
            )
            * score_scale
        )
        row_max = jnp.max(scores, axis=-1)
        log_mass = row_max + jnp.log(jnp.sum(jnp.exp(scores - row_max[..., None]), axis=-1))
        score_sets.append(scores)
        log_masses.append(jnp.swapaxes(log_mass, 1, 2))
    base_stat = spread_rows(log_masses[0], 1, offsets)
    peak_stat = base_stat
    for (seg_width, stride), log_mass in zip(layout[1:], log_masses[1:]):
        lifted = log_mass - pick_rows(base_stat, seg_width, stride, offsets)
        peak_stat = jnp.maximum(peak_stat, base_stat + spread_rows(lifted, stride, offsets))
    total_mass = jnp.zeros_like(base_stat)
    for (seg_width, stride), log_mass in zip(layout, log_masses):
        total_mass = total_mass + spread_rows(
            jnp.exp(log_mass - pick_rows(peak_stat, seg_width, stride, offsets)), stride, offsets
        )
    normalizer = peak_stat + jnp.log(total_mass)
    prob_sets = []
    attended = jnp.zeros(head_shape, jnp.float32)
    for (seg_width, stride), level, scores in zip(layout, levels, score_sets):
        row_norm = jnp.swapaxes(pick_rows(normalizer, seg_width, stride, offsets), 1, 2)
        probs = jnp.exp(scores - row_norm[..., None])
        probs_low = probs.astype(jnp.bfloat16)
        prob_sets.append((probs, probs_low))
        attended = attended + spread_rows(
            jnp.einsum("shqk,skhd->sqhd", probs_low, level[2], preferred_element_type=jnp.float32),
            stride,
            offsets,
        )
    delta_stat = jnp.sum(sources[3].astype(jnp.float32) * attended, axis=-1)
    grad_query = jnp.zeros(head_shape, jnp.float32)
    grad_key = jnp.zeros(head_shape, jnp.float32)
    grad_value = jnp.zeros(head_shape, jnp.float32)
    for level_index in range(4):
        seg_width, stride = layout[level_index]
        level_query, level_key, level_value, level_dout = levels[level_index]
        probs, probs_low = prob_sets[level_index]
        row_delta = jnp.swapaxes(pick_rows(delta_stat, seg_width, stride, offsets), 1, 2)[..., None]
        grad_probs = jnp.einsum(
            "sqhd,skhd->shqk", level_dout, level_value, preferred_element_type=jnp.float32
        )
        grad_scores = (probs * (grad_probs - row_delta)).astype(jnp.bfloat16)
        grad_query = grad_query + spread_rows(
            jnp.einsum(
                "shqk,skhd->sqhd", grad_scores, level_key, preferred_element_type=jnp.float32
            ),
            stride,
            offsets,
        )
        if level_index == 3:
            key_part = jnp.einsum(
                "shqk,sqhd->skhd", grad_scores, level_query, preferred_element_type=jnp.float32
            )
            value_part = jnp.einsum(
                "shqk,sqhd->skhd", probs_low, level_dout, preferred_element_type=jnp.float32
            )
            shards = lax.axis_size("seq")
            parts = jnp.concatenate(
                [key_part[0].reshape(shards, -1), value_part[0].reshape(shards, -1)], axis=1
            )
            own = jnp.sum(exchange(parts, "seq"), axis=0)
            own = own.reshape((2, far_count, heads_here, HEAD_DIM))
            key_own, value_own = own[0], own[1]
            grad_key = grad_key + spread_rows(key_own[None], stride, offsets)
            grad_value = grad_value + spread_rows(value_own[None], stride, offsets)
        else:
            key_part = jnp.einsum(
                "shqk,sqhd->skhd", grad_scores, level_query, preferred_element_type=jnp.float32
            )
            value_part = jnp.einsum(
                "shqk,sqhd->skhd", probs_low, level_dout, preferred_element_type=jnp.float32
            )
            if level_index == 2:
                half_keys = key_part.shape[1] // 2
                back_key, back_value = swapped(
                    (key_part[0, half_keys:], value_part[0, half_keys:]), "seq", 0
                )
                key_part = key_part[:, :half_keys] + back_key[None]
                value_part = value_part[:, :half_keys] + back_value[None]
            grad_key = grad_key + spread_rows(key_part, stride, offsets)
            grad_value = grad_value + spread_rows(value_part, stride, offsets)
    flat_shape = (row_count, heads_here * HEAD_DIM)
    grad_queries = jnp.transpose(
        (grad_query * score_scale).astype(jnp.bfloat16).reshape(flat_shape)
    )
    grad_keys = jnp.transpose((grad_key * score_scale).astype(jnp.bfloat16).reshape(flat_shape))
    grad_values = jnp.transpose(grad_value.astype(jnp.bfloat16).reshape(flat_shape))
    attended_low = attended.astype(jnp.bfloat16).reshape(flat_shape)
    partial_weight = (
        lax.dot_general(
            attended_low, full_grad, (((0,), (1,)), ((), ())), preferred_element_type=jnp.float32
        )
        * WEIGHT_SCALE
    )
    pieces = partial_weight.astype(jnp.bfloat16).reshape(lax.axis_size("seq"), -1)
    own_piece = jnp.sum(exchange(pieces, "seq").astype(jnp.float32), axis=0)
    grad_weight = gather_direct(own_piece.astype(jnp.bfloat16), "seq")
    grad_weight = grad_weight.astype(jnp.float32).reshape(partial_weight.shape)
    return (grad_queries, grad_keys, grad_values, grad_weight)


def solution(mesh):
    return jax.shard_map(
        local,
        mesh=mesh,
        in_specs=(
            P("dp", "seq"),
            P("dp", "seq"),
            P("dp", "seq"),
            P("dp", "seq"),
            P("dp", None),
            P("dp"),
        ),
        out_specs=(P("dp", "seq"), P("dp", "seq"), P("dp", "seq"), P("dp", None)),
        check_vma=False,
    )
```

```python
import jax
import jax.numpy as jnp
from jax import lax
from jax.experimental import pallas as pl
from jax.experimental.pallas import tpu as pltpu
from jax.sharding import Mesh
from jax.sharding import PartitionSpec as P

HEAD_DIM = 64
TOKENS_HERE = 256
RB = 2
RC = 16
RE = 128
NEAR = TOKENS_HERE // RC
SCORE_SCALE = HEAD_DIM ** (-0.5)
WEIGHT_SCALE = 0.03125

PLANES = 4
LANES = 128
GAP = 16
SLOT = HEAD_DIM + GAP

F32 = jnp.float32
BF16 = jnp.bfloat16


def mm(left, right, left_dim, right_dim):
    return lax.dot_general(
        left, right, (((left_dim,), (right_dim,)), ((), ())), preferred_element_type=F32
    )


def iota(shape, dim):
    return lax.broadcasted_iota(jnp.int32, shape, dim)


def one_hot(condition):
    return jnp.where(condition, 1.0, 0.0).astype(BF16)


def same_class(position, offset, stride):
    return (position & (stride - 1)) == (offset & (stride - 1))


def near_chooser(offset):
    shape = (NEAR, TOKENS_HERE)
    return one_hot(iota(shape, 1) == RC * iota(shape, 0) + (offset & (RC - 1)))


def far_chooser(offset, pair):
    shape = (GAP, TOKENS_HERE)
    row = iota(shape, 0)
    hit = iota(shape, 1) == RE * (row & 1) + offset
    return one_hot(hit & ((row >> 1) == pair))


def split3(value):
    high = value.astype(BF16).astype(F32)
    rest = value - high
    middle = rest.astype(BF16).astype(F32)
    return high, middle, rest - middle


def lay_stats(shape, dim, start, values):
    place = iota(shape, dim) - start
    out = jnp.zeros(shape, F32)
    for index, value in enumerate(values):
        for part_index, part in enumerate(split3(value)):
            out = jnp.where(place == 3 * index + part_index, part, out)
    return out


def take_stat(rows, index):
    place = iota(rows.shape, 1) - HEAD_DIM - 3 * index
    return jnp.sum(jnp.where((place >= 0) & (place < 3), rows, 0.0), axis=1, keepdims=True)


def left_half(rows):
    return jnp.where(iota(rows.shape, 1) < HEAD_DIM, rows.astype(F32), 0.0).astype(BF16)


def right_half(rows):
    return jnp.where(iota(rows.shape, 1) >= HEAD_DIM, rows.astype(F32), 0.0).astype(BF16)


def near_kernel(offset_ref, key_ref, value_ref, near_ref):
    for head in range(key_ref.shape[0] // HEAD_DIM):
        rows = slice(head * HEAD_DIM, (head + 1) * HEAD_DIM)
        both = jnp.concatenate([key_ref[rows], value_ref[rows]], axis=0)
        picked = mm(near_chooser(offset_ref[head]), both, 1, 1)
        near_ref[head * NEAR : (head + 1) * NEAR, :] = picked.astype(BF16)


def local_kernel(
    offset_ref,
    query_ref,
    key_ref,
    value_ref,
    grad_ref,
    weight_ref,
    near_ref,
    slots_ref,
    back_ref,
    mine_ref,
    grad_query_ref,
    grad_key_ref,
    grad_value_ref,
):
    heads = query_ref.shape[0] // HEAD_DIM
    tiles = grad_ref.shape[0] // LANES
    grad = grad_ref[...]
    dout = mm(weight_ref[...], grad, 1, 0).astype(BF16)
    blank = jnp.zeros((HEAD_DIM, TOKENS_HERE), BF16)
    key_pos = iota((TOKENS_HERE, TOKENS_HERE), 0)
    query_pos = iota((TOKENS_HERE, TOKENS_HERE), 1)
    query_row = iota((1, TOKENS_HERE), 1)
    partner_far = jnp.zeros((GAP, LANES), F32)
    for head in range(heads):
        offset = offset_ref[head]
        rows = slice(head * HEAD_DIM, (head + 1) * HEAD_DIM)
        near_rows = slice(head * NEAR, (head + 1) * NEAR)
        query, key, value = query_ref[rows], key_ref[rows], value_ref[rows]
        near = near_ref[near_rows]
        dout_head = dout[rows]
        query_over = jnp.concatenate([query, blank], axis=0)
        dout_under = jnp.concatenate([blank, dout_head], axis=0)
        count = 1.0 + jnp.where(
            same_class(key_pos, offset, RB) & same_class(query_pos, offset, RB), 1.0, 0.0
        )
        count = count + jnp.where(
            same_class(key_pos, offset, RC) & same_class(query_pos, offset, RC), 1.0, 0.0
        )
        in_near = same_class(query_row, offset, RC)
        in_far = same_class(query_row, offset, RE)

        scores = mm(key, query, 0, 0) * SCORE_SCALE
        near_scores = mm(near, query_over, 1, 0) * SCORE_SCALE
        near_max = jnp.max(near_scores, axis=0, keepdims=True)
        peak = jnp.max(scores, axis=0, keepdims=True)
        peak = jnp.where(in_near, jnp.maximum(peak, near_max), peak)
        mass = count * jnp.exp(scores - peak)
        near_mass = jnp.where(in_near, jnp.exp(near_scores - peak), 0.0)
        total = jnp.sum(mass, axis=0, keepdims=True) + jnp.sum(near_mass, axis=0, keepdims=True)
        log_mass = peak + jnp.log(total)
        inverse = 1.0 / total
        probs = mass * inverse
        near_probs = near_mass * inverse
        probs_low = probs.astype(BF16)
        near_low = near_probs.astype(BF16)
        attended = mm(value, probs_low, 1, 0) + mm(near, near_low, 0, 0)[HEAD_DIM:]
        delta = jnp.sum(dout_head.astype(F32) * attended, axis=0, keepdims=True)

        grad_probs = mm(value, dout_head, 0, 0)
        near_grad_probs = mm(near, dout_under, 1, 0)
        grad_scores = jnp.where(in_far, 0.0, probs * (grad_probs - delta)).astype(BF16)
        near_grad_scores = jnp.where(in_far, 0.0, near_probs * (near_grad_probs - delta)).astype(
            BF16
        )
        probs_kept = jnp.where(in_far, 0.0, probs).astype(BF16)
        near_kept = jnp.where(in_far, 0.0, near_probs).astype(BF16)
        grad_query_ref[rows] = (
            mm(key, grad_scores, 1, 0) + mm(near, near_grad_scores, 0, 0)[:HEAD_DIM]
        )
        grad_key_ref[rows] = mm(query, grad_scores, 1, 1)
        grad_value_ref[rows] = mm(dout_head, probs_kept, 1, 1)
        back = mm(near_grad_scores, query_over, 1, 1) + mm(near_kept, dout_under, 1, 1)
        back_ref[near_rows] = back.astype(BF16)

        attended_kept = jnp.where(in_far, 0.0, attended).astype(BF16)
        weight_part = mm(attended_kept, grad, 1, 1) * WEIGHT_SCALE
        query_key = jnp.concatenate([query, key], axis=0)
        value_dout = jnp.concatenate([value, dout_head], axis=0)
        stats = lay_stats((HEAD_DIM, TOKENS_HERE), 0, 0, (log_mass, delta))
        attended_stats = jnp.concatenate([attended.astype(BF16), stats.astype(BF16)], axis=0)
        mine = mm(far_chooser(offset, 0), query_key, 1, 1)
        mine = mine + mm(far_chooser(offset, 1), value_dout, 1, 1)
        mine = mine + mm(far_chooser(offset, 2), attended_stats, 1, 1)
        mine_ref[head * GAP : (head + 1) * GAP] = mine.astype(BF16)
        far_grad = mm(far_chooser(offset, 3), grad, 1, 1)
        for tile in range(tiles):
            lanes = slice(tile * LANES, (tile + 1) * LANES)
            slots_ref[head * tiles + tile, :HEAD_DIM] = weight_part[:, lanes].astype(BF16)
            slots_ref[head * tiles + tile, HEAD_DIM:] = (mine + far_grad[:, lanes]).astype(BF16)
        query_dout = jnp.concatenate([query, dout_head], axis=0)
        partner_far = partner_far + mm(far_chooser(offset, head), query_dout, 1, 1)
    back_ref[heads * NEAR :] = partner_far.astype(BF16)
    rest = slots_ref.shape[0] - heads * tiles
    slots_ref[heads * tiles :] = jnp.zeros((rest,) + slots_ref.shape[1:], BF16)


def merge_kernel(slots_ref, merged_ref, far_ref):
    sources = slots_ref.shape[0]
    total = slots_ref[0, :HEAD_DIM].astype(F32)
    for source in range(1, sources):
        total = total + slots_ref[source, :HEAD_DIM].astype(F32)
    half = GAP // 2
    for source in range(sources):
        block = slots_ref[source, HEAD_DIM:].astype(F32)
        far_ref[source * half : (source + 1) * half] = block[:half]
    pieces = [far_ref[pl.ds(kind, sources, stride=half), :] for kind in range(half)]
    full = jnp.concatenate([total] + pieces, axis=0).astype(BF16)
    for plane in range(PLANES):
        merged_ref[plane] = full


def far_kernel(plane_ref, merged_ref, slots_ref, first_ref, second_ref):
    sources = slots_ref.shape[0]
    width = 2 * sources
    count = PLANES * width

    def kind(index):
        start = HEAD_DIM + index * width
        return merged_ref[:, start : start + width, :].reshape(count, LANES)

    query_key, value_dout, attended_stats, far_grad = (kind(index) for index in range(4))
    shape = (LANES, HEAD_DIM)
    lower = one_hot(iota(shape, 0) == iota(shape, 1) + HEAD_DIM)
    query, value = query_key[:, :HEAD_DIM], value_dout[:, :HEAD_DIM]
    key, dout = (mm(both, lower, 1, 0).astype(BF16) for both in (query_key, value_dout))
    local_attended = attended_stats[:, :HEAD_DIM].astype(F32)
    stats = attended_stats.astype(F32)
    local_mass = take_stat(stats, 0)

    scores = mm(query, key, 1, 1) * SCORE_SCALE
    peak = jnp.maximum(jnp.max(scores, axis=1, keepdims=True), local_mass)
    mass = jnp.exp(scores - peak)
    local_part = jnp.exp(local_mass - peak)
    total = jnp.sum(mass, axis=1, keepdims=True) + local_part
    normalizer = peak + jnp.log(total)
    inverse = 1.0 / total
    probs = mass * inverse
    probs_low = probs.astype(BF16)
    attended = local_part * inverse * local_attended + mm(probs_low, value, 1, 0)
    delta = jnp.sum(dout.astype(F32) * attended, axis=1, keepdims=True)
    grad_probs = mm(dout, value, 1, 1)
    grad_scores = (probs * (grad_probs - delta)).astype(BF16)
    grad_query = mm(grad_scores, key, 1, 0).astype(BF16)
    grad_key = mm(grad_scores, query, 0, 0).astype(BF16)
    grad_value = mm(probs_low, dout, 0, 0).astype(BF16)
    weight_part = mm(attended.astype(BF16), far_grad, 0, 0) * WEIGHT_SCALE
    for plane in range(PLANES):
        weight_part = weight_part + merged_ref[plane, :HEAD_DIM].astype(F32)

    def other_plane(column):
        blocks = [column[(p ^ 1) * width : ((p ^ 1) + 1) * width] for p in range(PLANES)]
        return jnp.concatenate(blocks, axis=0)

    shape = (HEAD_DIM, LANES)
    to_left = one_hot(iota(shape, 0) == iota(shape, 1))
    to_right = one_hot(iota(shape, 0) + HEAD_DIM == iota(shape, 1))
    both_stats = (normalizer, delta, other_plane(normalizer), other_plane(delta))
    first_ref[...] = mm(grad_value, to_left, 1, 0) + lay_stats(
        (count, LANES), 1, HEAD_DIM, both_stats
    )
    second_ref[...] = mm(grad_query, to_left, 1, 0) + mm(grad_key, to_right, 1, 0)
    own = pl.ds(pl.multiple_of(plane_ref[0] * width, width), width)
    shape = (sources * GAP, width)
    row, column = iota(shape, 0), iota(shape, 1)
    same = (row // GAP) == (column % sources)
    slot_row, pair = row % GAP, column // sources
    placed = mm(one_hot(same & (slot_row == pair)), first_ref[own, :].astype(BF16), 1, 0)
    placed = placed + mm(
        one_hot(same & (slot_row == pair + 2)), second_ref[own, :].astype(BF16), 1, 0
    )
    slots_ref[:, HEAD_DIM:, :] = placed.astype(BF16).reshape(sources, GAP, LANES)
    weight_low = weight_part.astype(BF16)
    for source in range(sources):
        slots_ref[source, :HEAD_DIM] = weight_low


def final_kernel(
    offset_ref,
    query_ref,
    key_ref,
    value_ref,
    near_ref,
    back_ref,
    mine_ref,
    local_query_ref,
    local_key_ref,
    local_value_ref,
    slots_ref,
    grad_query_ref,
    grad_key_ref,
    grad_value_ref,
    grad_weight_ref,
):
    heads = query_ref.shape[0] // HEAD_DIM
    tiles = grad_weight_ref.shape[1] // LANES
    blank = jnp.zeros((HEAD_DIM, TOKENS_HERE), BF16)
    key_row = iota((1, TOKENS_HERE), 1)
    shape = (GAP, GAP)
    row, column = iota(shape, 0), iota(shape, 1)
    valid = iota((GAP, 1), 0) < 2
    partner_far = back_ref[heads * NEAR :]
    for head in range(heads):
        offset = offset_ref[head]
        rows = slice(head * HEAD_DIM, (head + 1) * HEAD_DIM)
        near_rows = slice(head * NEAR, (head + 1) * NEAR)
        query, key, value = query_ref[rows], key_ref[rows], value_ref[rows]
        near = near_ref[near_rows]
        mine = mine_ref[head * GAP : (head + 1) * GAP]
        returned = slots_ref[head * tiles, HEAD_DIM:]
        stats = returned.astype(F32)
        normalizer, delta, far_normalizer, far_delta = (take_stat(stats, i) for i in range(4))
        key_over = jnp.concatenate([key, blank], axis=0)
        value_under = jnp.concatenate([blank, value], axis=0)
        near_key, near_value = left_half(near), right_half(near)

        count = 1.0 + jnp.where(same_class(key_row, offset, RB), 1.0, 0.0)
        count = count + jnp.where(same_class(key_row, offset, RC), 1.0, 0.0)
        value_dout = mm(one_hot((row < 2) & (column == row + 2)), mine, 1, 0).astype(BF16)
        scores = mm(mine, key_over, 1, 0) * SCORE_SCALE
        probs = jnp.where(valid, count * jnp.exp(scores - normalizer), 0.0)
        grad_scores = (probs * (mm(value_dout, value_under, 1, 0) - delta)).astype(BF16)
        scores = mm(mine, near_key, 1, 1) * SCORE_SCALE
        near_probs = jnp.where(valid, jnp.exp(scores - normalizer), 0.0)
        near_grad_scores = (near_probs * (mm(value_dout, near_value, 1, 1) - delta)).astype(BF16)
        far_query = mm(grad_scores, key_over, 1, 1) + mm(near_grad_scores, near_key, 1, 0)
        far_query = far_query.astype(BF16)

        query_dout = one_hot((row < 2) & (column == row + 2 * head))
        query_dout = mm(query_dout, partner_far, 1, 0).astype(BF16)
        near_choice = near_chooser(offset)
        own_near = mm(near_choice, jnp.concatenate([key, value], axis=0), 1, 1).astype(BF16)
        scores = mm(query_dout, left_half(own_near), 1, 1) * SCORE_SCALE
        far_probs = jnp.where(valid, jnp.exp(scores - far_normalizer), 0.0)
        far_grad_probs = mm(query_dout, right_half(own_near), 1, 1)
        far_grad_scores = (far_probs * (far_grad_probs - far_delta)).astype(BF16)
        near_grad = left_half(mm(far_grad_scores, query_dout, 0, 0)).astype(F32)
        near_grad = near_grad + right_half(mm(far_probs.astype(BF16), query_dout, 0, 0)).astype(F32)
        near_grad = (near_grad + back_ref[near_rows].astype(F32)).astype(BF16)

        first_choice, second_choice = far_chooser(offset, 0), far_chooser(offset, 1)
        value_spread = mm(returned, first_choice, 0, 0)
        query_key_spread = mm(returned, second_choice, 0, 0)
        near_spread = mm(near_grad, near_choice, 0, 0)
        grad_query = local_query_ref[rows] + query_key_spread[:HEAD_DIM]
        grad_query = grad_query + mm(far_query, first_choice, 0, 0)[:HEAD_DIM]
        grad_key = local_key_ref[rows] + query_key_spread[HEAD_DIM:] + near_spread[:HEAD_DIM]
        grad_key = grad_key + mm(mine, grad_scores, 0, 0)[:HEAD_DIM]
        grad_value = local_value_ref[rows] + value_spread[:HEAD_DIM] + near_spread[HEAD_DIM:]
        grad_value = grad_value + mm(value_dout, probs.astype(BF16), 0, 0)[HEAD_DIM:]
        grad_query_ref[rows] = (grad_query * SCORE_SCALE).astype(BF16)
        grad_key_ref[rows] = (grad_key * SCORE_SCALE).astype(BF16)
        grad_value_ref[rows] = grad_value.astype(BF16)
        for tile in range(tiles):
            lanes = slice(tile * LANES, (tile + 1) * LANES)
            grad_weight_ref[rows, lanes] = slots_ref[head * tiles + tile, :HEAD_DIM].astype(F32)


def call(kernel, outs, scalars, arrays, scratch=()):
    specs = [pl.BlockSpec(memory_space=pltpu.SMEM)] * scalars
    specs = specs + [pl.BlockSpec(memory_space=pltpu.VMEM)] * (len(arrays) - scalars)
    shapes = [jax.ShapeDtypeStruct(shape, dtype) for shape, dtype in outs]
    return pl.pallas_call(
        kernel,
        out_shape=shapes,
        in_specs=specs,
        out_specs=[pl.BlockSpec(memory_space=pltpu.VMEM)] * len(shapes),
        scratch_shapes=list(scratch),
        compiler_params=pltpu.CompilerParams(vmem_limit_bytes=40 * 1024 * 1024),
        name=kernel.__name__,
    )(*arrays)


def local(queries, keys, values, grad_out, out_weight, offsets):
    features = queries.shape[0]
    model = out_weight.shape[1]
    heads = offsets.shape[0]
    sources = lax.axis_size("xz")
    rows = heads * NEAR
    other = [(i, i ^ 1) for i in range(PLANES)]

    (near_own,) = call(near_kernel, [((rows, LANES), BF16)], 1, (offsets, keys, values))
    near = lax.ppermute(near_own, "yh", other)
    full_grad = lax.all_gather(grad_out, "dp", axis=0, tiled=True)
    local_shape = ((features, TOKENS_HERE), F32)
    slots, back, mine, local_query, local_key, local_value = call(
        local_kernel,
        [
            ((sources, SLOT, LANES), BF16),
            ((rows + GAP, LANES), BF16),
            ((heads * GAP, LANES), BF16),
            local_shape,
            local_shape,
            local_shape,
        ],
        1,
        (offsets, queries, keys, values, full_grad, out_weight, near),
    )
    back = lax.ppermute(back, "yh", other)
    slots = lax.all_to_all(slots, "xz", 0, 0, tiled=True)
    merged_rows = HEAD_DIM + sources * GAP // 2
    (merged,) = call(
        merge_kernel,
        [((PLANES, merged_rows, LANES), BF16)],
        0,
        (slots,),
        [pltpu.VMEM((sources * GAP // 2, LANES), F32)],
    )
    merged = lax.all_to_all(merged, "yh", 0, 0, tiled=True)
    plane = lax.axis_index("yh").reshape(1)
    far_count = PLANES * sources * 2
    (slots,) = call(
        far_kernel,
        [((sources, SLOT, LANES), BF16)],
        1,
        (plane, merged),
        [pltpu.VMEM((far_count, LANES), F32), pltpu.VMEM((far_count, LANES), F32)],
    )
    slots = lax.all_to_all(slots, "xz", 0, 0, tiled=True)
    grad_shape = ((features, TOKENS_HERE), BF16)
    return tuple(
        call(
            final_kernel,
            [grad_shape, grad_shape, grad_shape, ((features, model), F32)],
            1,
            (
                offsets,
                queries,
                keys,
                values,
                near,
                back,
                mine,
                local_query,
                local_key,
                local_value,
                slots,
            ),
        )
    )


def solution(mesh):
    devices = mesh.devices.reshape(-1, PLANES, mesh.devices.shape[1])
    split_mesh = Mesh(devices, ("xz", "yh", "dp"))
    wide = P("dp", ("xz", "yh"))
    return jax.shard_map(
        local,
        mesh=split_mesh,
        in_specs=(wide, wide, wide, wide, P("dp", None), P("dp")),
        out_specs=(wide, wide, wide, P("dp", None)),
        check_vma=False,
    )
```

```python
import jax
import jax.numpy as jnp
from jax import lax
from jax.experimental import pallas as pl
from jax.experimental.pallas import tpu as pltpu
from jax.sharding import Mesh
from jax.sharding import PartitionSpec as P

HEAD_DIM = 64
TOKENS_HERE = 256
RB = 2
RC = 16
RE = 128
NEAR = TOKENS_HERE // RC
SCORE_SCALE = HEAD_DIM ** (-0.5)
WEIGHT_SCALE = 0.03125

PLANES = 4
LANES = 128
GAP = 16
SMALL = 8
CHUNK = 40
SLOT = CHUNK + SMALL

F32 = jnp.float32
BF16 = jnp.bfloat16


def mm(left, right, left_dim, right_dim):
    return lax.dot_general(
        left, right, (((left_dim,), (right_dim,)), ((), ())), preferred_element_type=F32
    )


def iota(shape, dim):
    return lax.broadcasted_iota(jnp.int32, shape, dim)


def one_hot(condition):
    return jnp.where(condition, 1.0, 0.0).astype(BF16)


def same_class(position, offset, stride):
    return (position & (stride - 1)) == (offset & (stride - 1))


def near_chooser(offset):
    shape = (NEAR, TOKENS_HERE)
    return one_hot(iota(shape, 1) == RC * iota(shape, 0) + (offset & (RC - 1)))


def far_chooser(offset, pair):
    shape = (GAP, TOKENS_HERE)
    row = iota(shape, 0)
    hit = iota(shape, 1) == RE * (row & 1) + offset
    return one_hot(hit & ((row >> 1) == pair))


def split3(value):
    high = value.astype(BF16).astype(F32)
    rest = value - high
    middle = rest.astype(BF16).astype(F32)
    return high, middle, rest - middle


def lay_stats(shape, dim, start, values):
    place = iota(shape, dim) - start
    out = jnp.zeros(shape, F32)
    for index, value in enumerate(values):
        for part_index, part in enumerate(split3(value)):
            out = jnp.where(place == 3 * index + part_index, part, out)
    return out


def take_stat(rows, index):
    place = iota(rows.shape, 1) - HEAD_DIM - 3 * index
    return jnp.sum(jnp.where((place >= 0) & (place < 3), rows, 0.0), axis=1, keepdims=True)


def left_half(rows):
    return jnp.where(iota(rows.shape, 1) < HEAD_DIM, rows.astype(F32), 0.0).astype(BF16)


def right_half(rows):
    return jnp.where(iota(rows.shape, 1) >= HEAD_DIM, rows.astype(F32), 0.0).astype(BF16)


def chunk_rows(folded, chunk):
    rows = folded[chunk * CHUNK : (chunk + 1) * CHUNK]
    short = CHUNK - rows.shape[0]
    if short:
        rows = jnp.concatenate([rows, jnp.zeros((short,) + rows.shape[1:], rows.dtype)], axis=0)
    return rows


def near_kernel(offset_ref, key_ref, value_ref, near_ref):
    for head in range(key_ref.shape[0] // HEAD_DIM):
        rows = slice(head * HEAD_DIM, (head + 1) * HEAD_DIM)
        both = jnp.concatenate([key_ref[rows], value_ref[rows]], axis=0)
        picked = mm(near_chooser(offset_ref[head]), both, 1, 1)
        near_ref[head * NEAR : (head + 1) * NEAR, :] = picked.astype(BF16)


def local_kernel(
    offset_ref,
    query_ref,
    key_ref,
    value_ref,
    grad_ref,
    weight_ref,
    near_ref,
    slots_ref,
    back_ref,
    mine_ref,
    grad_query_ref,
    grad_key_ref,
    grad_value_ref,
):
    heads = query_ref.shape[0] // HEAD_DIM
    half = grad_ref.shape[0] // 2
    chunks = pl.cdiv(half, CHUNK)
    grad = grad_ref[...]
    dout = mm(weight_ref[...], grad, 1, 0).astype(BF16)
    choosers = [far_chooser(offset_ref[head], 3) for head in range(heads)]
    choosers = jnp.concatenate(choosers, axis=0)
    wide = grad.astype(F32)
    filler = jnp.zeros((LANES - 2 * CHUNK, TOKENS_HERE), F32)
    far_grads = []
    for chunk in range(chunks):
        both = [chunk_rows(wide[:half], chunk), chunk_rows(wide[half:], chunk), filler]
        far_grads.append(mm(choosers, jnp.concatenate(both, axis=0).astype(BF16), 1, 1))
    blank = jnp.zeros((HEAD_DIM, TOKENS_HERE), BF16)
    key_pos = iota((TOKENS_HERE, TOKENS_HERE), 0)
    query_pos = iota((TOKENS_HERE, TOKENS_HERE), 1)
    query_row = iota((1, TOKENS_HERE), 1)
    partner_far = jnp.zeros((GAP, LANES), F32)
    for head in range(heads):
        offset = offset_ref[head]
        rows = slice(head * HEAD_DIM, (head + 1) * HEAD_DIM)
        near_rows = slice(head * NEAR, (head + 1) * NEAR)
        query, key, value = query_ref[rows], key_ref[rows], value_ref[rows]
        near = near_ref[near_rows]
        dout_head = dout[rows]
        query_over = jnp.concatenate([query, blank], axis=0)
        dout_under = jnp.concatenate([blank, dout_head], axis=0)
        count = 1.0 + jnp.where(
            same_class(key_pos, offset, RB) & same_class(query_pos, offset, RB), 1.0, 0.0
        )
        count = count + jnp.where(
            same_class(key_pos, offset, RC) & same_class(query_pos, offset, RC), 1.0, 0.0
        )
        in_near = same_class(query_row, offset, RC)
        in_far = same_class(query_row, offset, RE)

        scores = mm(key, query, 0, 0) * SCORE_SCALE
        near_scores = mm(near, query_over, 1, 0) * SCORE_SCALE
        near_max = jnp.max(near_scores, axis=0, keepdims=True)
        peak = jnp.max(scores, axis=0, keepdims=True)
        peak = jnp.where(in_near, jnp.maximum(peak, near_max), peak)
        mass = count * jnp.exp(scores - peak)
        near_mass = jnp.where(in_near, jnp.exp(near_scores - peak), 0.0)
        total = jnp.sum(mass, axis=0, keepdims=True) + jnp.sum(near_mass, axis=0, keepdims=True)
        log_mass = peak + jnp.log(total)
        inverse = 1.0 / total
        probs = mass * inverse
        near_probs = near_mass * inverse
        probs_low = probs.astype(BF16)
        near_low = near_probs.astype(BF16)
        attended = mm(value, probs_low, 1, 0) + mm(near, near_low, 0, 0)[HEAD_DIM:]
        delta = jnp.sum(dout_head.astype(F32) * attended, axis=0, keepdims=True)

        grad_probs = mm(value, dout_head, 0, 0)
        near_grad_probs = mm(near, dout_under, 1, 0)
        grad_scores = jnp.where(in_far, 0.0, probs * (grad_probs - delta)).astype(BF16)
        near_grad_scores = jnp.where(in_far, 0.0, near_probs * (near_grad_probs - delta)).astype(
            BF16
        )
        probs_kept = jnp.where(in_far, 0.0, probs).astype(BF16)
        near_kept = jnp.where(in_far, 0.0, near_probs).astype(BF16)
        grad_query_ref[rows] = (
            mm(key, grad_scores, 1, 0) + mm(near, near_grad_scores, 0, 0)[:HEAD_DIM]
        )
        grad_key_ref[rows] = mm(query, grad_scores, 1, 1)
        grad_value_ref[rows] = mm(dout_head, probs_kept, 1, 1)
        back = mm(near_grad_scores, query_over, 1, 1) + mm(near_kept, dout_under, 1, 1)
        back_ref[near_rows] = back.astype(BF16)

        attended_kept = jnp.where(in_far, 0.0, attended).astype(BF16)
        over = jnp.concatenate([attended_kept, blank], axis=0)
        under = jnp.concatenate([blank, attended_kept], axis=0)
        weight_part = mm(grad[:half], over, 1, 1) + mm(grad[half:], under, 1, 1)
        weight_part = weight_part * WEIGHT_SCALE
        query_key = jnp.concatenate([query, key], axis=0)
        value_dout = jnp.concatenate([value, dout_head], axis=0)
        stats = lay_stats((HEAD_DIM, TOKENS_HERE), 0, 0, (log_mass, delta))
        attended_stats = jnp.concatenate([attended.astype(BF16), stats.astype(BF16)], axis=0)
        mine = mm(far_chooser(offset, 0), query_key, 1, 1)
        mine = mine + mm(far_chooser(offset, 1), value_dout, 1, 1)
        mine = mine + mm(far_chooser(offset, 2), attended_stats, 1, 1)
        mine_ref[head * GAP : (head + 1) * GAP] = mine.astype(BF16)
        for chunk in range(chunks):
            far_grad = far_grads[chunk][head * GAP : head * GAP + SMALL]
            parts = [chunk_rows(weight_part, chunk), mine[:SMALL] + far_grad]
            slots_ref[head * chunks + chunk] = jnp.concatenate(parts, axis=0).astype(BF16)
        query_dout = jnp.concatenate([query, dout_head], axis=0)
        partner_far = partner_far + mm(far_chooser(offset, head), query_dout, 1, 1)
    back_ref[heads * NEAR :] = partner_far.astype(BF16)
    rest = slots_ref.shape[0] - heads * chunks
    slots_ref[heads * chunks :] = jnp.zeros((rest,) + slots_ref.shape[1:], BF16)


def merge_kernel(slots_ref, merged_ref, far_ref):
    sources = slots_ref.shape[0]
    total = jnp.zeros((SLOT, LANES), F32)
    for source in range(sources):
        block = slots_ref[source].astype(F32)
        total = total + block
        far_ref[source * SMALL : (source + 1) * SMALL] = block[CHUNK:]
    pieces = [far_ref[pl.ds(kind, sources, stride=SMALL), :] for kind in range(SMALL)]
    full = jnp.concatenate([total] + pieces, axis=0).astype(BF16)
    for plane in range(PLANES):
        merged_ref[plane] = full


def far_kernel(plane_ref, merged_ref, slots_ref, first_ref, second_ref):
    sources = slots_ref.shape[0]
    width = 2 * sources
    count = PLANES * width

    def kind(index):
        start = SLOT + index * width
        return merged_ref[:, start : start + width, :].reshape(count, LANES)

    query_key, value_dout, attended_stats, far_grad = (kind(index) for index in range(4))
    shape = (LANES, HEAD_DIM)
    lower = one_hot(iota(shape, 0) == iota(shape, 1) + HEAD_DIM)
    query, value = query_key[:, :HEAD_DIM], value_dout[:, :HEAD_DIM]
    key, dout = (mm(both, lower, 1, 0).astype(BF16) for both in (query_key, value_dout))
    local_attended = attended_stats[:, :HEAD_DIM].astype(F32)
    stats = attended_stats.astype(F32)
    local_mass = take_stat(stats, 0)

    scores = mm(query, key, 1, 1) * SCORE_SCALE
    peak = jnp.maximum(jnp.max(scores, axis=1, keepdims=True), local_mass)
    mass = jnp.exp(scores - peak)
    local_part = jnp.exp(local_mass - peak)
    total = jnp.sum(mass, axis=1, keepdims=True) + local_part
    normalizer = peak + jnp.log(total)
    inverse = 1.0 / total
    probs = mass * inverse
    probs_low = probs.astype(BF16)
    attended = local_part * inverse * local_attended + mm(probs_low, value, 1, 0)
    delta = jnp.sum(dout.astype(F32) * attended, axis=1, keepdims=True)
    grad_probs = mm(dout, value, 1, 1)
    grad_scores = (probs * (grad_probs - delta)).astype(BF16)
    grad_query = mm(grad_scores, key, 1, 0).astype(BF16)
    grad_key = mm(grad_scores, query, 0, 0).astype(BF16)
    grad_value = mm(probs_low, dout, 0, 0).astype(BF16)

    def other_plane(column):
        blocks = [column[(p ^ 1) * width : ((p ^ 1) + 1) * width] for p in range(PLANES)]
        return jnp.concatenate(blocks, axis=0)

    shape = (HEAD_DIM, LANES)
    to_left = one_hot(iota(shape, 0) == iota(shape, 1))
    to_right = one_hot(iota(shape, 0) + HEAD_DIM == iota(shape, 1))
    attended_low = attended.astype(BF16)
    over = mm(attended_low, to_left, 1, 0).astype(BF16)
    under = mm(attended_low, to_right, 1, 0).astype(BF16)
    weight_part = mm(far_grad, over, 0, 0)[:CHUNK] + mm(far_grad, under, 0, 0)[CHUNK : 2 * CHUNK]
    weight_part = weight_part * WEIGHT_SCALE
    for plane in range(PLANES):
        weight_part = weight_part + merged_ref[plane, :SLOT].astype(F32)[:CHUNK]
    both_stats = (normalizer, delta, other_plane(normalizer), other_plane(delta))
    first_ref[...] = mm(grad_value, to_left, 1, 0) + lay_stats(
        (count, LANES), 1, HEAD_DIM, both_stats
    )
    second_ref[...] = mm(grad_query, to_left, 1, 0) + mm(grad_key, to_right, 1, 0)
    own = pl.ds(pl.multiple_of(plane_ref[0] * width, width), width)
    shape = (sources * SMALL, width)
    row, column = iota(shape, 0), iota(shape, 1)
    same = (row // SMALL) == (column % sources)
    slot_row, pair = row % SMALL, column // sources
    placed = mm(one_hot(same & (slot_row == pair)), first_ref[own, :].astype(BF16), 1, 0)
    placed = placed + mm(
        one_hot(same & (slot_row == pair + 2)), second_ref[own, :].astype(BF16), 1, 0
    )
    for source in range(sources):
        parts = [weight_part, placed[source * SMALL : (source + 1) * SMALL]]
        slots_ref[source] = jnp.concatenate(parts, axis=0).astype(BF16)


def final_kernel(
    offset_ref,
    query_ref,
    key_ref,
    value_ref,
    near_ref,
    back_ref,
    mine_ref,
    local_query_ref,
    local_key_ref,
    local_value_ref,
    slots_ref,
    grad_query_ref,
    grad_key_ref,
    grad_value_ref,
    grad_weight_ref,
):
    heads = query_ref.shape[0] // HEAD_DIM
    half = grad_weight_ref.shape[1] // 2
    chunks = pl.cdiv(half, CHUNK)
    blank = jnp.zeros((HEAD_DIM, TOKENS_HERE), BF16)
    key_row = iota((1, TOKENS_HERE), 1)
    shape = (GAP, GAP)
    row, column = iota(shape, 0), iota(shape, 1)
    valid = iota((GAP, 1), 0) < 2
    partner_far = back_ref[heads * NEAR :]
    for head in range(heads):
        offset = offset_ref[head]
        rows = slice(head * HEAD_DIM, (head + 1) * HEAD_DIM)
        near_rows = slice(head * NEAR, (head + 1) * NEAR)
        query, key, value = query_ref[rows], key_ref[rows], value_ref[rows]
        near = near_ref[near_rows]
        mine = mine_ref[head * GAP : (head + 1) * GAP]
        blocks = [slots_ref[head * chunks + chunk].astype(F32) for chunk in range(chunks)]
        stats = jnp.concatenate(
            [blocks[0][CHUNK:], jnp.zeros((GAP - SMALL, LANES), F32)], axis=0
        )
        returned = stats.astype(BF16)
        normalizer, delta, far_normalizer, far_delta = (take_stat(stats, i) for i in range(4))
        key_over = jnp.concatenate([key, blank], axis=0)
        value_under = jnp.concatenate([blank, value], axis=0)
        near_key, near_value = left_half(near), right_half(near)

        count = 1.0 + jnp.where(same_class(key_row, offset, RB), 1.0, 0.0)
        count = count + jnp.where(same_class(key_row, offset, RC), 1.0, 0.0)
        value_dout = mm(one_hot((row < 2) & (column == row + 2)), mine, 1, 0).astype(BF16)
        scores = mm(mine, key_over, 1, 0) * SCORE_SCALE
        probs = jnp.where(valid, count * jnp.exp(scores - normalizer), 0.0)
        grad_scores = (probs * (mm(value_dout, value_under, 1, 0) - delta)).astype(BF16)
        scores = mm(mine, near_key, 1, 1) * SCORE_SCALE
        near_probs = jnp.where(valid, jnp.exp(scores - normalizer), 0.0)
        near_grad_scores = (near_probs * (mm(value_dout, near_value, 1, 1) - delta)).astype(BF16)
        far_query = mm(grad_scores, key_over, 1, 1) + mm(near_grad_scores, near_key, 1, 0)
        far_query = far_query.astype(BF16)

        query_dout = one_hot((row < 2) & (column == row + 2 * head))
        query_dout = mm(query_dout, partner_far, 1, 0).astype(BF16)
        near_choice = near_chooser(offset)
        own_near = mm(near_choice, jnp.concatenate([key, value], axis=0), 1, 1).astype(BF16)
        scores = mm(query_dout, left_half(own_near), 1, 1) * SCORE_SCALE
        far_probs = jnp.where(valid, jnp.exp(scores - far_normalizer), 0.0)
        far_grad_probs = mm(query_dout, right_half(own_near), 1, 1)
        far_grad_scores = (far_probs * (far_grad_probs - far_delta)).astype(BF16)
        near_grad = left_half(mm(far_grad_scores, query_dout, 0, 0)).astype(F32)
        near_grad = near_grad + right_half(mm(far_probs.astype(BF16), query_dout, 0, 0)).astype(F32)
        near_grad = (near_grad + back_ref[near_rows].astype(F32)).astype(BF16)

        first_choice, second_choice = far_chooser(offset, 0), far_chooser(offset, 1)
        value_spread = mm(returned, first_choice, 0, 0)
        query_key_spread = mm(returned, second_choice, 0, 0)
        near_spread = mm(near_grad, near_choice, 0, 0)
        grad_query = local_query_ref[rows] + query_key_spread[:HEAD_DIM]
        grad_query = grad_query + mm(far_query, first_choice, 0, 0)[:HEAD_DIM]
        grad_key = local_key_ref[rows] + query_key_spread[HEAD_DIM:] + near_spread[:HEAD_DIM]
        grad_key = grad_key + mm(mine, grad_scores, 0, 0)[:HEAD_DIM]
        grad_value = local_value_ref[rows] + value_spread[:HEAD_DIM] + near_spread[HEAD_DIM:]
        grad_value = grad_value + mm(value_dout, probs.astype(BF16), 0, 0)[HEAD_DIM:]
        grad_query_ref[rows] = (grad_query * SCORE_SCALE).astype(BF16)
        grad_key_ref[rows] = (grad_key * SCORE_SCALE).astype(BF16)
        grad_value_ref[rows] = grad_value.astype(BF16)
        folded = jnp.concatenate([block[:CHUNK] for block in blocks], axis=0)[:half]
        unfolded = jnp.transpose(folded)
        grad_weight_ref[rows, :half] = unfolded[:HEAD_DIM]
        grad_weight_ref[rows, half:] = unfolded[HEAD_DIM:]


def call(kernel, outs, scalars, arrays, scratch=()):
    specs = [pl.BlockSpec(memory_space=pltpu.SMEM)] * scalars
    specs = specs + [pl.BlockSpec(memory_space=pltpu.VMEM)] * (len(arrays) - scalars)
    shapes = [jax.ShapeDtypeStruct(shape, dtype) for shape, dtype in outs]
    return pl.pallas_call(
        kernel,
        out_shape=shapes,
        in_specs=specs,
        out_specs=[pl.BlockSpec(memory_space=pltpu.VMEM)] * len(shapes),
        scratch_shapes=list(scratch),
        compiler_params=pltpu.CompilerParams(vmem_limit_bytes=40 * 1024 * 1024),
        name=kernel.__name__,
    )(*arrays)


def local(queries, keys, values, grad_out, out_weight, offsets):
    features = queries.shape[0]
    model = out_weight.shape[1]
    heads = offsets.shape[0]
    sources = lax.axis_size("xz")
    rows = heads * NEAR
    other = [(i, i ^ 1) for i in range(PLANES)]

    (near_own,) = call(near_kernel, [((rows, LANES), BF16)], 1, (offsets, keys, values))
    near = lax.ppermute(near_own, "yh", other)
    full_grad = lax.all_gather(grad_out, "dp", axis=0, tiled=True)
    local_shape = ((features, TOKENS_HERE), F32)
    slots, back, mine, local_query, local_key, local_value = call(
        local_kernel,
        [
            ((sources, SLOT, LANES), BF16),
            ((rows + GAP, LANES), BF16),
            ((heads * GAP, LANES), BF16),
            local_shape,
            local_shape,
            local_shape,
        ],
        1,
        (offsets, queries, keys, values, full_grad, out_weight, near),
    )
    back = lax.ppermute(back, "yh", other)
    slots = lax.all_to_all(slots, "xz", 0, 0, tiled=True)
    merged_rows = SLOT + sources * SMALL
    (merged,) = call(
        merge_kernel,
        [((PLANES, merged_rows, LANES), BF16)],
        0,
        (slots,),
        [pltpu.VMEM((sources * SMALL, LANES), F32)],
    )
    merged = lax.all_to_all(merged, "yh", 0, 0, tiled=True)
    plane = lax.axis_index("yh").reshape(1)
    far_count = PLANES * sources * 2
    (slots,) = call(
        far_kernel,
        [((sources, SLOT, LANES), BF16)],
        1,
        (plane, merged),
        [pltpu.VMEM((far_count, LANES), F32), pltpu.VMEM((far_count, LANES), F32)],
    )
    slots = lax.all_to_all(slots, "xz", 0, 0, tiled=True)
    grad_shape = ((features, TOKENS_HERE), BF16)
    return tuple(
        call(
            final_kernel,
            [grad_shape, grad_shape, grad_shape, ((features, model), F32)],
            1,
            (
                offsets,
                queries,
                keys,
                values,
                near,
                back,
                mine,
                local_query,
                local_key,
                local_value,
                slots,
            ),
        )
    )


def solution(mesh):
    devices = mesh.devices.reshape(-1, PLANES, mesh.devices.shape[1])
    split_mesh = Mesh(devices, ("xz", "yh", "dp"))
    wide = P("dp", ("xz", "yh"))
    return jax.shard_map(
        local,
        mesh=split_mesh,
        in_specs=(wide, wide, wide, wide, P("dp", None), P("dp")),
        out_specs=(wide, wide, wide, P("dp", None)),
        check_vma=False,
    )
```

```python
import jax
import jax.numpy as jnp
from jax import lax
from jax.experimental import pallas as pl
from jax.experimental.pallas import tpu as pltpu
from jax.sharding import Mesh
from jax.sharding import PartitionSpec as P

HEAD_DIM = 64
TOKENS_HERE = 256
RB = 2
RC = 16
RE = 128
NEAR = TOKENS_HERE // RC
SCORE_SCALE = HEAD_DIM ** (-0.5)
WEIGHT_SCALE = 0.03125

PLANES = 4
LANES = 128
GAP = 16
SMALL = 8
CHUNK = 40
SLOT = CHUNK + SMALL
ABSENT = -1e30
LIMIT = 63_400_000

F32 = jnp.float32
BF16 = jnp.bfloat16


def mm(left, right, left_dim, right_dim):
    return lax.dot_general(
        left, right, (((left_dim,), (right_dim,)), ((), ())), preferred_element_type=F32
    )


def iota(shape, dim):
    return lax.broadcasted_iota(jnp.int32, shape, dim)


def one_hot(condition):
    return jnp.where(condition, 1.0, 0.0).astype(BF16)


def same_class(position, offset, stride):
    return (position & (stride - 1)) == (offset & (stride - 1))


def near_chooser(offset):
    shape = (NEAR, TOKENS_HERE)
    return one_hot(iota(shape, 1) == RC * iota(shape, 0) + (offset & (RC - 1)))


def far_chooser(offset, pair):
    shape = (GAP, TOKENS_HERE)
    row = iota(shape, 0)
    hit = iota(shape, 1) == RE * (row & 1) + offset
    return one_hot(hit & ((row >> 1) == pair))


def split3(value):
    high = value.astype(BF16).astype(F32)
    rest = value - high
    middle = rest.astype(BF16).astype(F32)
    return high, middle, rest - middle


def lay_stats(shape, dim, start, values):
    place = iota(shape, dim) - start
    out = jnp.zeros(shape, F32)
    for index, value in enumerate(values):
        for part_index, part in enumerate(split3(value)):
            out = jnp.where(place == 3 * index + part_index, part, out)
    return out


def take_stat(rows, index):
    place = iota(rows.shape, 1) - HEAD_DIM - 3 * index
    return jnp.sum(jnp.where((place >= 0) & (place < 3), rows, 0.0), axis=1, keepdims=True)


def chunk_rows(folded, chunk):
    rows = folded[chunk * CHUNK : (chunk + 1) * CHUNK]
    short = CHUNK - rows.shape[0]
    if short:
        rows = jnp.concatenate([rows, jnp.zeros((short,) + rows.shape[1:], rows.dtype)], axis=0)
    return rows


def near_kernel(
    offset_hbm, key_hbm, value_hbm, near_ref, offset_ref, key_ref, value_ref, semaphores
):
    pairs = ((offset_hbm, offset_ref), (key_hbm, key_ref), (value_hbm, value_ref))
    copies = [
        pltpu.make_async_copy(source, target, semaphores.at[index])
        for index, (source, target) in enumerate(pairs)
    ]
    for copy in copies:
        copy.start()
    for copy in copies:
        copy.wait()
    for head in range(key_ref.shape[0] // HEAD_DIM):
        rows = slice(head * HEAD_DIM, (head + 1) * HEAD_DIM)
        both = jnp.concatenate([key_ref[rows], value_ref[rows]], axis=0)
        picked = mm(near_chooser(offset_ref[head]), both, 1, 1)
        near_ref[head * NEAR : (head + 1) * NEAR, :] = picked.astype(BF16)


def pair_count(key_pos, query_pos, offset):
    count = 1.0 + jnp.where(
        same_class(key_pos, offset, RB) & same_class(query_pos, offset, RB), 1.0, 0.0
    )
    return count + jnp.where(
        same_class(key_pos, offset, RC) & same_class(query_pos, offset, RC), 1.0, 0.0
    )


def local_kernel(
    offset_ref,
    query_ref,
    key_ref,
    value_ref,
    grad_ref,
    weight_ref,
    near_ref,
    slots_ref,
    dout_ref,
    stats_ref,
):
    heads = query_ref.shape[0] // HEAD_DIM
    half = grad_ref.shape[0] // 2
    chunks = pl.cdiv(half, CHUNK)
    grad = grad_ref[...]
    dout = mm(weight_ref[...], grad, 1, 0).astype(BF16)
    dout_ref[...] = dout
    choosers = [far_chooser(offset_ref[head], 3) for head in range(heads)]
    choosers = jnp.concatenate(choosers, axis=0)
    wide = grad.astype(F32)
    filler = jnp.zeros((LANES - 2 * CHUNK, TOKENS_HERE), F32)
    far_grads = []
    for chunk in range(chunks):
        both = [chunk_rows(wide[:half], chunk), chunk_rows(wide[half:], chunk), filler]
        far_grads.append(mm(choosers, jnp.concatenate(both, axis=0).astype(BF16), 1, 1))
    blank = jnp.zeros((HEAD_DIM, TOKENS_HERE), BF16)
    key_pos = iota((TOKENS_HERE, TOKENS_HERE), 0)
    query_pos = iota((TOKENS_HERE, TOKENS_HERE), 1)
    query_row = iota((1, TOKENS_HERE), 1)
    for head in range(heads):
        offset = offset_ref[head]
        rows = slice(head * HEAD_DIM, (head + 1) * HEAD_DIM)
        query, key, value = query_ref[rows], key_ref[rows], value_ref[rows]
        near = near_ref[head * NEAR : (head + 1) * NEAR]
        dout_head = dout[rows]
        query_over = jnp.concatenate([query, blank], axis=0)
        in_near = same_class(query_row, offset, RC)
        in_far = same_class(query_row, offset, RE)

        scores = mm(key, query, 0, 0) * SCORE_SCALE
        near_scores = mm(near, query_over, 1, 0) * SCORE_SCALE
        near_max = jnp.max(near_scores, axis=0, keepdims=True)
        peak = jnp.max(scores, axis=0, keepdims=True)
        peak = jnp.where(in_near, jnp.maximum(peak, near_max), peak)
        mass = pair_count(key_pos, query_pos, offset) * jnp.exp(scores - peak)
        near_mass = jnp.where(in_near, jnp.exp(near_scores - peak), 0.0)
        total = jnp.sum(mass, axis=0, keepdims=True) + jnp.sum(near_mass, axis=0, keepdims=True)
        log_mass = peak + jnp.log(total)
        inverse = 1.0 / total
        probs_low = (mass * inverse).astype(BF16)
        near_low = (near_mass * inverse).astype(BF16)
        attended = mm(value, probs_low, 1, 0) + mm(near, near_low, 0, 0)[HEAD_DIM:]
        delta = jnp.sum(dout_head.astype(F32) * attended, axis=0, keepdims=True)
        place = iota((SMALL, TOKENS_HERE), 0)
        stats_ref[head * SMALL : (head + 1) * SMALL] = jnp.where(place == 0, log_mass, delta)

        attended_kept = jnp.where(in_far, 0.0, attended).astype(BF16)
        over = jnp.concatenate([attended_kept, blank], axis=0)
        under = jnp.concatenate([blank, attended_kept], axis=0)
        weight_part = mm(grad[:half], over, 1, 1) + mm(grad[half:], under, 1, 1)
        weight_part = weight_part * WEIGHT_SCALE
        query_key = jnp.concatenate([query, key], axis=0)
        value_dout = jnp.concatenate([value, dout_head], axis=0)
        stats = lay_stats((HEAD_DIM, TOKENS_HERE), 0, 0, (log_mass, delta))
        attended_stats = jnp.concatenate([attended.astype(BF16), stats.astype(BF16)], axis=0)
        mine = mm(far_chooser(offset, 0), query_key, 1, 1)
        mine = mine + mm(far_chooser(offset, 1), value_dout, 1, 1)
        mine = mine + mm(far_chooser(offset, 2), attended_stats, 1, 1)
        for chunk in range(chunks):
            far_grad = far_grads[chunk][head * GAP : head * GAP + SMALL]
            parts = [chunk_rows(weight_part, chunk), mine[:SMALL] + far_grad]
            slots_ref[head * chunks + chunk] = jnp.concatenate(parts, axis=0).astype(BF16)
    rest = slots_ref.shape[0] - heads * chunks
    slots_ref[heads * chunks :] = jnp.zeros((rest,) + slots_ref.shape[1:], BF16)


def local_grad_kernel(
    offset_ref,
    query_ref,
    key_ref,
    value_ref,
    dout_ref,
    stats_ref,
    near_ref,
    back_ref,
    grad_query_ref,
    grad_key_ref,
    grad_value_ref,
):
    heads = query_ref.shape[0] // HEAD_DIM
    blank = jnp.zeros((HEAD_DIM, TOKENS_HERE), BF16)
    key_pos = iota((TOKENS_HERE, TOKENS_HERE), 0)
    query_pos = iota((TOKENS_HERE, TOKENS_HERE), 1)
    query_row = iota((1, TOKENS_HERE), 1)
    far_rows = jnp.zeros((GAP, LANES), F32)
    for head in range(heads):
        offset = offset_ref[head]
        rows = slice(head * HEAD_DIM, (head + 1) * HEAD_DIM)
        near_rows = slice(head * NEAR, (head + 1) * NEAR)
        query, key, value = query_ref[rows], key_ref[rows], value_ref[rows]
        near = near_ref[near_rows]
        dout_head = dout_ref[rows]
        log_mass = stats_ref[head * SMALL : head * SMALL + 1]
        delta = stats_ref[head * SMALL + 1 : head * SMALL + 2]
        query_over = jnp.concatenate([query, blank], axis=0)
        dout_under = jnp.concatenate([blank, dout_head], axis=0)
        in_near = same_class(query_row, offset, RC)
        in_far = same_class(query_row, offset, RE)
        near_only = in_near & jnp.logical_not(in_far)

        scores = mm(key, query, 0, 0) * SCORE_SCALE
        near_scores = mm(near, query_over, 1, 0) * SCORE_SCALE
        probs = pair_count(key_pos, query_pos, offset) * jnp.exp(scores - log_mass)
        probs = jnp.where(in_far, 0.0, probs)
        near_probs = jnp.where(near_only, jnp.exp(near_scores - log_mass), 0.0)
        grad_scores = (probs * (mm(value, dout_head, 0, 0) - delta)).astype(BF16)
        near_grad_scores = (near_probs * (mm(near, dout_under, 1, 0) - delta)).astype(BF16)
        grad_query_ref[rows] = (
            mm(key, grad_scores, 1, 0) + mm(near, near_grad_scores, 0, 0)[:HEAD_DIM]
        )
        grad_key_ref[rows] = mm(query, grad_scores, 1, 1)
        grad_value_ref[rows] = mm(dout_head, probs.astype(BF16), 1, 1)
        back = mm(near_grad_scores, query_over, 1, 1)
        back = back + mm(near_probs.astype(BF16), dout_under, 1, 1)
        back_ref[near_rows] = back.astype(BF16)
        query_dout = jnp.concatenate([query, dout_head], axis=0)
        far_rows = far_rows + mm(far_chooser(offset, head), query_dout, 1, 1)
    back_ref[heads * NEAR :] = far_rows.astype(BF16)


def merge_kernel(slots_ref, merged_ref, far_ref):
    sources = slots_ref.shape[0]
    total = jnp.zeros((SLOT, LANES), F32)
    for source in range(sources):
        block = slots_ref[source].astype(F32)
        total = total + block
        far_ref[source * SMALL : (source + 1) * SMALL] = block[CHUNK:]
    pieces = [far_ref[pl.ds(kind, sources, stride=SMALL), :] for kind in range(SMALL)]
    full = jnp.concatenate([total] + pieces, axis=0).astype(BF16)
    for plane in range(PLANES):
        merged_ref[plane] = full


def far_kernel(plane_ref, merged_ref, slots_ref, returned_ref):
    sources = slots_ref.shape[0]
    width = 2 * sources
    count = PLANES * width

    def kind(index):
        start = SLOT + index * width
        return merged_ref[:, start : start + width, :].reshape(count, LANES)

    query_key, value_dout, attended_stats, far_grad = (kind(index) for index in range(4))
    shape = (LANES, HEAD_DIM)
    lower = one_hot(iota(shape, 0) == iota(shape, 1) + HEAD_DIM)
    query, value = query_key[:, :HEAD_DIM], value_dout[:, :HEAD_DIM]
    key, dout = (mm(both, lower, 1, 0).astype(BF16) for both in (query_key, value_dout))
    local_attended = attended_stats[:, :HEAD_DIM].astype(F32)
    stats = attended_stats.astype(F32)
    local_mass = take_stat(stats, 0)

    scores = mm(query, key, 1, 1) * SCORE_SCALE
    peak = jnp.maximum(jnp.max(scores, axis=1, keepdims=True), local_mass)
    mass = jnp.exp(scores - peak)
    local_part = jnp.exp(local_mass - peak)
    total = jnp.sum(mass, axis=1, keepdims=True) + local_part
    normalizer = peak + jnp.log(total)
    inverse = 1.0 / total
    probs = mass * inverse
    probs_low = probs.astype(BF16)
    attended = local_part * inverse * local_attended + mm(probs_low, value, 1, 0)
    delta = jnp.sum(dout.astype(F32) * attended, axis=1, keepdims=True)
    grad_probs = mm(dout, value, 1, 1)
    grad_scores = (probs * (grad_probs - delta)).astype(BF16)
    grad_query = mm(grad_scores, key, 1, 0).astype(BF16)
    grad_key = mm(grad_scores, query, 0, 0).astype(BF16)
    grad_value = mm(probs_low, dout, 0, 0).astype(BF16)

    def other_plane(column):
        blocks = [column[(p ^ 1) * width : ((p ^ 1) + 1) * width] for p in range(PLANES)]
        return jnp.concatenate(blocks, axis=0)

    shape = (HEAD_DIM, LANES)
    to_left = one_hot(iota(shape, 0) == iota(shape, 1))
    to_right = one_hot(iota(shape, 0) + HEAD_DIM == iota(shape, 1))
    attended_low = attended.astype(BF16)
    over = mm(attended_low, to_left, 1, 0).astype(BF16)
    under = mm(attended_low, to_right, 1, 0).astype(BF16)
    weight_part = mm(far_grad, over, 0, 0)[:CHUNK] + mm(far_grad, under, 0, 0)[CHUNK : 2 * CHUNK]
    weight_part = weight_part * WEIGHT_SCALE
    for plane in range(PLANES):
        weight_part = weight_part + merged_ref[plane, :SLOT].astype(F32)[:CHUNK]
    own_stats = lay_stats((count, LANES), 1, HEAD_DIM, (normalizer, delta))
    other_stats = lay_stats(
        (count, LANES), 1, HEAD_DIM, (other_plane(normalizer), other_plane(delta))
    )
    returned_ref[0] = mm(grad_value, to_left, 1, 0) + other_stats
    returned_ref[1] = mm(grad_query, to_left, 1, 0) + own_stats
    returned_ref[2] = mm(grad_key, to_left, 1, 0)
    own = pl.ds(pl.multiple_of(plane_ref[0] * width, width), width)
    shape = (sources * SMALL, width)
    row, column = iota(shape, 0), iota(shape, 1)
    same = (row // SMALL) == (column % sources)
    slot_row, pair = row % SMALL, column // sources
    placed = jnp.zeros((sources * SMALL, LANES), F32)
    for index in range(returned_ref.shape[0]):
        chosen = one_hot(same & (slot_row == pair + 2 * index))
        placed = placed + mm(chosen, returned_ref[index, own, :].astype(BF16), 1, 0)
    for source in range(sources):
        parts = [weight_part, placed[source * SMALL : (source + 1) * SMALL]]
        slots_ref[source] = jnp.concatenate(parts, axis=0).astype(BF16)


def prepare_kernel(
    offset_ref,
    key_ref,
    value_ref,
    near_ref,
    own_ref,
    partner_ref,
    local_key_ref,
    local_value_ref,
    rows_ref,
    scores_ref,
    grad_probs_ref,
    keys_ref,
    chooser_ref,
    grad_key_ref,
    grad_value_ref,
):
    heads = key_ref.shape[0] // HEAD_DIM
    first_far = heads * NEAR
    blank = jnp.zeros((HEAD_DIM, TOKENS_HERE + LANES), BF16)
    shape = (GAP, GAP)
    row, column = iota(shape, 0), iota(shape, 1)
    widen = one_hot(iota((NEAR, LANES), 0) == iota((NEAR, LANES), 1))
    shape = (GAP, TOKENS_HERE + LANES)
    block_row, place = iota(shape, 0), iota(shape, 1)
    here = place < TOKENS_HERE
    from_partner, from_here = block_row < 2, (block_row >= 2) & (block_row < 4)
    for head in range(heads):
        offset = offset_ref[head]
        rows = slice(head * HEAD_DIM, (head + 1) * HEAD_DIM)
        block = slice(head * GAP, (head + 1) * GAP)
        key, value = key_ref[rows], value_ref[rows]
        near = mm(near_ref[block], widen, 0, 0).astype(BF16)
        keys = jnp.concatenate([key, near[:HEAD_DIM]], axis=1)
        values = jnp.concatenate([value, near[HEAD_DIM:]], axis=1)
        keys = jnp.concatenate([keys, blank], axis=0)
        values = jnp.concatenate([blank, values], axis=0)
        from_partner_far = one_hot((row < 2) & (column == row + 2 * head))
        from_own_far = one_hot((row >= 2) & (row < 4) & (column == row - 2 + 2 * head))
        chosen = mm(from_partner_far, partner_ref[first_far:], 1, 0)
        chosen = (chosen + mm(from_own_far, own_ref[first_far:], 1, 0)).astype(BF16)
        in_near = here & same_class(place, offset, RC)
        extra = jnp.where(here & same_class(place, offset, RB), 1.0, 0.0)
        extra = extra + jnp.where(in_near, 1.0, 0.0)
        mask_here = jnp.where(place < TOKENS_HERE + NEAR, jnp.log(1.0 + extra), ABSENT)
        mask = jnp.where(from_here, mask_here, ABSENT)
        mask = jnp.where(from_partner & in_near, 0.0, mask)
        rows_ref[block] = chosen
        scores_ref[block] = mm(chosen, keys, 1, 0) * SCORE_SCALE + mask
        grad_probs_ref[block] = mm(chosen, values, 1, 0)
        keys_ref[head] = keys
        for pair in range(3):
            chooser_ref[head, pair] = far_chooser(offset, pair)
        spread = mm(partner_ref[block], near_chooser(offset), 0, 0)
        grad_key_ref[rows] = local_key_ref[rows] + spread[:HEAD_DIM]
        grad_value_ref[rows] = local_value_ref[rows] + spread[HEAD_DIM:]


def final_kernel(
    rows_ref,
    scores_ref,
    grad_probs_ref,
    keys_ref,
    chooser_ref,
    local_query_ref,
    local_key_ref,
    local_value_ref,
    slots_ref,
    grad_query_ref,
    grad_key_ref,
    grad_value_ref,
    grad_weight_ref,
):
    heads = local_query_ref.shape[0] // HEAD_DIM
    half = grad_weight_ref.shape[1] // 2
    chunks = pl.cdiv(half, CHUNK)
    for head in range(heads):
        rows = slice(head * HEAD_DIM, (head + 1) * HEAD_DIM)
        block = slice(head * GAP, (head + 1) * GAP)
        pieces = [slots_ref[head * chunks + chunk].astype(F32) for chunk in range(chunks)]
        folded = jnp.concatenate([piece[:CHUNK] for piece in pieces], axis=0)[:half]
        unfolded = jnp.transpose(folded)
        grad_weight_ref[rows, :half] = unfolded[:HEAD_DIM]
        grad_weight_ref[rows, half:] = unfolded[HEAD_DIM:]

        returned = jnp.concatenate(
            [pieces[0][CHUNK:], jnp.zeros((GAP - SMALL, LANES), F32)], axis=0
        )
        chosen = rows_ref[block]
        probs = jnp.exp(scores_ref[block] - take_stat(returned, 0))
        grad_scores = (probs * (grad_probs_ref[block] - take_stat(returned, 1))).astype(BF16)
        probs_low = probs[:, :TOKENS_HERE].astype(BF16)
        far_query = (returned + mm(grad_scores, keys_ref[head], 1, 1)).astype(BF16)
        returned = returned.astype(BF16)
        grad_query = mm(far_query, chooser_ref[head, 1], 0, 0)[:HEAD_DIM]
        grad_key = mm(returned, chooser_ref[head, 2], 0, 0)[:HEAD_DIM]
        grad_key = grad_key + mm(chosen, grad_scores[:, :TOKENS_HERE], 0, 0)[:HEAD_DIM]
        grad_value = mm(returned, chooser_ref[head, 0], 0, 0)[:HEAD_DIM]
        grad_value = grad_value + mm(chosen, probs_low, 0, 0)[HEAD_DIM:]
        grad_query = (local_query_ref[rows] + grad_query) * SCORE_SCALE
        grad_key = (local_key_ref[rows] + grad_key) * SCORE_SCALE
        grad_query_ref[rows] = grad_query.astype(BF16)
        grad_key_ref[rows] = grad_key.astype(BF16)
        grad_value_ref[rows] = (local_value_ref[rows] + grad_value).astype(BF16)


def call(kernel, outs, arrays, scalars=0, scratch=(), space=pltpu.VMEM, limit=40 << 20):
    specs = [pl.BlockSpec(memory_space=pltpu.SMEM)] * scalars
    specs = specs + [pl.BlockSpec(memory_space=space)] * (len(arrays) - scalars)
    shapes = [jax.ShapeDtypeStruct(shape, dtype) for shape, dtype in outs]
    return pl.pallas_call(
        kernel,
        out_shape=shapes,
        in_specs=specs,
        out_specs=[pl.BlockSpec(memory_space=pltpu.VMEM)] * len(shapes),
        scratch_shapes=list(scratch),
        compiler_params=pltpu.CompilerParams(vmem_limit_bytes=limit),
        name=kernel.__name__,
    )(*arrays)


def local(queries, keys, values, grad_out, out_weight, offsets):
    features = queries.shape[0]
    model = out_weight.shape[1]
    heads = offsets.shape[0]
    sources = lax.axis_size("xz")
    near_shape = ((heads * NEAR, LANES), BF16)
    back_shape = ((heads * NEAR + GAP, LANES), BF16)
    slots_shape = ((sources, SLOT, LANES), BF16)
    merged_shape = ((PLANES, SLOT + sources * SMALL, LANES), BF16)
    wide_shape = ((features, TOKENS_HERE), F32)
    grad_shape = ((features, TOKENS_HERE), BF16)
    block_shape = ((heads * GAP, TOKENS_HERE + LANES), F32)
    other = [(i, i ^ 1) for i in range(PLANES)]

    scratch = [
        pltpu.SMEM(offsets.shape, offsets.dtype),
        pltpu.VMEM(keys.shape, keys.dtype),
        pltpu.VMEM(values.shape, values.dtype),
        pltpu.SemaphoreType.DMA((3,)),
    ]
    (near,) = call(
        near_kernel,
        [near_shape],
        (offsets, keys, values),
        scratch=scratch,
        space=pltpu.HBM,
        limit=LIMIT,
    )
    near = lax.ppermute(near, "yh", other)
    full_grad = lax.all_gather(grad_out, "dp", axis=0, tiled=True)
    slots, dout, stats = call(
        local_kernel,
        [slots_shape, grad_shape, ((heads * SMALL, TOKENS_HERE), F32)],
        (offsets, queries, keys, values, full_grad, out_weight, near),
        scalars=1,
    )
    slots = lax.all_to_all(slots, "xz", 0, 0, tiled=True)
    own, local_query, local_key, local_value = call(
        local_grad_kernel,
        [back_shape, wide_shape, wide_shape, wide_shape],
        (offsets, queries, keys, values, dout, stats, near),
        scalars=1,
    )
    (merged,) = call(
        merge_kernel,
        [merged_shape],
        (slots,),
        scratch=[pltpu.VMEM((sources * SMALL, LANES), F32)],
    )
    merged = lax.all_to_all(merged, "yh", 0, 0, tiled=True)
    partner = lax.ppermute(own, "yh", other)
    prepared = call(
        prepare_kernel,
        [
            near_shape,
            block_shape,
            block_shape,
            ((heads, LANES, TOKENS_HERE + LANES), BF16),
            ((heads, 3, GAP, TOKENS_HERE), BF16),
            wide_shape,
            wide_shape,
        ],
        (offsets, keys, values, near, own, partner, local_key, local_value),
        scalars=1,
    )
    merged, prepared, local_query = lax.optimization_barrier((merged, prepared, local_query))
    rows, scores, grad_probs, wide_keys, chooser, local_key, local_value = prepared
    plane = lax.axis_index("yh").reshape(1)
    (slots,) = call(
        far_kernel,
        [slots_shape],
        (plane, merged),
        scalars=1,
        scratch=[pltpu.VMEM((3, PLANES * sources * 2, LANES), F32)],
    )
    slots = lax.all_to_all(slots, "xz", 0, 0, tiled=True)
    return tuple(
        call(
            final_kernel,
            [grad_shape, grad_shape, grad_shape, ((features, model), F32)],
            (
                rows,
                scores,
                grad_probs,
                wide_keys,
                chooser,
                local_query,
                local_key,
                local_value,
                slots,
            ),
        )
    )


def solution(mesh):
    devices = mesh.devices.reshape(-1, PLANES, mesh.devices.shape[1])
    split_mesh = Mesh(devices, ("xz", "yh", "dp"))
    wide = P("dp", ("xz", "yh"))
    return jax.shard_map(
        local,
        mesh=split_mesh,
        in_specs=(wide, wide, wide, wide, P("dp", None), P("dp")),
        out_specs=(wide, wide, wide, P("dp", None)),
        check_vma=False,
    )
```

```python
import jax
import jax.numpy as jnp
from jax import lax
from jax.experimental import pallas as pl
from jax.experimental.pallas import tpu as pltpu
from jax.sharding import Mesh
from jax.sharding import PartitionSpec as P

HEAD_DIM = 64
TOKENS_HERE = 256
RB = 2
RC = 16
RE = 128
NEAR = TOKENS_HERE // RC
SCORE_SCALE = HEAD_DIM ** (-0.5)
WEIGHT_SCALE = 0.03125

PLANES = 4
LANES = 128
GAP = 16
SMALL = 8
CHUNK = 40
SLOT = CHUNK + SMALL
ABSENT = -1e30
LIMIT = 63_400_000

F32 = jnp.float32
BF16 = jnp.bfloat16


def mm(left, right, left_dim, right_dim):
    return lax.dot_general(
        left, right, (((left_dim,), (right_dim,)), ((), ())), preferred_element_type=F32
    )


def iota(shape, dim):
    return lax.broadcasted_iota(jnp.int32, shape, dim)


def one_hot(condition):
    return jnp.where(condition, 1.0, 0.0).astype(BF16)


def same_class(position, offset, stride):
    return (position & (stride - 1)) == (offset & (stride - 1))


def near_chooser(offset):
    shape = (NEAR, TOKENS_HERE)
    return one_hot(iota(shape, 1) == RC * iota(shape, 0) + (offset & (RC - 1)))


def far_chooser(offset, pair):
    shape = (GAP, TOKENS_HERE)
    row = iota(shape, 0)
    hit = iota(shape, 1) == RE * (row & 1) + offset
    return one_hot(hit & ((row >> 1) == pair))


def split3(value):
    high = value.astype(BF16).astype(F32)
    rest = value - high
    middle = rest.astype(BF16).astype(F32)
    return high, middle, rest - middle


def lay_stats(shape, dim, start, values):
    place = iota(shape, dim) - start
    out = jnp.zeros(shape, F32)
    for index, value in enumerate(values):
        for part_index, part in enumerate(split3(value)):
            out = jnp.where(place == 3 * index + part_index, part, out)
    return out


def take_stat(rows, index):
    place = iota(rows.shape, 1) - HEAD_DIM - 3 * index
    return jnp.sum(jnp.where((place >= 0) & (place < 3), rows, 0.0), axis=1, keepdims=True)


def chunk_rows(folded, chunk):
    rows = folded[chunk * CHUNK : (chunk + 1) * CHUNK]
    short = CHUNK - rows.shape[0]
    if short:
        rows = jnp.concatenate([rows, jnp.zeros((short,) + rows.shape[1:], rows.dtype)], axis=0)
    return rows


def near_kernel(
    offset_hbm, key_hbm, value_hbm, near_ref, offset_ref, key_ref, value_ref, semaphores
):
    pairs = ((offset_hbm, offset_ref), (key_hbm, key_ref), (value_hbm, value_ref))
    copies = [
        pltpu.make_async_copy(source, target, semaphores.at[index])
        for index, (source, target) in enumerate(pairs)
    ]
    for copy in copies:
        copy.start()
    for copy in copies:
        copy.wait()
    for head in range(key_ref.shape[0] // HEAD_DIM):
        rows = slice(head * HEAD_DIM, (head + 1) * HEAD_DIM)
        both = jnp.concatenate([key_ref[rows], value_ref[rows]], axis=0)
        picked = mm(near_chooser(offset_ref[head]), both, 1, 1)
        near_ref[head * NEAR : (head + 1) * NEAR, :] = picked.astype(BF16)


def pair_count(key_pos, query_pos, offset):
    count = 1.0 + jnp.where(
        same_class(key_pos, offset, RB) & same_class(query_pos, offset, RB), 1.0, 0.0
    )
    return count + jnp.where(
        same_class(key_pos, offset, RC) & same_class(query_pos, offset, RC), 1.0, 0.0
    )


def local_kernel(
    offset_ref,
    query_ref,
    key_ref,
    value_ref,
    grad_ref,
    weight_ref,
    near_ref,
    slots_ref,
    dout_ref,
    stats_ref,
):
    heads = query_ref.shape[0] // HEAD_DIM
    half = grad_ref.shape[0] // 2
    chunks = pl.cdiv(half, CHUNK)
    grad = grad_ref[...]
    dout = mm(weight_ref[...], grad, 1, 0).astype(BF16)
    dout_ref[...] = dout
    choosers = [far_chooser(offset_ref[head], 3) for head in range(heads)]
    choosers = jnp.concatenate(choosers, axis=0)
    wide = grad.astype(F32)
    filler = jnp.zeros((LANES - 2 * CHUNK, TOKENS_HERE), F32)
    far_grads = []
    for chunk in range(chunks):
        both = [chunk_rows(wide[:half], chunk), chunk_rows(wide[half:], chunk), filler]
        far_grads.append(mm(choosers, jnp.concatenate(both, axis=0).astype(BF16), 1, 1))
    blank = jnp.zeros((HEAD_DIM, TOKENS_HERE), BF16)
    key_pos = iota((TOKENS_HERE, TOKENS_HERE), 0)
    query_pos = iota((TOKENS_HERE, TOKENS_HERE), 1)
    query_row = iota((1, TOKENS_HERE), 1)
    heads = range(heads)
    offsets = [offset_ref[head] for head in heads]
    rows = [slice(head * HEAD_DIM, (head + 1) * HEAD_DIM) for head in heads]
    near = [near_ref[head * NEAR : (head + 1) * NEAR] for head in heads]
    in_near = [same_class(query_row, offset, RC) for offset in offsets]
    in_far = [same_class(query_row, offset, RE) for offset in offsets]
    scores = [mm(key_ref[rows[h]], query_ref[rows[h]], 0, 0) * SCORE_SCALE for h in heads]
    near_scores = [
        mm(near[h], jnp.concatenate([query_ref[rows[h]], blank], axis=0), 1, 0) * SCORE_SCALE
        for h in heads
    ]
    peak = [jnp.max(scores[h], axis=0, keepdims=True) for h in heads]
    near_max = [jnp.max(near_scores[h], axis=0, keepdims=True) for h in heads]
    peak = [jnp.where(in_near[h], jnp.maximum(peak[h], near_max[h]), peak[h]) for h in heads]
    mass = [
        pair_count(key_pos, query_pos, offsets[h]) * jnp.exp(scores[h] - peak[h]) for h in heads
    ]
    near_mass = [jnp.where(in_near[h], jnp.exp(near_scores[h] - peak[h]), 0.0) for h in heads]
    total = [
        jnp.sum(mass[h], axis=0, keepdims=True) + jnp.sum(near_mass[h], axis=0, keepdims=True)
        for h in heads
    ]
    log_mass = [peak[h] + jnp.log(total[h]) for h in heads]
    inverse = [1.0 / total[h] for h in heads]
    probs_low = [(mass[h] * inverse[h]).astype(BF16) for h in heads]
    near_low = [(near_mass[h] * inverse[h]).astype(BF16) for h in heads]
    attended = [
        mm(value_ref[rows[h]], probs_low[h], 1, 0) + mm(near[h], near_low[h], 0, 0)[HEAD_DIM:]
        for h in heads
    ]
    kept = [jnp.where(in_far[h], 0.0, attended[h]).astype(BF16) for h in heads]
    over = [jnp.concatenate([kept[h], blank], axis=0) for h in heads]
    under = [jnp.concatenate([blank, kept[h]], axis=0) for h in heads]
    weight_part = [
        (mm(grad[:half], over[h], 1, 1) + mm(grad[half:], under[h], 1, 1)) * WEIGHT_SCALE
        for h in heads
    ]
    delta = [
        jnp.sum(dout[rows[h]].astype(F32) * attended[h], axis=0, keepdims=True) for h in heads
    ]
    place = iota((SMALL, TOKENS_HERE), 0)
    for h in heads:
        query_key = jnp.concatenate([query_ref[rows[h]], key_ref[rows[h]]], axis=0)
        value_dout = jnp.concatenate([value_ref[rows[h]], dout[rows[h]]], axis=0)
        stats = lay_stats((HEAD_DIM, TOKENS_HERE), 0, 0, (log_mass[h], delta[h]))
        attended_stats = jnp.concatenate([attended[h].astype(BF16), stats.astype(BF16)], axis=0)
        mine = mm(far_chooser(offsets[h], 0), query_key, 1, 1)
        mine = mine + mm(far_chooser(offsets[h], 1), value_dout, 1, 1)
        mine = mine + mm(far_chooser(offsets[h], 2), attended_stats, 1, 1)
        stats_ref[h * SMALL : (h + 1) * SMALL] = jnp.where(place == 0, log_mass[h], delta[h])
        for chunk in range(chunks):
            far_grad = far_grads[chunk][h * GAP : h * GAP + SMALL]
            parts = [chunk_rows(weight_part[h], chunk), mine[:SMALL] + far_grad]
            slots_ref[h * chunks + chunk] = jnp.concatenate(parts, axis=0).astype(BF16)
    heads = len(heads)
    rest = slots_ref.shape[0] - heads * chunks
    slots_ref[heads * chunks :] = jnp.zeros((rest,) + slots_ref.shape[1:], BF16)


def local_grad_kernel(
    offset_ref,
    query_ref,
    key_ref,
    value_ref,
    dout_ref,
    stats_ref,
    near_ref,
    back_ref,
    grad_query_ref,
    grad_key_ref,
    grad_value_ref,
):
    heads = query_ref.shape[0] // HEAD_DIM
    blank = jnp.zeros((HEAD_DIM, TOKENS_HERE), BF16)
    key_pos = iota((TOKENS_HERE, TOKENS_HERE), 0)
    query_pos = iota((TOKENS_HERE, TOKENS_HERE), 1)
    query_row = iota((1, TOKENS_HERE), 1)
    far_rows = jnp.zeros((GAP, LANES), F32)
    for head in range(heads):
        offset = offset_ref[head]
        rows = slice(head * HEAD_DIM, (head + 1) * HEAD_DIM)
        near_rows = slice(head * NEAR, (head + 1) * NEAR)
        query, key, value = query_ref[rows], key_ref[rows], value_ref[rows]
        near = near_ref[near_rows]
        dout_head = dout_ref[rows]
        log_mass = stats_ref[head * SMALL : head * SMALL + 1]
        delta = stats_ref[head * SMALL + 1 : head * SMALL + 2]
        query_over = jnp.concatenate([query, blank], axis=0)
        dout_under = jnp.concatenate([blank, dout_head], axis=0)
        in_near = same_class(query_row, offset, RC)
        in_far = same_class(query_row, offset, RE)
        near_only = in_near & jnp.logical_not(in_far)

        scores = mm(key, query, 0, 0) * SCORE_SCALE
        near_scores = mm(near, query_over, 1, 0) * SCORE_SCALE
        probs = pair_count(key_pos, query_pos, offset) * jnp.exp(scores - log_mass)
        probs = jnp.where(in_far, 0.0, probs)
        near_probs = jnp.where(near_only, jnp.exp(near_scores - log_mass), 0.0)
        grad_scores = (probs * (mm(value, dout_head, 0, 0) - delta)).astype(BF16)
        near_grad_scores = (near_probs * (mm(near, dout_under, 1, 0) - delta)).astype(BF16)
        grad_query_ref[rows] = (
            mm(key, grad_scores, 1, 0) + mm(near, near_grad_scores, 0, 0)[:HEAD_DIM]
        )
        grad_key_ref[rows] = mm(query, grad_scores, 1, 1)
        grad_value_ref[rows] = mm(dout_head, probs.astype(BF16), 1, 1)
        back = mm(near_grad_scores, query_over, 1, 1)
        back = back + mm(near_probs.astype(BF16), dout_under, 1, 1)
        back_ref[near_rows] = back.astype(BF16)
        query_dout = jnp.concatenate([query, dout_head], axis=0)
        far_rows = far_rows + mm(far_chooser(offset, head), query_dout, 1, 1)
    back_ref[heads * NEAR :] = far_rows.astype(BF16)


def merge_kernel(slots_ref, merged_ref, far_ref):
    sources = slots_ref.shape[0]
    total = jnp.zeros((SLOT, LANES), F32)
    for source in range(sources):
        block = slots_ref[source].astype(F32)
        total = total + block
        far_ref[source * SMALL : (source + 1) * SMALL] = block[CHUNK:]
    pieces = [far_ref[pl.ds(kind, sources, stride=SMALL), :] for kind in range(SMALL)]
    full = jnp.concatenate([total] + pieces, axis=0).astype(BF16)
    for plane in range(PLANES):
        merged_ref[plane] = full


def far_kernel(plane_ref, merged_ref, slots_ref, returned_ref):
    sources = slots_ref.shape[0]
    width = 2 * sources
    count = PLANES * width

    def kind(index):
        start = SLOT + index * width
        return merged_ref[:, start : start + width, :].reshape(count, LANES)

    query_key, value_dout, attended_stats, far_grad = (kind(index) for index in range(4))
    shape = (LANES, HEAD_DIM)
    lower = one_hot(iota(shape, 0) == iota(shape, 1) + HEAD_DIM)
    query, value = query_key[:, :HEAD_DIM], value_dout[:, :HEAD_DIM]
    key, dout = (mm(both, lower, 1, 0).astype(BF16) for both in (query_key, value_dout))
    local_attended = attended_stats[:, :HEAD_DIM].astype(F32)
    stats = attended_stats.astype(F32)
    local_mass = take_stat(stats, 0)

    scores = mm(query, key, 1, 1) * SCORE_SCALE
    peak = jnp.maximum(jnp.max(scores, axis=1, keepdims=True), local_mass)
    mass = jnp.exp(scores - peak)
    local_part = jnp.exp(local_mass - peak)
    total = jnp.sum(mass, axis=1, keepdims=True) + local_part
    normalizer = peak + jnp.log(total)
    inverse = 1.0 / total
    probs = mass * inverse
    probs_low = probs.astype(BF16)
    attended = local_part * inverse * local_attended + mm(probs_low, value, 1, 0)
    delta = jnp.sum(dout.astype(F32) * attended, axis=1, keepdims=True)
    grad_probs = mm(dout, value, 1, 1)
    grad_scores = (probs * (grad_probs - delta)).astype(BF16)
    grad_query = mm(grad_scores, key, 1, 0).astype(BF16)
    grad_key = mm(grad_scores, query, 0, 0).astype(BF16)
    grad_value = mm(probs_low, dout, 0, 0).astype(BF16)

    def other_plane(column):
        blocks = [column[(p ^ 1) * width : ((p ^ 1) + 1) * width] for p in range(PLANES)]
        return jnp.concatenate(blocks, axis=0)

    shape = (HEAD_DIM, LANES)
    to_left = one_hot(iota(shape, 0) == iota(shape, 1))
    to_right = one_hot(iota(shape, 0) + HEAD_DIM == iota(shape, 1))
    attended_low = attended.astype(BF16)
    over = mm(attended_low, to_left, 1, 0).astype(BF16)
    under = mm(attended_low, to_right, 1, 0).astype(BF16)
    weight_part = mm(far_grad, over, 0, 0)[:CHUNK] + mm(far_grad, under, 0, 0)[CHUNK : 2 * CHUNK]
    weight_part = weight_part * WEIGHT_SCALE
    for plane in range(PLANES):
        weight_part = weight_part + merged_ref[plane, :SLOT].astype(F32)[:CHUNK]
    own_stats = lay_stats((count, LANES), 1, HEAD_DIM, (normalizer, delta))
    other_stats = lay_stats(
        (count, LANES), 1, HEAD_DIM, (other_plane(normalizer), other_plane(delta))
    )
    returned_ref[0] = mm(grad_value, to_left, 1, 0) + other_stats
    returned_ref[1] = mm(grad_query, to_left, 1, 0) + own_stats
    returned_ref[2] = mm(grad_key, to_left, 1, 0)
    own = pl.ds(pl.multiple_of(plane_ref[0] * width, width), width)
    shape = (sources * SMALL, width)
    row, column = iota(shape, 0), iota(shape, 1)
    same = (row // SMALL) == (column % sources)
    slot_row, pair = row % SMALL, column // sources
    placed = jnp.zeros((sources * SMALL, LANES), F32)
    for index in range(returned_ref.shape[0]):
        chosen = one_hot(same & (slot_row == pair + 2 * index))
        placed = placed + mm(chosen, returned_ref[index, own, :].astype(BF16), 1, 0)
    for source in range(sources):
        parts = [weight_part, placed[source * SMALL : (source + 1) * SMALL]]
        slots_ref[source] = jnp.concatenate(parts, axis=0).astype(BF16)


def prepare_kernel(
    offset_ref,
    key_ref,
    value_ref,
    near_ref,
    own_ref,
    partner_ref,
    local_key_ref,
    local_value_ref,
    rows_ref,
    scores_ref,
    grad_probs_ref,
    keys_ref,
    chooser_ref,
    grad_key_ref,
    grad_value_ref,
):
    heads = key_ref.shape[0] // HEAD_DIM
    first_far = heads * NEAR
    blank = jnp.zeros((HEAD_DIM, TOKENS_HERE + LANES), BF16)
    shape = (GAP, GAP)
    row, column = iota(shape, 0), iota(shape, 1)
    widen = one_hot(iota((NEAR, LANES), 0) == iota((NEAR, LANES), 1))
    shape = (GAP, TOKENS_HERE + LANES)
    block_row, place = iota(shape, 0), iota(shape, 1)
    here = place < TOKENS_HERE
    from_partner, from_here = block_row < 2, (block_row >= 2) & (block_row < 4)
    for head in range(heads):
        offset = offset_ref[head]
        rows = slice(head * HEAD_DIM, (head + 1) * HEAD_DIM)
        block = slice(head * GAP, (head + 1) * GAP)
        key, value = key_ref[rows], value_ref[rows]
        near = mm(near_ref[block], widen, 0, 0).astype(BF16)
        keys = jnp.concatenate([key, near[:HEAD_DIM]], axis=1)
        values = jnp.concatenate([value, near[HEAD_DIM:]], axis=1)
        keys = jnp.concatenate([keys, blank], axis=0)
        values = jnp.concatenate([blank, values], axis=0)
        from_partner_far = one_hot((row < 2) & (column == row + 2 * head))
        from_own_far = one_hot((row >= 2) & (row < 4) & (column == row - 2 + 2 * head))
        chosen = mm(from_partner_far, partner_ref[first_far:], 1, 0)
        chosen = (chosen + mm(from_own_far, own_ref[first_far:], 1, 0)).astype(BF16)
        in_near = here & same_class(place, offset, RC)
        extra = jnp.where(here & same_class(place, offset, RB), 1.0, 0.0)
        extra = extra + jnp.where(in_near, 1.0, 0.0)
        mask_here = jnp.where(place < TOKENS_HERE + NEAR, jnp.log(1.0 + extra), ABSENT)
        mask = jnp.where(from_here, mask_here, ABSENT)
        mask = jnp.where(from_partner & in_near, 0.0, mask)
        rows_ref[block] = chosen
        scores_ref[block] = mm(chosen, keys, 1, 0) * SCORE_SCALE + mask
        grad_probs_ref[block] = mm(chosen, values, 1, 0)
        keys_ref[head] = keys
        for pair in range(3):
            chooser_ref[head, pair] = far_chooser(offset, pair)
        spread = mm(partner_ref[block], near_chooser(offset), 0, 0)
        grad_key_ref[rows] = local_key_ref[rows] + spread[:HEAD_DIM]
        grad_value_ref[rows] = local_value_ref[rows] + spread[HEAD_DIM:]


def final_kernel(
    rows_ref,
    scores_ref,
    grad_probs_ref,
    keys_ref,
    chooser_ref,
    local_query_ref,
    local_key_ref,
    local_value_ref,
    slots_ref,
    grad_query_ref,
    grad_key_ref,
    grad_value_ref,
    grad_weight_ref,
):
    heads = local_query_ref.shape[0] // HEAD_DIM
    half = grad_weight_ref.shape[1] // 2
    chunks = pl.cdiv(half, CHUNK)
    for head in range(heads):
        rows = slice(head * HEAD_DIM, (head + 1) * HEAD_DIM)
        block = slice(head * GAP, (head + 1) * GAP)
        pieces = [slots_ref[head * chunks + chunk].astype(F32) for chunk in range(chunks)]
        folded = jnp.concatenate([piece[:CHUNK] for piece in pieces], axis=0)[:half]
        unfolded = jnp.transpose(folded)
        grad_weight_ref[rows, :half] = unfolded[:HEAD_DIM]
        grad_weight_ref[rows, half:] = unfolded[HEAD_DIM:]

        returned = jnp.concatenate(
            [pieces[0][CHUNK:], jnp.zeros((GAP - SMALL, LANES), F32)], axis=0
        )
        chosen = rows_ref[block]
        probs = jnp.exp(scores_ref[block] - take_stat(returned, 0))
        grad_scores = (probs * (grad_probs_ref[block] - take_stat(returned, 1))).astype(BF16)
        probs_low = probs[:, :TOKENS_HERE].astype(BF16)
        far_query = (returned + mm(grad_scores, keys_ref[head], 1, 1)).astype(BF16)
        returned = returned.astype(BF16)
        grad_query = mm(far_query, chooser_ref[head, 1], 0, 0)[:HEAD_DIM]
        grad_key = mm(returned, chooser_ref[head, 2], 0, 0)[:HEAD_DIM]
        grad_key = grad_key + mm(chosen, grad_scores[:, :TOKENS_HERE], 0, 0)[:HEAD_DIM]
        grad_value = mm(returned, chooser_ref[head, 0], 0, 0)[:HEAD_DIM]
        grad_value = grad_value + mm(chosen, probs_low, 0, 0)[HEAD_DIM:]
        grad_query = (local_query_ref[rows] + grad_query) * SCORE_SCALE
        grad_key = (local_key_ref[rows] + grad_key) * SCORE_SCALE
        grad_query_ref[rows] = grad_query.astype(BF16)
        grad_key_ref[rows] = grad_key.astype(BF16)
        grad_value_ref[rows] = (local_value_ref[rows] + grad_value).astype(BF16)


def call(kernel, outs, arrays, scalars=0, scratch=(), space=pltpu.VMEM, limit=40 << 20):
    specs = [pl.BlockSpec(memory_space=pltpu.SMEM)] * scalars
    specs = specs + [pl.BlockSpec(memory_space=space)] * (len(arrays) - scalars)
    shapes = [jax.ShapeDtypeStruct(shape, dtype) for shape, dtype in outs]
    return pl.pallas_call(
        kernel,
        out_shape=shapes,
        in_specs=specs,
        out_specs=[pl.BlockSpec(memory_space=pltpu.VMEM)] * len(shapes),
        scratch_shapes=list(scratch),
        compiler_params=pltpu.CompilerParams(vmem_limit_bytes=limit),
        name=kernel.__name__,
    )(*arrays)


def local(queries, keys, values, grad_out, out_weight, offsets):
    features = queries.shape[0]
    model = out_weight.shape[1]
    heads = offsets.shape[0]
    sources = lax.axis_size("xz")
    near_shape = ((heads * NEAR, LANES), BF16)
    back_shape = ((heads * NEAR + GAP, LANES), BF16)
    slots_shape = ((sources, SLOT, LANES), BF16)
    merged_shape = ((PLANES, SLOT + sources * SMALL, LANES), BF16)
    wide_shape = ((features, TOKENS_HERE), F32)
    grad_shape = ((features, TOKENS_HERE), BF16)
    block_shape = ((heads * GAP, TOKENS_HERE + LANES), F32)
    other = [(i, i ^ 1) for i in range(PLANES)]

    scratch = [
        pltpu.SMEM(offsets.shape, offsets.dtype),
        pltpu.VMEM(keys.shape, keys.dtype),
        pltpu.VMEM(values.shape, values.dtype),
        pltpu.SemaphoreType.DMA((3,)),
    ]
    (near,) = call(
        near_kernel,
        [near_shape],
        (offsets, keys, values),
        scratch=scratch,
        space=pltpu.HBM,
        limit=LIMIT,
    )
    near = lax.ppermute(near, "yh", other)
    full_grad = lax.all_gather(grad_out, "dp", axis=0, tiled=True)
    slots, dout, stats = call(
        local_kernel,
        [slots_shape, grad_shape, ((heads * SMALL, TOKENS_HERE), F32)],
        (offsets, queries, keys, values, full_grad, out_weight, near),
        scalars=1,
    )
    slots = lax.all_to_all(slots, "xz", 0, 0, tiled=True)
    own, local_query, local_key, local_value = call(
        local_grad_kernel,
        [back_shape, wide_shape, wide_shape, wide_shape],
        (offsets, queries, keys, values, dout, stats, near),
        scalars=1,
    )
    partner = lax.ppermute(own, "yh", other)
    prepared = call(
        prepare_kernel,
        [
            near_shape,
            block_shape,
            block_shape,
            ((heads, LANES, TOKENS_HERE + LANES), BF16),
            ((heads, 3, GAP, TOKENS_HERE), BF16),
            wide_shape,
            wide_shape,
        ],
        (offsets, keys, values, near, own, partner, local_key, local_value),
        scalars=1,
    )
    plane = lax.axis_index("yh").reshape(1)
    slots, prepared, local_query, plane = lax.optimization_barrier(
        (slots, prepared, local_query, plane)
    )
    rows, scores, grad_probs, wide_keys, chooser, local_key, local_value = prepared
    (merged,) = call(
        merge_kernel,
        [merged_shape],
        (slots,),
        scratch=[pltpu.VMEM((sources * SMALL, LANES), F32)],
    )
    merged = lax.all_to_all(merged, "yh", 0, 0, tiled=True)
    (slots,) = call(
        far_kernel,
        [slots_shape],
        (plane, merged),
        scalars=1,
        scratch=[pltpu.VMEM((3, PLANES * sources * 2, LANES), F32)],
    )
    slots = lax.all_to_all(slots, "xz", 0, 0, tiled=True)
    return tuple(
        call(
            final_kernel,
            [grad_shape, grad_shape, grad_shape, ((features, model), F32)],
            (
                rows,
                scores,
                grad_probs,
                wide_keys,
                chooser,
                local_query,
                local_key,
                local_value,
                slots,
            ),
        )
    )


def solution(mesh):
    devices = mesh.devices.reshape(-1, PLANES, mesh.devices.shape[1])
    split_mesh = Mesh(devices, ("xz", "yh", "dp"))
    wide = P("dp", ("xz", "yh"))
    return jax.shard_map(
        local,
        mesh=split_mesh,
        in_specs=(wide, wide, wide, wide, P("dp", None), P("dp")),
        out_specs=(wide, wide, wide, P("dp", None)),
        check_vma=False,
    )
```

```python
import jax
import jax.numpy as jnp
from jax import lax
from jax.experimental import pallas as pl
from jax.experimental.pallas import tpu as pltpu
from jax.sharding import Mesh
from jax.sharding import PartitionSpec as P

HEAD_DIM = 64
TOKENS_HERE = 256
RB = 2
RC = 16
RE = 128
NEAR = TOKENS_HERE // RC
SCORE_SCALE = HEAD_DIM ** (-0.5)
WEIGHT_SCALE = 0.03125

PLANES = 4
LANES = 128
GAP = 16
SMALL = 8
CHUNK = 40
SLOT = CHUNK + SMALL
ABSENT = -1e30
LIMIT = 63_400_000

F32 = jnp.float32
BF16 = jnp.bfloat16


def mm(left, right, left_dim, right_dim):
    return lax.dot_general(
        left, right, (((left_dim,), (right_dim,)), ((), ())), preferred_element_type=F32
    )


def iota(shape, dim):
    return lax.broadcasted_iota(jnp.int32, shape, dim)


def one_hot(condition):
    return jnp.where(condition, 1.0, 0.0).astype(BF16)


def same_class(position, offset, stride):
    return (position & (stride - 1)) == (offset & (stride - 1))


def near_chooser(offset):
    shape = (NEAR, TOKENS_HERE)
    return one_hot(iota(shape, 1) == RC * iota(shape, 0) + (offset & (RC - 1)))


def far_chooser(offset, pair):
    shape = (GAP, TOKENS_HERE)
    row = iota(shape, 0)
    hit = iota(shape, 1) == RE * (row & 1) + offset
    return one_hot(hit & ((row >> 1) == pair))


def split3(value):
    high = value.astype(BF16).astype(F32)
    rest = value - high
    middle = rest.astype(BF16).astype(F32)
    return high, middle, rest - middle


def lay_stats(shape, dim, start, values):
    place = iota(shape, dim) - start
    out = jnp.zeros(shape, F32)
    for index, value in enumerate(values):
        for part_index, part in enumerate(split3(value)):
            out = jnp.where(place == 3 * index + part_index, part, out)
    return out


def take_stat(rows, index):
    place = iota(rows.shape, 1) - HEAD_DIM - 3 * index
    return jnp.sum(jnp.where((place >= 0) & (place < 3), rows, 0.0), axis=1, keepdims=True)


def chunk_rows(folded, chunk):
    rows = folded[chunk * CHUNK : (chunk + 1) * CHUNK]
    short = CHUNK - rows.shape[0]
    if short:
        rows = jnp.concatenate([rows, jnp.zeros((short,) + rows.shape[1:], rows.dtype)], axis=0)
    return rows


def near_kernel(
    offset_hbm, key_hbm, value_hbm, near_ref, offset_ref, key_ref, value_ref, semaphores
):
    pairs = ((offset_hbm, offset_ref), (key_hbm, key_ref), (value_hbm, value_ref))
    copies = [
        pltpu.make_async_copy(source, target, semaphores.at[index])
        for index, (source, target) in enumerate(pairs)
    ]
    for copy in copies:
        copy.start()
    for copy in copies:
        copy.wait()
    for head in range(key_ref.shape[0] // HEAD_DIM):
        rows = slice(head * HEAD_DIM, (head + 1) * HEAD_DIM)
        both = jnp.concatenate([key_ref[rows], value_ref[rows]], axis=0)
        picked = mm(near_chooser(offset_ref[head]), both, 1, 1)
        near_ref[head * NEAR : (head + 1) * NEAR, :] = picked.astype(BF16)


def pair_count(key_pos, query_pos, offset):
    count = 1.0 + jnp.where(
        same_class(key_pos, offset, RB) & same_class(query_pos, offset, RB), 1.0, 0.0
    )
    return count + jnp.where(
        same_class(key_pos, offset, RC) & same_class(query_pos, offset, RC), 1.0, 0.0
    )


def local_kernel(
    offset_ref,
    side_ref,
    query_ref,
    key_ref,
    value_ref,
    grad_ref,
    weight_ref,
    near_ref,
    slots_ref,
    dout_ref,
    stats_ref,
):
    heads = query_ref.shape[0] // HEAD_DIM
    side = side_ref[0]
    blocks = [grad_ref[2 * core + (chip ^ side)] for chip in range(2) for core in range(2)]
    grad = jnp.concatenate(blocks, axis=0)
    half = grad.shape[0] // 2
    chunks = pl.cdiv(half, CHUNK)
    dout = mm(weight_ref[...], grad, 1, 0).astype(BF16)
    dout_ref[...] = dout
    choosers = [far_chooser(offset_ref[head], 3) for head in range(heads)]
    choosers = jnp.concatenate(choosers, axis=0)
    wide = grad.astype(F32)
    filler = jnp.zeros((LANES - 2 * CHUNK, TOKENS_HERE), F32)
    far_grads = []
    for chunk in range(chunks):
        both = [chunk_rows(wide[:half], chunk), chunk_rows(wide[half:], chunk), filler]
        far_grads.append(mm(choosers, jnp.concatenate(both, axis=0).astype(BF16), 1, 1))
    blank = jnp.zeros((HEAD_DIM, TOKENS_HERE), BF16)
    key_pos = iota((TOKENS_HERE, TOKENS_HERE), 0)
    query_pos = iota((TOKENS_HERE, TOKENS_HERE), 1)
    query_row = iota((1, TOKENS_HERE), 1)
    heads = range(heads)
    offsets = [offset_ref[head] for head in heads]
    rows = [slice(head * HEAD_DIM, (head + 1) * HEAD_DIM) for head in heads]
    near = [near_ref[head * NEAR : (head + 1) * NEAR] for head in heads]
    in_near = [same_class(query_row, offset, RC) for offset in offsets]
    in_far = [same_class(query_row, offset, RE) for offset in offsets]
    scores = [mm(key_ref[rows[h]], query_ref[rows[h]], 0, 0) * SCORE_SCALE for h in heads]
    near_scores = [
        mm(near[h], jnp.concatenate([query_ref[rows[h]], blank], axis=0), 1, 0) * SCORE_SCALE
        for h in heads
    ]
    peak = [jnp.max(scores[h], axis=0, keepdims=True) for h in heads]
    near_max = [jnp.max(near_scores[h], axis=0, keepdims=True) for h in heads]
    peak = [jnp.where(in_near[h], jnp.maximum(peak[h], near_max[h]), peak[h]) for h in heads]
    mass = [
        pair_count(key_pos, query_pos, offsets[h]) * jnp.exp(scores[h] - peak[h]) for h in heads
    ]
    near_mass = [jnp.where(in_near[h], jnp.exp(near_scores[h] - peak[h]), 0.0) for h in heads]
    total = [
        jnp.sum(mass[h], axis=0, keepdims=True) + jnp.sum(near_mass[h], axis=0, keepdims=True)
        for h in heads
    ]
    log_mass = [peak[h] + jnp.log(total[h]) for h in heads]
    inverse = [1.0 / total[h] for h in heads]
    probs_low = [(mass[h] * inverse[h]).astype(BF16) for h in heads]
    near_low = [(near_mass[h] * inverse[h]).astype(BF16) for h in heads]
    attended = [
        mm(value_ref[rows[h]], probs_low[h], 1, 0) + mm(near[h], near_low[h], 0, 0)[HEAD_DIM:]
        for h in heads
    ]
    kept = [jnp.where(in_far[h], 0.0, attended[h]).astype(BF16) for h in heads]
    over = [jnp.concatenate([kept[h], blank], axis=0) for h in heads]
    under = [jnp.concatenate([blank, kept[h]], axis=0) for h in heads]
    weight_part = [
        (mm(grad[:half], over[h], 1, 1) + mm(grad[half:], under[h], 1, 1)) * WEIGHT_SCALE
        for h in heads
    ]
    delta = [
        jnp.sum(dout[rows[h]].astype(F32) * attended[h], axis=0, keepdims=True) for h in heads
    ]
    place = iota((SMALL, TOKENS_HERE), 0)
    for h in heads:
        query_key = jnp.concatenate([query_ref[rows[h]], key_ref[rows[h]]], axis=0)
        value_dout = jnp.concatenate([value_ref[rows[h]], dout[rows[h]]], axis=0)
        stats = lay_stats((HEAD_DIM, TOKENS_HERE), 0, 0, (log_mass[h], delta[h]))
        attended_stats = jnp.concatenate([attended[h].astype(BF16), stats.astype(BF16)], axis=0)
        mine = mm(far_chooser(offsets[h], 0), query_key, 1, 1)
        mine = mine + mm(far_chooser(offsets[h], 1), value_dout, 1, 1)
        mine = mine + mm(far_chooser(offsets[h], 2), attended_stats, 1, 1)
        stats_ref[h * SMALL : (h + 1) * SMALL] = jnp.where(place == 0, log_mass[h], delta[h])
        for chunk in range(chunks):
            far_grad = far_grads[chunk][h * GAP : h * GAP + SMALL]
            parts = [chunk_rows(weight_part[h], chunk), mine[:SMALL] + far_grad]
            slots_ref[h * chunks + chunk] = jnp.concatenate(parts, axis=0).astype(BF16)
    heads = len(heads)
    rest = slots_ref.shape[0] - heads * chunks
    slots_ref[heads * chunks :] = jnp.zeros((rest,) + slots_ref.shape[1:], BF16)


def local_grad_kernel(
    offset_ref,
    query_ref,
    key_ref,
    value_ref,
    dout_ref,
    stats_ref,
    near_ref,
    back_ref,
    grad_query_ref,
    grad_key_ref,
    grad_value_ref,
):
    heads = query_ref.shape[0] // HEAD_DIM
    blank = jnp.zeros((HEAD_DIM, TOKENS_HERE), BF16)
    key_pos = iota((TOKENS_HERE, TOKENS_HERE), 0)
    query_pos = iota((TOKENS_HERE, TOKENS_HERE), 1)
    query_row = iota((1, TOKENS_HERE), 1)
    far_rows = jnp.zeros((GAP, LANES), F32)
    for head in range(heads):
        offset = offset_ref[head]
        rows = slice(head * HEAD_DIM, (head + 1) * HEAD_DIM)
        near_rows = slice(head * NEAR, (head + 1) * NEAR)
        query, key, value = query_ref[rows], key_ref[rows], value_ref[rows]
        near = near_ref[near_rows]
        dout_head = dout_ref[rows]
        log_mass = stats_ref[head * SMALL : head * SMALL + 1]
        delta = stats_ref[head * SMALL + 1 : head * SMALL + 2]
        query_over = jnp.concatenate([query, blank], axis=0)
        dout_under = jnp.concatenate([blank, dout_head], axis=0)
        in_near = same_class(query_row, offset, RC)
        in_far = same_class(query_row, offset, RE)
        near_only = in_near & jnp.logical_not(in_far)

        scores = mm(key, query, 0, 0) * SCORE_SCALE
        near_scores = mm(near, query_over, 1, 0) * SCORE_SCALE
        probs = pair_count(key_pos, query_pos, offset) * jnp.exp(scores - log_mass)
        probs = jnp.where(in_far, 0.0, probs)
        near_probs = jnp.where(near_only, jnp.exp(near_scores - log_mass), 0.0)
        grad_scores = (probs * (mm(value, dout_head, 0, 0) - delta)).astype(BF16)
        near_grad_scores = (near_probs * (mm(near, dout_under, 1, 0) - delta)).astype(BF16)
        grad_query_ref[rows] = (
            mm(key, grad_scores, 1, 0) + mm(near, near_grad_scores, 0, 0)[:HEAD_DIM]
        )
        grad_key_ref[rows] = mm(query, grad_scores, 1, 1)
        grad_value_ref[rows] = mm(dout_head, probs.astype(BF16), 1, 1)
        back = mm(near_grad_scores, query_over, 1, 1)
        back = back + mm(near_probs.astype(BF16), dout_under, 1, 1)
        back_ref[near_rows] = back.astype(BF16)
        query_dout = jnp.concatenate([query, dout_head], axis=0)
        far_rows = far_rows + mm(far_chooser(offset, head), query_dout, 1, 1)
    back_ref[heads * NEAR :] = far_rows.astype(BF16)


def merge_kernel(slots_ref, merged_ref, far_ref):
    sources = slots_ref.shape[0]
    total = jnp.zeros((SLOT, LANES), F32)
    for source in range(sources):
        block = slots_ref[source].astype(F32)
        total = total + block
        far_ref[source * SMALL : (source + 1) * SMALL] = block[CHUNK:]
    pieces = [far_ref[pl.ds(kind, sources, stride=SMALL), :] for kind in range(SMALL)]
    full = jnp.concatenate([total] + pieces, axis=0).astype(BF16)
    for plane in range(PLANES):
        merged_ref[plane] = full


def far_kernel(plane_ref, merged_ref, slots_ref, returned_ref):
    sources = slots_ref.shape[0]
    width = 2 * sources
    count = PLANES * width

    def kind(index):
        start = SLOT + index * width
        return merged_ref[:, start : start + width, :].reshape(count, LANES)

    query_key, value_dout, attended_stats, far_grad = (kind(index) for index in range(4))
    shape = (LANES, HEAD_DIM)
    lower = one_hot(iota(shape, 0) == iota(shape, 1) + HEAD_DIM)
    query, value = query_key[:, :HEAD_DIM], value_dout[:, :HEAD_DIM]
    key, dout = (mm(both, lower, 1, 0).astype(BF16) for both in (query_key, value_dout))
    local_attended = attended_stats[:, :HEAD_DIM].astype(F32)
    stats = attended_stats.astype(F32)
    local_mass = take_stat(stats, 0)

    scores = mm(query, key, 1, 1) * SCORE_SCALE
    peak = jnp.maximum(jnp.max(scores, axis=1, keepdims=True), local_mass)
    mass = jnp.exp(scores - peak)
    local_part = jnp.exp(local_mass - peak)
    total = jnp.sum(mass, axis=1, keepdims=True) + local_part
    normalizer = peak + jnp.log(total)
    inverse = 1.0 / total
    probs = mass * inverse
    probs_low = probs.astype(BF16)
    attended = local_part * inverse * local_attended + mm(probs_low, value, 1, 0)
    delta = jnp.sum(dout.astype(F32) * attended, axis=1, keepdims=True)
    grad_probs = mm(dout, value, 1, 1)
    grad_scores = (probs * (grad_probs - delta)).astype(BF16)
    grad_query = mm(grad_scores, key, 1, 0).astype(BF16)
    grad_key = mm(grad_scores, query, 0, 0).astype(BF16)
    grad_value = mm(probs_low, dout, 0, 0).astype(BF16)

    def other_plane(column):
        blocks = [column[(p ^ 1) * width : ((p ^ 1) + 1) * width] for p in range(PLANES)]
        return jnp.concatenate(blocks, axis=0)

    shape = (HEAD_DIM, LANES)
    to_left = one_hot(iota(shape, 0) == iota(shape, 1))
    to_right = one_hot(iota(shape, 0) + HEAD_DIM == iota(shape, 1))
    attended_low = attended.astype(BF16)
    over = mm(attended_low, to_left, 1, 0).astype(BF16)
    under = mm(attended_low, to_right, 1, 0).astype(BF16)
    weight_part = mm(far_grad, over, 0, 0)[:CHUNK] + mm(far_grad, under, 0, 0)[CHUNK : 2 * CHUNK]
    weight_part = weight_part * WEIGHT_SCALE
    for plane in range(PLANES):
        weight_part = weight_part + merged_ref[plane, :SLOT].astype(F32)[:CHUNK]
    own_stats = lay_stats((count, LANES), 1, HEAD_DIM, (normalizer, delta))
    other_stats = lay_stats(
        (count, LANES), 1, HEAD_DIM, (other_plane(normalizer), other_plane(delta))
    )
    returned_ref[0] = mm(grad_value, to_left, 1, 0) + other_stats
    returned_ref[1] = mm(grad_query, to_left, 1, 0) + own_stats
    returned_ref[2] = mm(grad_key, to_left, 1, 0)
    own = pl.ds(pl.multiple_of(plane_ref[0] * width, width), width)
    shape = (sources * SMALL, width)
    row, column = iota(shape, 0), iota(shape, 1)
    same = (row // SMALL) == (column % sources)
    slot_row, pair = row % SMALL, column // sources
    placed = jnp.zeros((sources * SMALL, LANES), F32)
    for index in range(returned_ref.shape[0]):
        chosen = one_hot(same & (slot_row == pair + 2 * index))
        placed = placed + mm(chosen, returned_ref[index, own, :].astype(BF16), 1, 0)
    for source in range(sources):
        parts = [weight_part, placed[source * SMALL : (source + 1) * SMALL]]
        slots_ref[source] = jnp.concatenate(parts, axis=0).astype(BF16)


def prepare_kernel(
    offset_ref,
    key_ref,
    value_ref,
    near_ref,
    own_ref,
    partner_ref,
    local_key_ref,
    local_value_ref,
    rows_ref,
    scores_ref,
    grad_probs_ref,
    keys_ref,
    chooser_ref,
    grad_key_ref,
    grad_value_ref,
):
    heads = key_ref.shape[0] // HEAD_DIM
    first_far = heads * NEAR
    blank = jnp.zeros((HEAD_DIM, TOKENS_HERE + LANES), BF16)
    shape = (GAP, GAP)
    row, column = iota(shape, 0), iota(shape, 1)
    widen = one_hot(iota((NEAR, LANES), 0) == iota((NEAR, LANES), 1))
    shape = (GAP, TOKENS_HERE + LANES)
    block_row, place = iota(shape, 0), iota(shape, 1)
    here = place < TOKENS_HERE
    from_partner, from_here = block_row < 2, (block_row >= 2) & (block_row < 4)
    for head in range(heads):
        offset = offset_ref[head]
        rows = slice(head * HEAD_DIM, (head + 1) * HEAD_DIM)
        block = slice(head * GAP, (head + 1) * GAP)
        key, value = key_ref[rows], value_ref[rows]
        near = mm(near_ref[block], widen, 0, 0).astype(BF16)
        keys = jnp.concatenate([key, near[:HEAD_DIM]], axis=1)
        values = jnp.concatenate([value, near[HEAD_DIM:]], axis=1)
        keys = jnp.concatenate([keys, blank], axis=0)
        values = jnp.concatenate([blank, values], axis=0)
        from_partner_far = one_hot((row < 2) & (column == row + 2 * head))
        from_own_far = one_hot((row >= 2) & (row < 4) & (column == row - 2 + 2 * head))
        chosen = mm(from_partner_far, partner_ref[first_far:], 1, 0)
        chosen = (chosen + mm(from_own_far, own_ref[first_far:], 1, 0)).astype(BF16)
        in_near = here & same_class(place, offset, RC)
        extra = jnp.where(here & same_class(place, offset, RB), 1.0, 0.0)
        extra = extra + jnp.where(in_near, 1.0, 0.0)
        mask_here = jnp.where(place < TOKENS_HERE + NEAR, jnp.log(1.0 + extra), ABSENT)
        mask = jnp.where(from_here, mask_here, ABSENT)
        mask = jnp.where(from_partner & in_near, 0.0, mask)
        rows_ref[block] = chosen
        scores_ref[block] = mm(chosen, keys, 1, 0) * SCORE_SCALE + mask
        grad_probs_ref[block] = mm(chosen, values, 1, 0)
        keys_ref[head] = keys
        for pair in range(3):
            chooser_ref[head, pair] = far_chooser(offset, pair)
        spread = mm(partner_ref[block], near_chooser(offset), 0, 0)
        grad_key_ref[rows] = local_key_ref[rows] + spread[:HEAD_DIM]
        grad_value_ref[rows] = local_value_ref[rows] + spread[HEAD_DIM:]


def final_kernel(
    rows_ref,
    scores_ref,
    grad_probs_ref,
    keys_ref,
    chooser_ref,
    local_query_ref,
    local_key_ref,
    local_value_ref,
    slots_ref,
    grad_query_ref,
    grad_key_ref,
    grad_value_ref,
    grad_weight_ref,
):
    heads = local_query_ref.shape[0] // HEAD_DIM
    half = grad_weight_ref.shape[1] // 2
    chunks = pl.cdiv(half, CHUNK)
    for head in range(heads):
        rows = slice(head * HEAD_DIM, (head + 1) * HEAD_DIM)
        block = slice(head * GAP, (head + 1) * GAP)
        pieces = [slots_ref[head * chunks + chunk].astype(F32) for chunk in range(chunks)]
        folded = jnp.concatenate([piece[:CHUNK] for piece in pieces], axis=0)[:half]
        unfolded = jnp.transpose(folded)
        grad_weight_ref[rows, :half] = unfolded[:HEAD_DIM]
        grad_weight_ref[rows, half:] = unfolded[HEAD_DIM:]

        returned = jnp.concatenate(
            [pieces[0][CHUNK:], jnp.zeros((GAP - SMALL, LANES), F32)], axis=0
        )
        chosen = rows_ref[block]
        probs = jnp.exp(scores_ref[block] - take_stat(returned, 0))
        grad_scores = (probs * (grad_probs_ref[block] - take_stat(returned, 1))).astype(BF16)
        probs_low = probs[:, :TOKENS_HERE].astype(BF16)
        far_query = (returned + mm(grad_scores, keys_ref[head], 1, 1)).astype(BF16)
        returned = returned.astype(BF16)
        grad_query = mm(far_query, chooser_ref[head, 1], 0, 0)[:HEAD_DIM]
        grad_key = mm(returned, chooser_ref[head, 2], 0, 0)[:HEAD_DIM]
        grad_key = grad_key + mm(chosen, grad_scores[:, :TOKENS_HERE], 0, 0)[:HEAD_DIM]
        grad_value = mm(returned, chooser_ref[head, 0], 0, 0)[:HEAD_DIM]
        grad_value = grad_value + mm(chosen, probs_low, 0, 0)[HEAD_DIM:]
        grad_query = (local_query_ref[rows] + grad_query) * SCORE_SCALE
        grad_key = (local_key_ref[rows] + grad_key) * SCORE_SCALE
        grad_query_ref[rows] = grad_query.astype(BF16)
        grad_key_ref[rows] = grad_key.astype(BF16)
        grad_value_ref[rows] = (local_value_ref[rows] + grad_value).astype(BF16)


def call(kernel, outs, arrays, scalars=0, scratch=(), space=pltpu.VMEM, limit=40 << 20):
    specs = [pl.BlockSpec(memory_space=pltpu.SMEM)] * scalars
    specs = specs + [pl.BlockSpec(memory_space=space)] * (len(arrays) - scalars)
    shapes = [jax.ShapeDtypeStruct(shape, dtype) for shape, dtype in outs]
    return pl.pallas_call(
        kernel,
        out_shape=shapes,
        in_specs=specs,
        out_specs=[pl.BlockSpec(memory_space=pltpu.VMEM)] * len(shapes),
        scratch_shapes=list(scratch),
        compiler_params=pltpu.CompilerParams(vmem_limit_bytes=limit),
        name=kernel.__name__,
    )(*arrays)


def local(queries, keys, values, grad_out, out_weight, offsets):
    features = queries.shape[0]
    model = out_weight.shape[1]
    heads = offsets.shape[0]
    sources = lax.axis_size("xz")
    near_shape = ((heads * NEAR, LANES), BF16)
    back_shape = ((heads * NEAR + GAP, LANES), BF16)
    slots_shape = ((sources, SLOT, LANES), BF16)
    merged_shape = ((PLANES, SLOT + sources * SMALL, LANES), BF16)
    wide_shape = ((features, TOKENS_HERE), F32)
    grad_shape = ((features, TOKENS_HERE), BF16)
    block_shape = ((heads * GAP, TOKENS_HERE + LANES), F32)
    other = [(i, i ^ 1) for i in range(PLANES)]

    scratch = [
        pltpu.SMEM(offsets.shape, offsets.dtype),
        pltpu.VMEM(keys.shape, keys.dtype),
        pltpu.VMEM(values.shape, values.dtype),
        pltpu.SemaphoreType.DMA((3,)),
    ]
    other_grad = lax.ppermute(grad_out, "chip", [(0, 1), (1, 0)])
    (near,) = call(
        near_kernel,
        [near_shape],
        (offsets, keys, values),
        scratch=scratch,
        space=pltpu.HBM,
        limit=LIMIT,
    )
    near = lax.ppermute(near, "yh", other)
    pair_grads = lax.all_gather(jnp.stack([grad_out, other_grad]), "core", axis=0, tiled=True)
    side = lax.axis_index("chip").reshape(1)
    slots, dout, stats = call(
        local_kernel,
        [slots_shape, grad_shape, ((heads * SMALL, TOKENS_HERE), F32)],
        (offsets, side, queries, keys, values, pair_grads, out_weight, near),
        scalars=2,
    )
    slots = lax.all_to_all(slots, "xz", 0, 0, tiled=True)
    own, local_query, local_key, local_value = call(
        local_grad_kernel,
        [back_shape, wide_shape, wide_shape, wide_shape],
        (offsets, queries, keys, values, dout, stats, near),
        scalars=1,
    )
    partner = lax.ppermute(own, "yh", other)
    prepared = call(
        prepare_kernel,
        [
            near_shape,
            block_shape,
            block_shape,
            ((heads, LANES, TOKENS_HERE + LANES), BF16),
            ((heads, 3, GAP, TOKENS_HERE), BF16),
            wide_shape,
            wide_shape,
        ],
        (offsets, keys, values, near, own, partner, local_key, local_value),
        scalars=1,
    )
    plane = lax.axis_index("yh").reshape(1)
    slots, prepared, local_query, plane = lax.optimization_barrier(
        (slots, prepared, local_query, plane)
    )
    rows, scores, grad_probs, wide_keys, chooser, local_key, local_value = prepared
    (merged,) = call(
        merge_kernel,
        [merged_shape],
        (slots,),
        scratch=[pltpu.VMEM((sources * SMALL, LANES), F32)],
    )
    merged = lax.all_to_all(merged, "yh", 0, 0, tiled=True)
    (slots,) = call(
        far_kernel,
        [slots_shape],
        (plane, merged),
        scalars=1,
        scratch=[pltpu.VMEM((3, PLANES * sources * 2, LANES), F32)],
    )
    slots = lax.all_to_all(slots, "xz", 0, 0, tiled=True)
    return tuple(
        call(
            final_kernel,
            [grad_shape, grad_shape, grad_shape, ((features, model), F32)],
            (
                rows,
                scores,
                grad_probs,
                wide_keys,
                chooser,
                local_query,
                local_key,
                local_value,
                slots,
            ),
        )
    )


def solution(mesh):
    devices = mesh.devices.reshape(-1, PLANES, 2, mesh.devices.shape[1] // 2)
    split_mesh = Mesh(devices, ("xz", "yh", "chip", "core"))
    parts = ("chip", "core")
    wide = P(parts, ("xz", "yh"))
    return jax.shard_map(
        local,
        mesh=split_mesh,
        in_specs=(wide, wide, wide, wide, P(parts, None), P(parts)),
        out_specs=(wide, wide, wide, P(parts, None)),
        check_vma=False,
    )
```

```python
import jax
import jax.numpy as jnp
from jax import lax
from jax.experimental import pallas as pl
from jax.experimental.pallas import tpu as pltpu
from jax.sharding import Mesh
from jax.sharding import PartitionSpec as P

HEAD_DIM = 64
TOKENS_HERE = 256
RB = 2
RC = 16
RE = 128
NEAR = TOKENS_HERE // RC
SCORE_SCALE = HEAD_DIM ** (-0.5)
WEIGHT_SCALE = 0.03125

PLANES = 4
LANES = 128
GAP = 16
SMALL = 8
CHUNK = 40
SLOT = CHUNK + SMALL
ABSENT = -1e30
LIMIT = 63_400_000

F32 = jnp.float32
BF16 = jnp.bfloat16


def mm(left, right, left_dim, right_dim):
    return lax.dot_general(
        left, right, (((left_dim,), (right_dim,)), ((), ())), preferred_element_type=F32
    )


def iota(shape, dim):
    return lax.broadcasted_iota(jnp.int32, shape, dim)


def one_hot(condition):
    return jnp.where(condition, 1.0, 0.0).astype(BF16)


def same_class(position, offset, stride):
    return (position & (stride - 1)) == (offset & (stride - 1))


def near_chooser(offset):
    shape = (NEAR, TOKENS_HERE)
    return one_hot(iota(shape, 1) == RC * iota(shape, 0) + (offset & (RC - 1)))


def far_chooser(offset, pair):
    shape = (GAP, TOKENS_HERE)
    row = iota(shape, 0)
    hit = iota(shape, 1) == RE * (row & 1) + offset
    return one_hot(hit & ((row >> 1) == pair))


def split3(value):
    high = value.astype(BF16).astype(F32)
    rest = value - high
    middle = rest.astype(BF16).astype(F32)
    return high, middle, rest - middle


def lay_stats(shape, dim, start, values):
    place = iota(shape, dim) - start
    out = jnp.zeros(shape, F32)
    for index, value in enumerate(values):
        for part_index, part in enumerate(split3(value)):
            out = jnp.where(place == 3 * index + part_index, part, out)
    return out


def take_stat(rows, index):
    place = iota(rows.shape, 1) - HEAD_DIM - 3 * index
    return jnp.sum(jnp.where((place >= 0) & (place < 3), rows, 0.0), axis=1, keepdims=True)


def chunk_rows(folded, chunk):
    rows = folded[chunk * CHUNK : (chunk + 1) * CHUNK]
    short = CHUNK - rows.shape[0]
    if short:
        rows = jnp.concatenate([rows, jnp.zeros((short,) + rows.shape[1:], rows.dtype)], axis=0)
    return rows


def near_kernel(
    offset_hbm, key_hbm, value_hbm, near_ref, offset_ref, key_ref, value_ref, semaphores
):
    pairs = ((offset_hbm, offset_ref), (key_hbm, key_ref), (value_hbm, value_ref))
    copies = [
        pltpu.make_async_copy(source, target, semaphores.at[index])
        for index, (source, target) in enumerate(pairs)
    ]
    for copy in copies:
        copy.start()
    for copy in copies:
        copy.wait()
    for head in range(key_ref.shape[0] // HEAD_DIM):
        rows = slice(head * HEAD_DIM, (head + 1) * HEAD_DIM)
        both = jnp.concatenate([key_ref[rows], value_ref[rows]], axis=0)
        picked = mm(near_chooser(offset_ref[head]), both, 1, 1)
        near_ref[head * NEAR : (head + 1) * NEAR, :] = picked.astype(BF16)
    heads = near_ref.shape[0] // NEAR - 1
    row = iota((GAP, LANES), 0)
    told = jnp.zeros((GAP, LANES), F32)
    for head in range(heads):
        told = jnp.where(row == head, offset_ref[head].astype(F32), told)
    near_ref[heads * NEAR :] = told.astype(BF16)


def told_offset(near_ref, head):
    told = near_ref[near_ref.shape[0] - GAP :].astype(F32)
    return told[head : head + 1, :1].astype(jnp.int32)


def pair_count(key_pos, query_pos, offset):
    count = 1.0 + jnp.where(
        same_class(key_pos, offset, RB) & same_class(query_pos, offset, RB), 1.0, 0.0
    )
    return count + jnp.where(
        same_class(key_pos, offset, RC) & same_class(query_pos, offset, RC), 1.0, 0.0
    )


def local_kernel(
    side_ref,
    query_ref,
    key_ref,
    value_ref,
    grad_ref,
    weight_ref,
    near_ref,
    slots_ref,
    dout_ref,
    stats_ref,
):
    heads = query_ref.shape[0] // HEAD_DIM
    side = side_ref[0]
    blocks = [grad_ref[2 * core + (chip ^ side)] for chip in range(2) for core in range(2)]
    grad = jnp.concatenate(blocks, axis=0)
    half = grad.shape[0] // 2
    chunks = pl.cdiv(half, CHUNK)
    dout = mm(weight_ref[...], grad, 1, 0).astype(BF16)
    dout_ref[...] = dout
    offsets = [told_offset(near_ref, head) for head in range(heads)]
    choosers = [far_chooser(offsets[head], 3) for head in range(heads)]
    choosers = jnp.concatenate(choosers, axis=0)
    wide = grad.astype(F32)
    filler = jnp.zeros((LANES - 2 * CHUNK, TOKENS_HERE), F32)
    far_grads = []
    for chunk in range(chunks):
        both = [chunk_rows(wide[:half], chunk), chunk_rows(wide[half:], chunk), filler]
        far_grads.append(mm(choosers, jnp.concatenate(both, axis=0).astype(BF16), 1, 1))
    blank = jnp.zeros((HEAD_DIM, TOKENS_HERE), BF16)
    key_pos = iota((TOKENS_HERE, TOKENS_HERE), 0)
    query_pos = iota((TOKENS_HERE, TOKENS_HERE), 1)
    query_row = iota((1, TOKENS_HERE), 1)
    heads = range(heads)
    rows = [slice(head * HEAD_DIM, (head + 1) * HEAD_DIM) for head in heads]
    near = [near_ref[head * NEAR : (head + 1) * NEAR] for head in heads]
    in_near = [same_class(query_row, offset, RC) for offset in offsets]
    in_far = [same_class(query_row, offset, RE) for offset in offsets]
    scores = [mm(key_ref[rows[h]], query_ref[rows[h]], 0, 0) * SCORE_SCALE for h in heads]
    near_scores = [
        mm(near[h], jnp.concatenate([query_ref[rows[h]], blank], axis=0), 1, 0) * SCORE_SCALE
        for h in heads
    ]
    peak = [jnp.max(scores[h], axis=0, keepdims=True) for h in heads]
    near_max = [jnp.max(near_scores[h], axis=0, keepdims=True) for h in heads]
    peak = [jnp.where(in_near[h], jnp.maximum(peak[h], near_max[h]), peak[h]) for h in heads]
    mass = [
        pair_count(key_pos, query_pos, offsets[h]) * jnp.exp(scores[h] - peak[h]) for h in heads
    ]
    near_mass = [jnp.where(in_near[h], jnp.exp(near_scores[h] - peak[h]), 0.0) for h in heads]
    total = [
        jnp.sum(mass[h], axis=0, keepdims=True) + jnp.sum(near_mass[h], axis=0, keepdims=True)
        for h in heads
    ]
    log_mass = [peak[h] + jnp.log(total[h]) for h in heads]
    inverse = [1.0 / total[h] for h in heads]
    probs_low = [(mass[h] * inverse[h]).astype(BF16) for h in heads]
    near_low = [(near_mass[h] * inverse[h]).astype(BF16) for h in heads]
    attended = [
        mm(value_ref[rows[h]], probs_low[h], 1, 0) + mm(near[h], near_low[h], 0, 0)[HEAD_DIM:]
        for h in heads
    ]
    kept = [jnp.where(in_far[h], 0.0, attended[h]).astype(BF16) for h in heads]
    over = [jnp.concatenate([kept[h], blank], axis=0) for h in heads]
    under = [jnp.concatenate([blank, kept[h]], axis=0) for h in heads]
    weight_part = [
        (mm(grad[:half], over[h], 1, 1) + mm(grad[half:], under[h], 1, 1)) * WEIGHT_SCALE
        for h in heads
    ]
    delta = [
        jnp.sum(dout[rows[h]].astype(F32) * attended[h], axis=0, keepdims=True) for h in heads
    ]
    place = iota((SMALL, TOKENS_HERE), 0)
    for h in heads:
        query_key = jnp.concatenate([query_ref[rows[h]], key_ref[rows[h]]], axis=0)
        value_dout = jnp.concatenate([value_ref[rows[h]], dout[rows[h]]], axis=0)
        stats = lay_stats((HEAD_DIM, TOKENS_HERE), 0, 0, (log_mass[h], delta[h]))
        attended_stats = jnp.concatenate([attended[h].astype(BF16), stats.astype(BF16)], axis=0)
        mine = mm(far_chooser(offsets[h], 0), query_key, 1, 1)
        mine = mine + mm(far_chooser(offsets[h], 1), value_dout, 1, 1)
        mine = mine + mm(far_chooser(offsets[h], 2), attended_stats, 1, 1)
        stats_ref[h * SMALL : (h + 1) * SMALL] = jnp.where(place == 0, log_mass[h], delta[h])
        for chunk in range(chunks):
            far_grad = far_grads[chunk][h * GAP : h * GAP + SMALL]
            parts = [chunk_rows(weight_part[h], chunk), mine[:SMALL] + far_grad]
            slots_ref[h * chunks + chunk] = jnp.concatenate(parts, axis=0).astype(BF16)
    heads = len(heads)
    rest = slots_ref.shape[0] - heads * chunks
    slots_ref[heads * chunks :] = jnp.zeros((rest,) + slots_ref.shape[1:], BF16)


def local_grad_kernel(
    query_ref,
    key_ref,
    value_ref,
    dout_ref,
    stats_ref,
    near_ref,
    back_ref,
    grad_query_ref,
    grad_key_ref,
    grad_value_ref,
):
    heads = query_ref.shape[0] // HEAD_DIM
    blank = jnp.zeros((HEAD_DIM, TOKENS_HERE), BF16)
    key_pos = iota((TOKENS_HERE, TOKENS_HERE), 0)
    query_pos = iota((TOKENS_HERE, TOKENS_HERE), 1)
    query_row = iota((1, TOKENS_HERE), 1)
    far_rows = jnp.zeros((GAP, LANES), F32)
    for head in range(heads):
        offset = told_offset(near_ref, head)
        rows = slice(head * HEAD_DIM, (head + 1) * HEAD_DIM)
        near_rows = slice(head * NEAR, (head + 1) * NEAR)
        query, key, value = query_ref[rows], key_ref[rows], value_ref[rows]
        near = near_ref[near_rows]
        dout_head = dout_ref[rows]
        log_mass = stats_ref[head * SMALL : head * SMALL + 1]
        delta = stats_ref[head * SMALL + 1 : head * SMALL + 2]
        query_over = jnp.concatenate([query, blank], axis=0)
        dout_under = jnp.concatenate([blank, dout_head], axis=0)
        in_near = same_class(query_row, offset, RC)
        in_far = same_class(query_row, offset, RE)
        near_only = in_near & jnp.logical_not(in_far)

        scores = mm(key, query, 0, 0) * SCORE_SCALE
        near_scores = mm(near, query_over, 1, 0) * SCORE_SCALE
        probs = pair_count(key_pos, query_pos, offset) * jnp.exp(scores - log_mass)
        probs = jnp.where(in_far, 0.0, probs)
        near_probs = jnp.where(near_only, jnp.exp(near_scores - log_mass), 0.0)
        grad_scores = (probs * (mm(value, dout_head, 0, 0) - delta)).astype(BF16)
        near_grad_scores = (near_probs * (mm(near, dout_under, 1, 0) - delta)).astype(BF16)
        grad_query_ref[rows] = (
            mm(key, grad_scores, 1, 0) + mm(near, near_grad_scores, 0, 0)[:HEAD_DIM]
        )
        grad_key_ref[rows] = mm(query, grad_scores, 1, 1)
        grad_value_ref[rows] = mm(dout_head, probs.astype(BF16), 1, 1)
        back = mm(near_grad_scores, query_over, 1, 1)
        back = back + mm(near_probs.astype(BF16), dout_under, 1, 1)
        back_ref[near_rows] = back.astype(BF16)
        query_dout = jnp.concatenate([query, dout_head], axis=0)
        far_rows = far_rows + mm(far_chooser(offset, head), query_dout, 1, 1)
    back_ref[heads * NEAR :] = far_rows.astype(BF16)


def merge_kernel(slots_ref, merged_ref, far_ref):
    sources = slots_ref.shape[0]
    total = jnp.zeros((SLOT, LANES), F32)
    for source in range(sources):
        block = slots_ref[source].astype(F32)
        total = total + block
        far_ref[source * SMALL : (source + 1) * SMALL] = block[CHUNK:]
    pieces = [far_ref[pl.ds(kind, sources, stride=SMALL), :] for kind in range(SMALL)]
    full = jnp.concatenate([total] + pieces, axis=0).astype(BF16)
    for plane in range(PLANES):
        merged_ref[plane] = full


def far_kernel(plane_ref, merged_ref, slots_ref, returned_ref):
    sources = slots_ref.shape[0]
    width = 2 * sources
    count = PLANES * width

    def kind(index):
        start = SLOT + index * width
        return merged_ref[:, start : start + width, :].reshape(count, LANES)

    query_key, value_dout, attended_stats, far_grad = (kind(index) for index in range(4))
    shape = (LANES, HEAD_DIM)
    lower = one_hot(iota(shape, 0) == iota(shape, 1) + HEAD_DIM)
    query, value = query_key[:, :HEAD_DIM], value_dout[:, :HEAD_DIM]
    key, dout = (mm(both, lower, 1, 0).astype(BF16) for both in (query_key, value_dout))
    local_attended = attended_stats[:, :HEAD_DIM].astype(F32)
    stats = attended_stats.astype(F32)
    local_mass = take_stat(stats, 0)

    scores = mm(query, key, 1, 1) * SCORE_SCALE
    peak = jnp.maximum(jnp.max(scores, axis=1, keepdims=True), local_mass)
    mass = jnp.exp(scores - peak)
    local_part = jnp.exp(local_mass - peak)
    total = jnp.sum(mass, axis=1, keepdims=True) + local_part
    normalizer = peak + jnp.log(total)
    inverse = 1.0 / total
    probs = mass * inverse
    probs_low = probs.astype(BF16)
    attended = local_part * inverse * local_attended + mm(probs_low, value, 1, 0)
    delta = jnp.sum(dout.astype(F32) * attended, axis=1, keepdims=True)
    grad_probs = mm(dout, value, 1, 1)
    grad_scores = (probs * (grad_probs - delta)).astype(BF16)
    grad_query = mm(grad_scores, key, 1, 0).astype(BF16)
    grad_key = mm(grad_scores, query, 0, 0).astype(BF16)
    grad_value = mm(probs_low, dout, 0, 0).astype(BF16)

    def other_plane(column):
        blocks = [column[(p ^ 1) * width : ((p ^ 1) + 1) * width] for p in range(PLANES)]
        return jnp.concatenate(blocks, axis=0)

    shape = (HEAD_DIM, LANES)
    to_left = one_hot(iota(shape, 0) == iota(shape, 1))
    to_right = one_hot(iota(shape, 0) + HEAD_DIM == iota(shape, 1))
    attended_low = attended.astype(BF16)
    over = mm(attended_low, to_left, 1, 0).astype(BF16)
    under = mm(attended_low, to_right, 1, 0).astype(BF16)
    weight_part = mm(far_grad, over, 0, 0)[:CHUNK] + mm(far_grad, under, 0, 0)[CHUNK : 2 * CHUNK]
    weight_part = weight_part * WEIGHT_SCALE
    for plane in range(PLANES):
        weight_part = weight_part + merged_ref[plane, :SLOT].astype(F32)[:CHUNK]
    own_stats = lay_stats((count, LANES), 1, HEAD_DIM, (normalizer, delta))
    other_stats = lay_stats(
        (count, LANES), 1, HEAD_DIM, (other_plane(normalizer), other_plane(delta))
    )
    returned_ref[0] = mm(grad_value, to_left, 1, 0) + other_stats
    returned_ref[1] = mm(grad_query, to_left, 1, 0) + own_stats
    returned_ref[2] = mm(grad_key, to_left, 1, 0)
    own = pl.ds(pl.multiple_of(plane_ref[0] * width, width), width)
    shape = (sources * SMALL, width)
    row, column = iota(shape, 0), iota(shape, 1)
    same = (row // SMALL) == (column % sources)
    slot_row, pair = row % SMALL, column // sources
    placed = jnp.zeros((sources * SMALL, LANES), F32)
    for index in range(returned_ref.shape[0]):
        chosen = one_hot(same & (slot_row == pair + 2 * index))
        placed = placed + mm(chosen, returned_ref[index, own, :].astype(BF16), 1, 0)
    for source in range(sources):
        parts = [weight_part, placed[source * SMALL : (source + 1) * SMALL]]
        slots_ref[source] = jnp.concatenate(parts, axis=0).astype(BF16)


def prepare_kernel(
    key_ref,
    value_ref,
    near_ref,
    own_ref,
    partner_ref,
    local_key_ref,
    local_value_ref,
    rows_ref,
    scores_ref,
    grad_probs_ref,
    keys_ref,
    chooser_ref,
    grad_key_ref,
    grad_value_ref,
):
    heads = key_ref.shape[0] // HEAD_DIM
    first_far = heads * NEAR
    blank = jnp.zeros((HEAD_DIM, TOKENS_HERE + LANES), BF16)
    shape = (GAP, GAP)
    row, column = iota(shape, 0), iota(shape, 1)
    widen = one_hot(iota((NEAR, LANES), 0) == iota((NEAR, LANES), 1))
    shape = (GAP, TOKENS_HERE + LANES)
    block_row, place = iota(shape, 0), iota(shape, 1)
    here = place < TOKENS_HERE
    from_partner, from_here = block_row < 2, (block_row >= 2) & (block_row < 4)
    for head in range(heads):
        offset = told_offset(near_ref, head)
        rows = slice(head * HEAD_DIM, (head + 1) * HEAD_DIM)
        block = slice(head * GAP, (head + 1) * GAP)
        key, value = key_ref[rows], value_ref[rows]
        near = mm(near_ref[block], widen, 0, 0).astype(BF16)
        keys = jnp.concatenate([key, near[:HEAD_DIM]], axis=1)
        values = jnp.concatenate([value, near[HEAD_DIM:]], axis=1)
        keys = jnp.concatenate([keys, blank], axis=0)
        values = jnp.concatenate([blank, values], axis=0)
        from_partner_far = one_hot((row < 2) & (column == row + 2 * head))
        from_own_far = one_hot((row >= 2) & (row < 4) & (column == row - 2 + 2 * head))
        chosen = mm(from_partner_far, partner_ref[first_far:], 1, 0)
        chosen = (chosen + mm(from_own_far, own_ref[first_far:], 1, 0)).astype(BF16)
        in_near = here & same_class(place, offset, RC)
        extra = jnp.where(here & same_class(place, offset, RB), 1.0, 0.0)
        extra = extra + jnp.where(in_near, 1.0, 0.0)
        mask_here = jnp.where(place < TOKENS_HERE + NEAR, jnp.log(1.0 + extra), ABSENT)
        mask = jnp.where(from_here, mask_here, ABSENT)
        mask = jnp.where(from_partner & in_near, 0.0, mask)
        rows_ref[block] = chosen
        scores_ref[block] = mm(chosen, keys, 1, 0) * SCORE_SCALE + mask
        grad_probs_ref[block] = mm(chosen, values, 1, 0)
        keys_ref[head] = keys
        for pair in range(3):
            chooser_ref[head, pair] = far_chooser(offset, pair)
        spread = mm(partner_ref[block], near_chooser(offset), 0, 0)
        grad_key_ref[rows] = local_key_ref[rows] + spread[:HEAD_DIM]
        grad_value_ref[rows] = local_value_ref[rows] + spread[HEAD_DIM:]


def final_kernel(
    rows_ref,
    scores_ref,
    grad_probs_ref,
    keys_ref,
    chooser_ref,
    local_query_ref,
    local_key_ref,
    local_value_ref,
    slots_ref,
    grad_query_ref,
    grad_key_ref,
    grad_value_ref,
    grad_weight_ref,
):
    heads = local_query_ref.shape[0] // HEAD_DIM
    half = grad_weight_ref.shape[1] // 2
    chunks = pl.cdiv(half, CHUNK)
    for head in range(heads):
        rows = slice(head * HEAD_DIM, (head + 1) * HEAD_DIM)
        block = slice(head * GAP, (head + 1) * GAP)
        pieces = [slots_ref[head * chunks + chunk].astype(F32) for chunk in range(chunks)]
        folded = jnp.concatenate([piece[:CHUNK] for piece in pieces], axis=0)[:half]
        unfolded = jnp.transpose(folded)
        grad_weight_ref[rows, :half] = unfolded[:HEAD_DIM]
        grad_weight_ref[rows, half:] = unfolded[HEAD_DIM:]

        returned = jnp.concatenate(
            [pieces[0][CHUNK:], jnp.zeros((GAP - SMALL, LANES), F32)], axis=0
        )
        chosen = rows_ref[block]
        probs = jnp.exp(scores_ref[block] - take_stat(returned, 0))
        grad_scores = (probs * (grad_probs_ref[block] - take_stat(returned, 1))).astype(BF16)
        probs_low = probs[:, :TOKENS_HERE].astype(BF16)
        far_query = (returned + mm(grad_scores, keys_ref[head], 1, 1)).astype(BF16)
        returned = returned.astype(BF16)
        grad_query = mm(far_query, chooser_ref[head, 1], 0, 0)[:HEAD_DIM]
        grad_key = mm(returned, chooser_ref[head, 2], 0, 0)[:HEAD_DIM]
        grad_key = grad_key + mm(chosen, grad_scores[:, :TOKENS_HERE], 0, 0)[:HEAD_DIM]
        grad_value = mm(returned, chooser_ref[head, 0], 0, 0)[:HEAD_DIM]
        grad_value = grad_value + mm(chosen, probs_low, 0, 0)[HEAD_DIM:]
        grad_query = (local_query_ref[rows] + grad_query) * SCORE_SCALE
        grad_key = (local_key_ref[rows] + grad_key) * SCORE_SCALE
        grad_query_ref[rows] = grad_query.astype(BF16)
        grad_key_ref[rows] = grad_key.astype(BF16)
        grad_value_ref[rows] = (local_value_ref[rows] + grad_value).astype(BF16)


def call(kernel, outs, arrays, scalars=0, scratch=(), space=pltpu.VMEM, limit=40 << 20):
    specs = [pl.BlockSpec(memory_space=pltpu.SMEM)] * scalars
    specs = specs + [pl.BlockSpec(memory_space=space)] * (len(arrays) - scalars)
    shapes = [jax.ShapeDtypeStruct(shape, dtype) for shape, dtype in outs]
    return pl.pallas_call(
        kernel,
        out_shape=shapes,
        in_specs=specs,
        out_specs=[pl.BlockSpec(memory_space=pltpu.VMEM)] * len(shapes),
        scratch_shapes=list(scratch),
        compiler_params=pltpu.CompilerParams(vmem_limit_bytes=limit),
        name=kernel.__name__,
    )(*arrays)


def local(queries, keys, values, grad_out, out_weight, offsets):
    features = queries.shape[0]
    model = out_weight.shape[1]
    heads = offsets.shape[0]
    sources = lax.axis_size("xz")
    near_shape = ((heads * NEAR + GAP, LANES), BF16)
    back_shape = ((heads * NEAR + GAP, LANES), BF16)
    slots_shape = ((sources, SLOT, LANES), BF16)
    merged_shape = ((PLANES, SLOT + sources * SMALL, LANES), BF16)
    wide_shape = ((features, TOKENS_HERE), F32)
    grad_shape = ((features, TOKENS_HERE), BF16)
    block_shape = ((heads * GAP, TOKENS_HERE + LANES), F32)
    other = [(i, i ^ 1) for i in range(PLANES)]

    scratch = [
        pltpu.SMEM(offsets.shape, offsets.dtype),
        pltpu.VMEM(keys.shape, keys.dtype),
        pltpu.VMEM(values.shape, values.dtype),
        pltpu.SemaphoreType.DMA((3,)),
    ]
    other_grad = lax.ppermute(grad_out, "chip", [(0, 1), (1, 0)])
    (near,) = call(
        near_kernel,
        [near_shape],
        (offsets, keys, values),
        scratch=scratch,
        space=pltpu.HBM,
        limit=LIMIT,
    )
    near = lax.ppermute(near, "yh", other)
    pair_grads = lax.all_gather(jnp.stack([grad_out, other_grad]), "core", axis=0, tiled=True)
    side = lax.axis_index("chip").reshape(1)
    slots, dout, stats = call(
        local_kernel,
        [slots_shape, grad_shape, ((heads * SMALL, TOKENS_HERE), F32)],
        (side, queries, keys, values, pair_grads, out_weight, near),
        scalars=1,
    )
    slots = lax.all_to_all(slots, "xz", 0, 0, tiled=True)
    own, local_query, local_key, local_value = call(
        local_grad_kernel,
        [back_shape, wide_shape, wide_shape, wide_shape],
        (queries, keys, values, dout, stats, near),
    )
    partner = lax.ppermute(own, "yh", other)
    prepared = call(
        prepare_kernel,
        [
            ((heads * GAP, LANES), BF16),
            block_shape,
            block_shape,
            ((heads, LANES, TOKENS_HERE + LANES), BF16),
            ((heads, 3, GAP, TOKENS_HERE), BF16),
            wide_shape,
            wide_shape,
        ],
        (keys, values, near, own, partner, local_key, local_value),
    )
    plane = lax.axis_index("yh").reshape(1)
    slots, prepared, local_query, plane = lax.optimization_barrier(
        (slots, prepared, local_query, plane)
    )
    rows, scores, grad_probs, wide_keys, chooser, local_key, local_value = prepared
    (merged,) = call(
        merge_kernel,
        [merged_shape],
        (slots,),
        scratch=[pltpu.VMEM((sources * SMALL, LANES), F32)],
    )
    merged = lax.all_to_all(merged, "yh", 0, 0, tiled=True)
    (slots,) = call(
        far_kernel,
        [slots_shape],
        (plane, merged),
        scalars=1,
        scratch=[pltpu.VMEM((3, PLANES * sources * 2, LANES), F32)],
    )
    slots = lax.all_to_all(slots, "xz", 0, 0, tiled=True)
    return tuple(
        call(
            final_kernel,
            [grad_shape, grad_shape, grad_shape, ((features, model), F32)],
            (
                rows,
                scores,
                grad_probs,
                wide_keys,
                chooser,
                local_query,
                local_key,
                local_value,
                slots,
            ),
        )
    )


def solution(mesh):
    devices = mesh.devices.reshape(-1, PLANES, 2, mesh.devices.shape[1] // 2)
    split_mesh = Mesh(devices, ("xz", "yh", "chip", "core"))
    parts = ("chip", "core")
    wide = P(parts, ("xz", "yh"))
    return jax.shard_map(
        local,
        mesh=split_mesh,
        in_specs=(wide, wide, wide, wide, P(parts, None), P(parts)),
        out_specs=(wide, wide, wide, P(parts, None)),
        check_vma=False,
    )
```

```python
import jax
import jax.numpy as jnp
from jax import lax
from jax.experimental import pallas as pl
from jax.experimental.pallas import tpu as pltpu
from jax.sharding import Mesh
from jax.sharding import PartitionSpec as P

HEAD_DIM = 64
TOKENS_HERE = 256
RB = 2
RC = 16
RE = 128
NEAR = TOKENS_HERE // RC
SCORE_SCALE = HEAD_DIM ** (-0.5)
WEIGHT_SCALE = 0.03125

PLANES = 4
LANES = 128
GAP = 16
SMALL = 8
CHUNK = 40
SLOT = CHUNK + SMALL
ABSENT = -1e30
LIMIT = 63_400_000

F32 = jnp.float32
BF16 = jnp.bfloat16


def mm(left, right, left_dim, right_dim):
    return lax.dot_general(
        left, right, (((left_dim,), (right_dim,)), ((), ())), preferred_element_type=F32
    )


def iota(shape, dim):
    return lax.broadcasted_iota(jnp.int32, shape, dim)


def one_hot(condition):
    return jnp.where(condition, 1.0, 0.0).astype(BF16)


def same_class(position, offset, stride):
    return (position & (stride - 1)) == (offset & (stride - 1))


def near_chooser(offset):
    shape = (NEAR, TOKENS_HERE)
    return one_hot(iota(shape, 1) == RC * iota(shape, 0) + (offset & (RC - 1)))


def far_chooser(offset, pair):
    shape = (GAP, TOKENS_HERE)
    row = iota(shape, 0)
    hit = iota(shape, 1) == RE * (row & 1) + offset
    return one_hot(hit & ((row >> 1) == pair))


def split3(value):
    high = value.astype(BF16).astype(F32)
    rest = value - high
    middle = rest.astype(BF16).astype(F32)
    return high, middle, rest - middle


def lay_stats(shape, dim, start, values):
    place = iota(shape, dim) - start
    out = jnp.zeros(shape, F32)
    for index, value in enumerate(values):
        for part_index, part in enumerate(split3(value)):
            out = jnp.where(place == 3 * index + part_index, part, out)
    return out


def take_stat(rows, start, index):
    place = iota(rows.shape, 1) - start - 3 * index
    return jnp.sum(jnp.where((place >= 0) & (place < 3), rows, 0.0), axis=1, keepdims=True)


def chunk_rows(folded, chunk):
    rows = folded[chunk * CHUNK : (chunk + 1) * CHUNK]
    short = CHUNK - rows.shape[0]
    if short:
        rows = jnp.concatenate([rows, jnp.zeros((short,) + rows.shape[1:], rows.dtype)], axis=0)
    return rows


def near_kernel(
    offset_hbm, key_hbm, value_hbm, near_ref, offset_ref, key_ref, value_ref, semaphores
):
    pairs = ((offset_hbm, offset_ref), (key_hbm, key_ref), (value_hbm, value_ref))
    copies = [
        pltpu.make_async_copy(source, target, semaphores.at[index])
        for index, (source, target) in enumerate(pairs)
    ]
    for copy in copies:
        copy.start()
    for copy in copies:
        copy.wait()
    for head in range(key_ref.shape[0] // HEAD_DIM):
        rows = slice(head * HEAD_DIM, (head + 1) * HEAD_DIM)
        both = jnp.concatenate([key_ref[rows], value_ref[rows]], axis=0)
        picked = mm(near_chooser(offset_ref[head]), both, 1, 1)
        near_ref[head * NEAR : (head + 1) * NEAR, :] = picked.astype(BF16)
    heads = near_ref.shape[0] // NEAR - 1
    row = iota((GAP, LANES), 0)
    told = jnp.zeros((GAP, LANES), F32)
    for head in range(heads):
        told = jnp.where(row == head, offset_ref[head].astype(F32), told)
    near_ref[heads * NEAR :] = told.astype(BF16)


def told_offset(near_ref, head):
    told = near_ref[near_ref.shape[0] - GAP :].astype(F32)
    return told[head : head + 1, :1].astype(jnp.int32)


def pair_count(key_pos, query_pos, offset):
    count = 1.0 + jnp.where(
        same_class(key_pos, offset, RB) & same_class(query_pos, offset, RB), 1.0, 0.0
    )
    return count + jnp.where(
        same_class(key_pos, offset, RC) & same_class(query_pos, offset, RC), 1.0, 0.0
    )


def local_kernel(
    side_ref,
    query_ref,
    key_ref,
    value_ref,
    grad_ref,
    weight_ref,
    near_ref,
    slots_ref,
    dout_ref,
    stats_ref,
):
    heads = query_ref.shape[0] // HEAD_DIM
    side = side_ref[0]
    blocks = [grad_ref[2 * core + (chip ^ side)] for chip in range(2) for core in range(2)]
    grad = jnp.concatenate(blocks, axis=0)
    half = grad.shape[0] // 2
    chunks = pl.cdiv(half, CHUNK)
    dout = mm(weight_ref[...], grad, 1, 0).astype(BF16)
    dout_ref[...] = dout
    offsets = [told_offset(near_ref, head) for head in range(heads)]
    choosers = [far_chooser(offsets[head], 3) for head in range(heads)]
    choosers = jnp.concatenate(choosers, axis=0)
    wide = grad.astype(F32)
    filler = jnp.zeros((LANES - 2 * CHUNK, TOKENS_HERE), F32)
    far_grads = []
    for chunk in range(chunks):
        both = [chunk_rows(wide[:half], chunk), chunk_rows(wide[half:], chunk), filler]
        far_grads.append(mm(choosers, jnp.concatenate(both, axis=0).astype(BF16), 1, 1))
    blank = jnp.zeros((HEAD_DIM, TOKENS_HERE), BF16)
    key_pos = iota((TOKENS_HERE, TOKENS_HERE), 0)
    query_pos = iota((TOKENS_HERE, TOKENS_HERE), 1)
    query_row = iota((1, TOKENS_HERE), 1)
    heads = range(heads)
    rows = [slice(head * HEAD_DIM, (head + 1) * HEAD_DIM) for head in heads]
    near = [near_ref[head * NEAR : (head + 1) * NEAR] for head in heads]
    in_near = [same_class(query_row, offset, RC) for offset in offsets]
    in_far = [same_class(query_row, offset, RE) for offset in offsets]
    scores = [mm(key_ref[rows[h]], query_ref[rows[h]], 0, 0) * SCORE_SCALE for h in heads]
    near_scores = [
        mm(near[h], jnp.concatenate([query_ref[rows[h]], blank], axis=0), 1, 0) * SCORE_SCALE
        for h in heads
    ]
    peak = [jnp.max(scores[h], axis=0, keepdims=True) for h in heads]
    near_max = [jnp.max(near_scores[h], axis=0, keepdims=True) for h in heads]
    peak = [jnp.where(in_near[h], jnp.maximum(peak[h], near_max[h]), peak[h]) for h in heads]
    mass = [
        pair_count(key_pos, query_pos, offsets[h]) * jnp.exp(scores[h] - peak[h]) for h in heads
    ]
    near_mass = [jnp.where(in_near[h], jnp.exp(near_scores[h] - peak[h]), 0.0) for h in heads]
    total = [
        jnp.sum(mass[h], axis=0, keepdims=True) + jnp.sum(near_mass[h], axis=0, keepdims=True)
        for h in heads
    ]
    log_mass = [peak[h] + jnp.log(total[h]) for h in heads]
    inverse = [1.0 / total[h] for h in heads]
    probs_low = [(mass[h] * inverse[h]).astype(BF16) for h in heads]
    near_low = [(near_mass[h] * inverse[h]).astype(BF16) for h in heads]
    attended = [
        mm(value_ref[rows[h]], probs_low[h], 1, 0) + mm(near[h], near_low[h], 0, 0)[HEAD_DIM:]
        for h in heads
    ]
    kept = [jnp.where(in_far[h], 0.0, attended[h]).astype(BF16) for h in heads]
    over = [jnp.concatenate([kept[h], blank], axis=0) for h in heads]
    under = [jnp.concatenate([blank, kept[h]], axis=0) for h in heads]
    weight_part = [
        (mm(grad[:half], over[h], 1, 1) + mm(grad[half:], under[h], 1, 1)) * WEIGHT_SCALE
        for h in heads
    ]
    delta = [
        jnp.sum(dout[rows[h]].astype(F32) * attended[h], axis=0, keepdims=True) for h in heads
    ]
    place = iota((SMALL, TOKENS_HERE), 0)
    for h in heads:
        query_dout = jnp.concatenate([query_ref[rows[h]], dout[rows[h]]], axis=0)
        key_value = jnp.concatenate([key_ref[rows[h]], value_ref[rows[h]]], axis=0)
        stats = lay_stats((HEAD_DIM, TOKENS_HERE), 0, 0, (log_mass[h], delta[h]))
        stats_attended = jnp.concatenate([stats.astype(BF16), attended[h].astype(BF16)], axis=0)
        mine = mm(far_chooser(offsets[h], 0), query_dout, 1, 1)
        mine = mine + mm(far_chooser(offsets[h], 1), key_value, 1, 1)
        mine = mine + mm(far_chooser(offsets[h], 2), stats_attended, 1, 1)
        stats_ref[h * SMALL : (h + 1) * SMALL] = jnp.where(place == 0, log_mass[h], delta[h])
        for chunk in range(chunks):
            far_grad = far_grads[chunk][h * GAP : h * GAP + SMALL]
            parts = [chunk_rows(weight_part[h], chunk), mine[:SMALL] + far_grad]
            slots_ref[h * chunks + chunk] = jnp.concatenate(parts, axis=0).astype(BF16)
    heads = len(heads)
    rest = slots_ref.shape[0] - heads * chunks
    slots_ref[heads * chunks :] = jnp.zeros((rest,) + slots_ref.shape[1:], BF16)


def local_grad_kernel(
    query_ref,
    key_ref,
    value_ref,
    dout_ref,
    stats_ref,
    near_ref,
    back_ref,
    grad_query_ref,
    grad_key_ref,
    grad_value_ref,
):
    heads = query_ref.shape[0] // HEAD_DIM
    blank = jnp.zeros((HEAD_DIM, TOKENS_HERE), BF16)
    key_pos = iota((TOKENS_HERE, TOKENS_HERE), 0)
    query_pos = iota((TOKENS_HERE, TOKENS_HERE), 1)
    query_row = iota((1, TOKENS_HERE), 1)
    far_rows = jnp.zeros((GAP, LANES), F32)
    for head in range(heads):
        offset = told_offset(near_ref, head)
        rows = slice(head * HEAD_DIM, (head + 1) * HEAD_DIM)
        near_rows = slice(head * NEAR, (head + 1) * NEAR)
        query, key, value = query_ref[rows], key_ref[rows], value_ref[rows]
        near = near_ref[near_rows]
        dout_head = dout_ref[rows]
        log_mass = stats_ref[head * SMALL : head * SMALL + 1]
        delta = stats_ref[head * SMALL + 1 : head * SMALL + 2]
        query_over = jnp.concatenate([query, blank], axis=0)
        dout_under = jnp.concatenate([blank, dout_head], axis=0)
        in_near = same_class(query_row, offset, RC)
        in_far = same_class(query_row, offset, RE)
        near_only = in_near & jnp.logical_not(in_far)

        scores = mm(key, query, 0, 0) * SCORE_SCALE
        near_scores = mm(near, query_over, 1, 0) * SCORE_SCALE
        probs = pair_count(key_pos, query_pos, offset) * jnp.exp(scores - log_mass)
        probs = jnp.where(in_far, 0.0, probs)
        near_probs = jnp.where(near_only, jnp.exp(near_scores - log_mass), 0.0)
        grad_scores = (probs * (mm(value, dout_head, 0, 0) - delta)).astype(BF16)
        near_grad_scores = (near_probs * (mm(near, dout_under, 1, 0) - delta)).astype(BF16)
        grad_query_ref[rows] = (
            mm(key, grad_scores, 1, 0) + mm(near, near_grad_scores, 0, 0)[:HEAD_DIM]
        )
        grad_key_ref[rows] = mm(query, grad_scores, 1, 1)
        grad_value_ref[rows] = mm(dout_head, probs.astype(BF16), 1, 1)
        back = mm(near_grad_scores, query_over, 1, 1)
        back = back + mm(near_probs.astype(BF16), dout_under, 1, 1)
        back_ref[near_rows] = back.astype(BF16)
        query_dout = jnp.concatenate([query, dout_head], axis=0)
        far_rows = far_rows + mm(far_chooser(offset, head), query_dout, 1, 1)
    back_ref[heads * NEAR :] = far_rows.astype(BF16)


def merge_kernel(slots_ref, merged_ref, far_ref):
    sources = slots_ref.shape[0]
    total = jnp.zeros((SLOT, LANES), F32)
    for source in range(sources):
        block = slots_ref[source].astype(F32)
        total = total + block
        far_ref[source * SMALL : (source + 1) * SMALL] = block[CHUNK:]
    pieces = [far_ref[pl.ds(kind, sources, stride=SMALL), :] for kind in range(SMALL)]
    full = jnp.concatenate([total] + pieces, axis=0).astype(BF16)
    for plane in range(PLANES):
        merged_ref[plane] = full


def far_kernel(plane_ref, merged_ref, slots_ref, returned_ref):
    sources = slots_ref.shape[0]
    width = 2 * sources
    count = PLANES * width

    def kind(index):
        start = SLOT + index * width
        return merged_ref[:, start : start + width, :].reshape(count, LANES)

    query_dout, key_value, stats_attended, far_grad = (kind(index) for index in range(4))
    left = iota((count, LANES), 1) < HEAD_DIM
    shape = (LANES, LANES)
    swap = one_hot(iota(shape, 0) == (iota(shape, 1) ^ HEAD_DIM))
    value_key = mm(key_value, swap, 1, 0).astype(BF16)
    stats = stats_attended.astype(F32)
    attended_stats = mm(stats_attended, swap, 1, 0)
    wide = query_dout.astype(F32)
    query = jnp.where(left, wide, 0.0).astype(BF16)
    dout_wide = jnp.where(left, 0.0, wide)
    local_mass = take_stat(stats, 0, 0)

    scores = mm(query, key_value, 1, 1) * SCORE_SCALE
    grad_probs = mm(dout_wide.astype(BF16), key_value, 1, 1)
    peak = jnp.maximum(jnp.max(scores, axis=1, keepdims=True), local_mass)
    mass = jnp.exp(scores - peak)
    local_part = jnp.exp(local_mass - peak)
    total = jnp.sum(mass, axis=1, keepdims=True) + local_part
    normalizer = peak + jnp.log(total)
    inverse = 1.0 / total
    local_part = local_part * inverse
    probs = mass * inverse
    probs_low = probs.astype(BF16)
    under = local_part * stats + mm(probs_low, key_value, 1, 0)
    delta = jnp.sum(dout_wide * under, axis=1, keepdims=True)
    over = local_part * attended_stats + mm(probs_low, value_key, 1, 0)
    over = jnp.where(left, over, 0.0).astype(BF16)
    under = jnp.where(left, 0.0, under).astype(BF16)
    grad_scores = (probs * (grad_probs - delta)).astype(BF16)

    def other_plane(column):
        blocks = [column[(p ^ 1) * width : ((p ^ 1) + 1) * width] for p in range(PLANES)]
        return jnp.concatenate(blocks, axis=0)

    weight_part = mm(far_grad, over, 0, 0)[:CHUNK] + mm(far_grad, under, 0, 0)[CHUNK : 2 * CHUNK]
    weight_part = weight_part * WEIGHT_SCALE
    for plane in range(PLANES):
        weight_part = weight_part + merged_ref[plane, :SLOT].astype(F32)[:CHUNK]
    own_stats = lay_stats((count, LANES), 1, HEAD_DIM, (normalizer, delta))
    other_stats = lay_stats((count, LANES), 1, 0, (other_plane(normalizer), other_plane(delta)))
    returned_ref[0] = jnp.where(left, other_stats, mm(probs_low, query_dout, 0, 0))
    returned_ref[1] = jnp.where(left, mm(grad_scores, key_value, 1, 0), own_stats)
    returned_ref[2] = jnp.where(left, mm(grad_scores, query_dout, 0, 0), 0.0)
    own = pl.ds(pl.multiple_of(plane_ref[0] * width, width), width)
    shape = (sources * SMALL, width)
    row, column = iota(shape, 0), iota(shape, 1)
    same = (row // SMALL) == (column % sources)
    slot_row, pair = row % SMALL, column // sources
    placed = jnp.zeros((sources * SMALL, LANES), F32)
    for index in range(returned_ref.shape[0]):
        chosen = one_hot(same & (slot_row == pair + 2 * index))
        placed = placed + mm(chosen, returned_ref[index, own, :].astype(BF16), 1, 0)
    for source in range(sources):
        parts = [weight_part, placed[source * SMALL : (source + 1) * SMALL]]
        slots_ref[source] = jnp.concatenate(parts, axis=0).astype(BF16)


def prepare_kernel(
    key_ref,
    value_ref,
    near_ref,
    own_ref,
    partner_ref,
    local_key_ref,
    local_value_ref,
    rows_ref,
    scores_ref,
    grad_probs_ref,
    keys_ref,
    chooser_ref,
    grad_key_ref,
    grad_value_ref,
):
    heads = key_ref.shape[0] // HEAD_DIM
    first_far = heads * NEAR
    blank = jnp.zeros((HEAD_DIM, TOKENS_HERE + LANES), BF16)
    shape = (GAP, GAP)
    row, column = iota(shape, 0), iota(shape, 1)
    widen = one_hot(iota((NEAR, LANES), 0) == iota((NEAR, LANES), 1))
    shape = (GAP, TOKENS_HERE + LANES)
    block_row, place = iota(shape, 0), iota(shape, 1)
    here = place < TOKENS_HERE
    from_partner, from_here = block_row < 2, (block_row >= 2) & (block_row < 4)
    for head in range(heads):
        offset = told_offset(near_ref, head)
        rows = slice(head * HEAD_DIM, (head + 1) * HEAD_DIM)
        block = slice(head * GAP, (head + 1) * GAP)
        key, value = key_ref[rows], value_ref[rows]
        near = mm(near_ref[block], widen, 0, 0).astype(BF16)
        keys = jnp.concatenate([key, near[:HEAD_DIM]], axis=1)
        values = jnp.concatenate([value, near[HEAD_DIM:]], axis=1)
        keys = jnp.concatenate([keys, blank], axis=0)
        values = jnp.concatenate([blank, values], axis=0)
        from_partner_far = one_hot((row < 2) & (column == row + 2 * head))
        from_own_far = one_hot((row >= 2) & (row < 4) & (column == row - 2 + 2 * head))
        chosen = mm(from_partner_far, partner_ref[first_far:], 1, 0)
        chosen = (chosen + mm(from_own_far, own_ref[first_far:], 1, 0)).astype(BF16)
        in_near = here & same_class(place, offset, RC)
        extra = jnp.where(here & same_class(place, offset, RB), 1.0, 0.0)
        extra = extra + jnp.where(in_near, 1.0, 0.0)
        mask_here = jnp.where(place < TOKENS_HERE + NEAR, jnp.log(1.0 + extra), ABSENT)
        mask = jnp.where(from_here, mask_here, ABSENT)
        mask = jnp.where(from_partner & in_near, 0.0, mask)
        rows_ref[block] = chosen
        scores_ref[block] = mm(chosen, keys, 1, 0) * SCORE_SCALE + mask
        grad_probs_ref[block] = mm(chosen, values, 1, 0)
        keys_ref[head] = keys
        for pair in range(3):
            chooser_ref[head, pair] = far_chooser(offset, pair)
        spread = mm(partner_ref[block], near_chooser(offset), 0, 0)
        grad_key_ref[rows] = local_key_ref[rows] + spread[:HEAD_DIM]
        grad_value_ref[rows] = local_value_ref[rows] + spread[HEAD_DIM:]


def final_kernel(
    rows_ref,
    scores_ref,
    grad_probs_ref,
    keys_ref,
    chooser_ref,
    local_query_ref,
    local_key_ref,
    local_value_ref,
    slots_ref,
    grad_query_ref,
    grad_key_ref,
    grad_value_ref,
    grad_weight_ref,
):
    heads = local_query_ref.shape[0] // HEAD_DIM
    half = grad_weight_ref.shape[1] // 2
    chunks = pl.cdiv(half, CHUNK)
    for head in range(heads):
        rows = slice(head * HEAD_DIM, (head + 1) * HEAD_DIM)
        block = slice(head * GAP, (head + 1) * GAP)
        pieces = [slots_ref[head * chunks + chunk].astype(F32) for chunk in range(chunks)]
        folded = jnp.concatenate([piece[:CHUNK] for piece in pieces], axis=0)[:half]
        unfolded = jnp.transpose(folded)
        grad_weight_ref[rows, :half] = unfolded[:HEAD_DIM]
        grad_weight_ref[rows, half:] = unfolded[HEAD_DIM:]

        returned = jnp.concatenate(
            [pieces[0][CHUNK:], jnp.zeros((GAP - SMALL, LANES), F32)], axis=0
        )
        chosen = rows_ref[block]
        start = jnp.where(iota(returned.shape, 0) < 2, 0, HEAD_DIM)
        normalizer, delta = (take_stat(returned, start, index) for index in range(2))
        probs = jnp.exp(scores_ref[block] - normalizer)
        grad_scores = (probs * (grad_probs_ref[block] - delta)).astype(BF16)
        probs_low = probs[:, :TOKENS_HERE].astype(BF16)
        far_query = (returned + mm(grad_scores, keys_ref[head], 1, 1)).astype(BF16)
        returned = returned.astype(BF16)
        grad_query = mm(far_query, chooser_ref[head, 1], 0, 0)[:HEAD_DIM]
        grad_key = mm(returned, chooser_ref[head, 2], 0, 0)[:HEAD_DIM]
        grad_key = grad_key + mm(chosen, grad_scores[:, :TOKENS_HERE], 0, 0)[:HEAD_DIM]
        grad_value = mm(returned, chooser_ref[head, 0], 0, 0)[HEAD_DIM:]
        grad_value = grad_value + mm(chosen, probs_low, 0, 0)[HEAD_DIM:]
        grad_query = (local_query_ref[rows] + grad_query) * SCORE_SCALE
        grad_key = (local_key_ref[rows] + grad_key) * SCORE_SCALE
        grad_query_ref[rows] = grad_query.astype(BF16)
        grad_key_ref[rows] = grad_key.astype(BF16)
        grad_value_ref[rows] = (local_value_ref[rows] + grad_value).astype(BF16)


def call(kernel, outs, arrays, scalars=0, scratch=(), space=pltpu.VMEM, limit=40 << 20):
    specs = [pl.BlockSpec(memory_space=pltpu.SMEM)] * scalars
    specs = specs + [pl.BlockSpec(memory_space=space)] * (len(arrays) - scalars)
    shapes = [jax.ShapeDtypeStruct(shape, dtype) for shape, dtype in outs]
    return pl.pallas_call(
        kernel,
        out_shape=shapes,
        in_specs=specs,
        out_specs=[pl.BlockSpec(memory_space=pltpu.VMEM)] * len(shapes),
        scratch_shapes=list(scratch),
        compiler_params=pltpu.CompilerParams(vmem_limit_bytes=limit),
        name=kernel.__name__,
    )(*arrays)


def local(queries, keys, values, grad_out, out_weight, offsets):
    features = queries.shape[0]
    model = out_weight.shape[1]
    heads = offsets.shape[0]
    sources = lax.axis_size("xz")
    near_shape = ((heads * NEAR + GAP, LANES), BF16)
    back_shape = ((heads * NEAR + GAP, LANES), BF16)
    slots_shape = ((sources, SLOT, LANES), BF16)
    merged_shape = ((PLANES, SLOT + sources * SMALL, LANES), BF16)
    wide_shape = ((features, TOKENS_HERE), F32)
    grad_shape = ((features, TOKENS_HERE), BF16)
    block_shape = ((heads * GAP, TOKENS_HERE + LANES), F32)
    other = [(i, i ^ 1) for i in range(PLANES)]

    scratch = [
        pltpu.SMEM(offsets.shape, offsets.dtype),
        pltpu.VMEM(keys.shape, keys.dtype),
        pltpu.VMEM(values.shape, values.dtype),
        pltpu.SemaphoreType.DMA((3,)),
    ]
    other_grad = lax.ppermute(grad_out, "chip", [(0, 1), (1, 0)])
    (near,) = call(
        near_kernel,
        [near_shape],
        (offsets, keys, values),
        scratch=scratch,
        space=pltpu.HBM,
        limit=LIMIT,
    )
    near = lax.ppermute(near, "yh", other)
    pair_grads = lax.all_gather(jnp.stack([grad_out, other_grad]), "core", axis=0, tiled=True)
    side = lax.axis_index("chip").reshape(1)
    slots, dout, stats = call(
        local_kernel,
        [slots_shape, grad_shape, ((heads * SMALL, TOKENS_HERE), F32)],
        (side, queries, keys, values, pair_grads, out_weight, near),
        scalars=1,
    )
    slots = lax.all_to_all(slots, "xz", 0, 0, tiled=True)
    own, local_query, local_key, local_value = call(
        local_grad_kernel,
        [back_shape, wide_shape, wide_shape, wide_shape],
        (queries, keys, values, dout, stats, near),
    )
    partner = lax.ppermute(own, "yh", other)
    prepared = call(
        prepare_kernel,
        [
            ((heads * GAP, LANES), BF16),
            block_shape,
            block_shape,
            ((heads, LANES, TOKENS_HERE + LANES), BF16),
            ((heads, 3, GAP, TOKENS_HERE), BF16),
            wide_shape,
            wide_shape,
        ],
        (keys, values, near, own, partner, local_key, local_value),
    )
    plane = lax.axis_index("yh").reshape(1)
    slots, prepared, local_query, plane = lax.optimization_barrier(
        (slots, prepared, local_query, plane)
    )
    rows, scores, grad_probs, wide_keys, chooser, local_key, local_value = prepared
    (merged,) = call(
        merge_kernel,
        [merged_shape],
        (slots,),
        scratch=[pltpu.VMEM((sources * SMALL, LANES), F32)],
    )
    merged = lax.all_to_all(merged, "yh", 0, 0, tiled=True)
    (slots,) = call(
        far_kernel,
        [slots_shape],
        (plane, merged),
        scalars=1,
        scratch=[pltpu.VMEM((3, PLANES * sources * 2, LANES), F32)],
    )
    slots = lax.all_to_all(slots, "xz", 0, 0, tiled=True)
    return tuple(
        call(
            final_kernel,
            [grad_shape, grad_shape, grad_shape, ((features, model), F32)],
            (
                rows,
                scores,
                grad_probs,
                wide_keys,
                chooser,
                local_query,
                local_key,
                local_value,
                slots,
            ),
        )
    )


def solution(mesh):
    devices = mesh.devices.reshape(-1, PLANES, 2, mesh.devices.shape[1] // 2)
    split_mesh = Mesh(devices, ("xz", "yh", "chip", "core"))
    parts = ("chip", "core")
    wide = P(parts, ("xz", "yh"))
    return jax.shard_map(
        local,
        mesh=split_mesh,
        in_specs=(wide, wide, wide, wide, P(parts, None), P(parts)),
        out_specs=(wide, wide, wide, P(parts, None)),
        check_vma=False,
    )
```

```python
import jax
import jax.numpy as jnp
from jax import lax
from jax.experimental import pallas as pl
from jax.experimental.pallas import tpu as pltpu
from jax.sharding import Mesh
from jax.sharding import PartitionSpec as P

HEAD_DIM = 64
TOKENS_HERE = 256
RB = 2
RC = 16
RE = 128
NEAR = TOKENS_HERE // RC
SCORE_SCALE = HEAD_DIM ** (-0.5)
WEIGHT_SCALE = 0.03125

PLANES = 4
LANES = 128
GAP = 16
SMALL = 8
CHUNK = 40
SLOT = CHUNK + SMALL
ABSENT = -1e30
LIMIT = 63_400_000

F32 = jnp.float32
BF16 = jnp.bfloat16


def mm(left, right, left_dim, right_dim):
    return lax.dot_general(
        left, right, (((left_dim,), (right_dim,)), ((), ())), preferred_element_type=F32
    )


def iota(shape, dim):
    return lax.broadcasted_iota(jnp.int32, shape, dim)


def one_hot(condition):
    return jnp.where(condition, 1.0, 0.0).astype(BF16)


def same_class(position, offset, stride):
    return (position & (stride - 1)) == (offset & (stride - 1))


def near_chooser(offset):
    shape = (NEAR, TOKENS_HERE)
    return one_hot(iota(shape, 1) == RC * iota(shape, 0) + (offset & (RC - 1)))


def far_chooser(offset, pair):
    shape = (GAP, TOKENS_HERE)
    row = iota(shape, 0)
    hit = iota(shape, 1) == RE * (row & 1) + offset
    return one_hot(hit & ((row >> 1) == pair))


def split3(value):
    high = value.astype(BF16).astype(F32)
    rest = value - high
    middle = rest.astype(BF16).astype(F32)
    return high, middle, rest - middle


def lay_stats(shape, dim, start, values):
    place = iota(shape, dim) - start
    out = jnp.zeros(shape, F32)
    for index, value in enumerate(values):
        for part_index, part in enumerate(split3(value)):
            out = jnp.where(place == 3 * index + part_index, part, out)
    return out


def take_stat(rows, start, index):
    place = iota(rows.shape, 1) - start - 3 * index
    return jnp.sum(jnp.where((place >= 0) & (place < 3), rows, 0.0), axis=1, keepdims=True)


def chunk_rows(folded, chunk):
    rows = folded[chunk * CHUNK : (chunk + 1) * CHUNK]
    short = CHUNK - rows.shape[0]
    if short:
        rows = jnp.concatenate([rows, jnp.zeros((short,) + rows.shape[1:], rows.dtype)], axis=0)
    return rows


def near_kernel(
    offset_hbm, key_hbm, value_hbm, near_ref, offset_ref, key_ref, value_ref, semaphores
):
    pairs = ((offset_hbm, offset_ref), (key_hbm, key_ref), (value_hbm, value_ref))
    copies = [
        pltpu.make_async_copy(source, target, semaphores.at[index])
        for index, (source, target) in enumerate(pairs)
    ]
    for copy in copies:
        copy.start()
    for copy in copies:
        copy.wait()
    for head in range(key_ref.shape[0] // HEAD_DIM):
        rows = slice(head * HEAD_DIM, (head + 1) * HEAD_DIM)
        both = jnp.concatenate([key_ref[rows], value_ref[rows]], axis=0)
        picked = mm(near_chooser(offset_ref[head]), both, 1, 1)
        near_ref[head * NEAR : (head + 1) * NEAR, :] = picked.astype(BF16)
    heads = near_ref.shape[0] // NEAR - 1
    row = iota((GAP, LANES), 0)
    told = jnp.zeros((GAP, LANES), F32)
    for head in range(heads):
        told = jnp.where(row == head, offset_ref[head].astype(F32), told)
    near_ref[heads * NEAR :] = told.astype(BF16)


def told_offset(near_ref, head):
    told = near_ref[near_ref.shape[0] - GAP :].astype(F32)
    return told[head : head + 1, :1].astype(jnp.int32)


def pair_count(key_pos, query_pos, offset):
    count = 1.0
    for stride in (RB, RC):
        keys = jnp.where(same_class(key_pos, offset, stride), 1.0, 0.0)
        count = count + keys * jnp.where(same_class(query_pos, offset, stride), 1.0, 0.0)
    return count


def local_kernel(
    side_ref,
    query_ref,
    key_ref,
    value_ref,
    grad_ref,
    weight_ref,
    near_ref,
    slots_ref,
    dout_ref,
    stats_ref,
):
    heads = query_ref.shape[0] // HEAD_DIM
    side = side_ref[0]
    blocks = [grad_ref[2 * core + (chip ^ side)] for chip in range(2) for core in range(2)]
    grad = jnp.concatenate(blocks, axis=0)
    half = grad.shape[0] // 2
    chunks = pl.cdiv(half, CHUNK)
    dout = mm(weight_ref[...], grad, 1, 0).astype(BF16)
    dout_ref[...] = dout
    offsets = [told_offset(near_ref, head) for head in range(heads)]
    choosers = [far_chooser(offsets[head], 3) for head in range(heads)]
    choosers = jnp.concatenate(choosers, axis=0)
    wide = grad.astype(F32)
    filler = jnp.zeros((LANES - 2 * CHUNK, TOKENS_HERE), F32)
    far_grads = []
    for chunk in range(chunks):
        both = [chunk_rows(wide[:half], chunk), chunk_rows(wide[half:], chunk), filler]
        far_grads.append(mm(choosers, jnp.concatenate(both, axis=0).astype(BF16), 1, 1))
    blank = jnp.zeros((HEAD_DIM, TOKENS_HERE), BF16)
    key_pos = iota((TOKENS_HERE, 1), 0)
    query_row = iota((1, TOKENS_HERE), 1)
    query_pos = query_row
    heads = range(heads)
    rows = [slice(head * HEAD_DIM, (head + 1) * HEAD_DIM) for head in heads]
    near = [near_ref[head * NEAR : (head + 1) * NEAR] for head in heads]
    in_near = [same_class(query_row, offset, RC) for offset in offsets]
    in_far = [same_class(query_row, offset, RE) for offset in offsets]
    scores = [mm(key_ref[rows[h]], query_ref[rows[h]], 0, 0) * SCORE_SCALE for h in heads]
    near_scores = [
        mm(near[h], jnp.concatenate([query_ref[rows[h]], blank], axis=0), 1, 0) * SCORE_SCALE
        for h in heads
    ]
    peak = [jnp.max(scores[h], axis=0, keepdims=True) for h in heads]
    near_max = [jnp.max(near_scores[h], axis=0, keepdims=True) for h in heads]
    peak = [jnp.where(in_near[h], jnp.maximum(peak[h], near_max[h]), peak[h]) for h in heads]
    mass = [
        pair_count(key_pos, query_pos, offsets[h]) * jnp.exp(scores[h] - peak[h]) for h in heads
    ]
    near_mass = [jnp.where(in_near[h], jnp.exp(near_scores[h] - peak[h]), 0.0) for h in heads]
    total = [
        jnp.sum(mass[h], axis=0, keepdims=True) + jnp.sum(near_mass[h], axis=0, keepdims=True)
        for h in heads
    ]
    log_mass = [peak[h] + jnp.log(total[h]) for h in heads]
    inverse = [1.0 / total[h] for h in heads]
    probs_low = [(mass[h] * inverse[h]).astype(BF16) for h in heads]
    near_low = [(near_mass[h] * inverse[h]).astype(BF16) for h in heads]
    attended = [
        mm(value_ref[rows[h]], probs_low[h], 1, 0) + mm(near[h], near_low[h], 0, 0)[HEAD_DIM:]
        for h in heads
    ]
    kept = [jnp.where(in_far[h], 0.0, attended[h]).astype(BF16) for h in heads]
    over = [jnp.concatenate([kept[h], blank], axis=0) for h in heads]
    under = [jnp.concatenate([blank, kept[h]], axis=0) for h in heads]
    weight_part = [
        (mm(grad[:half], over[h], 1, 1) + mm(grad[half:], under[h], 1, 1)) * WEIGHT_SCALE
        for h in heads
    ]
    delta = [
        jnp.sum(dout[rows[h]].astype(F32) * attended[h], axis=0, keepdims=True) for h in heads
    ]
    place = iota((SMALL, TOKENS_HERE), 0)
    for h in heads:
        query_dout = jnp.concatenate([query_ref[rows[h]], dout[rows[h]]], axis=0)
        key_value = jnp.concatenate([key_ref[rows[h]], value_ref[rows[h]]], axis=0)
        stats = lay_stats((HEAD_DIM, TOKENS_HERE), 0, 0, (log_mass[h], delta[h]))
        stats_attended = jnp.concatenate([stats.astype(BF16), attended[h].astype(BF16)], axis=0)
        mine = mm(far_chooser(offsets[h], 0), query_dout, 1, 1)
        mine = mine + mm(far_chooser(offsets[h], 1), key_value, 1, 1)
        mine = mine + mm(far_chooser(offsets[h], 2), stats_attended, 1, 1)
        stats_ref[h * SMALL : (h + 1) * SMALL] = jnp.where(place == 0, log_mass[h], delta[h])
        for chunk in range(chunks):
            far_grad = far_grads[chunk][h * GAP : h * GAP + SMALL]
            parts = [chunk_rows(weight_part[h], chunk), mine[:SMALL] + far_grad]
            slots_ref[h * chunks + chunk] = jnp.concatenate(parts, axis=0).astype(BF16)
    heads = len(heads)
    rest = slots_ref.shape[0] - heads * chunks
    slots_ref[heads * chunks :] = jnp.zeros((rest,) + slots_ref.shape[1:], BF16)


def local_grad_kernel(
    query_ref,
    key_ref,
    value_ref,
    dout_ref,
    stats_ref,
    near_ref,
    back_ref,
    grad_query_ref,
    grad_key_ref,
    grad_value_ref,
):
    heads = query_ref.shape[0] // HEAD_DIM
    blank = jnp.zeros((HEAD_DIM, TOKENS_HERE), BF16)
    key_pos = iota((TOKENS_HERE, 1), 0)
    query_row = iota((1, TOKENS_HERE), 1)
    query_pos = query_row
    far_rows = jnp.zeros((GAP, LANES), F32)
    for head in range(heads):
        offset = told_offset(near_ref, head)
        rows = slice(head * HEAD_DIM, (head + 1) * HEAD_DIM)
        near_rows = slice(head * NEAR, (head + 1) * NEAR)
        query, key, value = query_ref[rows], key_ref[rows], value_ref[rows]
        near = near_ref[near_rows]
        dout_head = dout_ref[rows]
        log_mass = stats_ref[head * SMALL : head * SMALL + 1]
        delta = stats_ref[head * SMALL + 1 : head * SMALL + 2]
        query_over = jnp.concatenate([query, blank], axis=0)
        dout_under = jnp.concatenate([blank, dout_head], axis=0)
        in_near = same_class(query_row, offset, RC)
        in_far = same_class(query_row, offset, RE)
        near_only = in_near & jnp.logical_not(in_far)

        scores = mm(key, query, 0, 0) * SCORE_SCALE
        near_scores = mm(near, query_over, 1, 0) * SCORE_SCALE
        probs = pair_count(key_pos, query_pos, offset) * jnp.exp(scores - log_mass)
        probs = jnp.where(in_far, 0.0, probs)
        near_probs = jnp.where(near_only, jnp.exp(near_scores - log_mass), 0.0)
        grad_scores = (probs * (mm(value, dout_head, 0, 0) - delta)).astype(BF16)
        near_grad_scores = (near_probs * (mm(near, dout_under, 1, 0) - delta)).astype(BF16)
        grad_query_ref[rows] = (
            mm(key, grad_scores, 1, 0) + mm(near, near_grad_scores, 0, 0)[:HEAD_DIM]
        )
        grad_key_ref[rows] = mm(query, grad_scores, 1, 1)
        grad_value_ref[rows] = mm(dout_head, probs.astype(BF16), 1, 1)
        back = mm(near_grad_scores, query_over, 1, 1)
        back = back + mm(near_probs.astype(BF16), dout_under, 1, 1)
        back_ref[near_rows] = back.astype(BF16)
        query_dout = jnp.concatenate([query, dout_head], axis=0)
        far_rows = far_rows + mm(far_chooser(offset, head), query_dout, 1, 1)
    back_ref[heads * NEAR :] = far_rows.astype(BF16)


def merge_kernel(slots_ref, merged_ref, far_ref):
    sources = slots_ref.shape[0]
    total = jnp.zeros((SLOT, LANES), F32)
    for source in range(sources):
        block = slots_ref[source].astype(F32)
        total = total + block
        far_ref[source * SMALL : (source + 1) * SMALL] = block[CHUNK:]
    pieces = [far_ref[pl.ds(kind, sources, stride=SMALL), :] for kind in range(SMALL)]
    full = jnp.concatenate([total] + pieces, axis=0).astype(BF16)
    for plane in range(PLANES):
        merged_ref[plane] = full


def far_kernel(plane_ref, merged_ref, slots_ref, returned_ref):
    sources = slots_ref.shape[0]
    width = 2 * sources
    count = PLANES * width

    def kind(index):
        start = SLOT + index * width
        return merged_ref[:, start : start + width, :].reshape(count, LANES)

    query_dout, key_value, stats_attended, far_grad = (kind(index) for index in range(4))
    left = iota((count, LANES), 1) < HEAD_DIM
    shape = (LANES, LANES)
    swap = one_hot(iota(shape, 0) == (iota(shape, 1) ^ HEAD_DIM))
    value_key = mm(key_value, swap, 1, 0).astype(BF16)
    stats = stats_attended.astype(F32)
    attended_stats = mm(stats_attended, swap, 1, 0)
    wide = query_dout.astype(F32)
    query = jnp.where(left, wide, 0.0).astype(BF16)
    dout_wide = jnp.where(left, 0.0, wide)
    local_mass = take_stat(stats, 0, 0)

    scores = mm(query, key_value, 1, 1) * SCORE_SCALE
    grad_probs = mm(dout_wide.astype(BF16), key_value, 1, 1)
    peak = jnp.maximum(jnp.max(scores, axis=1, keepdims=True), local_mass)
    mass = jnp.exp(scores - peak)
    local_part = jnp.exp(local_mass - peak)
    total = jnp.sum(mass, axis=1, keepdims=True) + local_part
    normalizer = peak + jnp.log(total)
    inverse = 1.0 / total
    local_part = local_part * inverse
    probs = mass * inverse
    probs_low = probs.astype(BF16)
    under = local_part * stats + mm(probs_low, key_value, 1, 0)
    delta = jnp.sum(dout_wide * under, axis=1, keepdims=True)
    over = local_part * attended_stats + mm(probs_low, value_key, 1, 0)
    over = jnp.where(left, over, 0.0).astype(BF16)
    under = jnp.where(left, 0.0, under).astype(BF16)
    grad_scores = (probs * (grad_probs - delta)).astype(BF16)

    def other_plane(column):
        blocks = [column[(p ^ 1) * width : ((p ^ 1) + 1) * width] for p in range(PLANES)]
        return jnp.concatenate(blocks, axis=0)

    weight_part = mm(far_grad, over, 0, 0)[:CHUNK] + mm(far_grad, under, 0, 0)[CHUNK : 2 * CHUNK]
    weight_part = weight_part * WEIGHT_SCALE
    for plane in range(PLANES):
        weight_part = weight_part + merged_ref[plane, :SLOT].astype(F32)[:CHUNK]
    own_stats = lay_stats((count, LANES), 1, HEAD_DIM, (normalizer, delta))
    other_stats = lay_stats((count, LANES), 1, 0, (other_plane(normalizer), other_plane(delta)))
    returned_ref[0] = jnp.where(left, other_stats, mm(probs_low, query_dout, 0, 0))
    returned_ref[1] = jnp.where(left, mm(grad_scores, key_value, 1, 0), own_stats)
    returned_ref[2] = jnp.where(left, mm(grad_scores, query_dout, 0, 0), 0.0)
    own = pl.ds(pl.multiple_of(plane_ref[0] * width, width), width)
    shape = (sources * SMALL, width)
    row, column = iota(shape, 0), iota(shape, 1)
    same = (row // SMALL) == (column % sources)
    slot_row, pair = row % SMALL, column // sources
    placed = jnp.zeros((sources * SMALL, LANES), F32)
    for index in range(returned_ref.shape[0]):
        chosen = one_hot(same & (slot_row == pair + 2 * index))
        placed = placed + mm(chosen, returned_ref[index, own, :].astype(BF16), 1, 0)
    for source in range(sources):
        parts = [weight_part, placed[source * SMALL : (source + 1) * SMALL]]
        slots_ref[source] = jnp.concatenate(parts, axis=0).astype(BF16)


def prepare_kernel(
    key_ref,
    value_ref,
    near_ref,
    own_ref,
    partner_ref,
    local_key_ref,
    local_value_ref,
    rows_ref,
    scores_ref,
    grad_probs_ref,
    keys_ref,
    chooser_ref,
    grad_key_ref,
    grad_value_ref,
):
    heads = key_ref.shape[0] // HEAD_DIM
    first_far = heads * NEAR
    blank = jnp.zeros((HEAD_DIM, TOKENS_HERE + LANES), BF16)
    shape = (GAP, GAP)
    row, column = iota(shape, 0), iota(shape, 1)
    widen = one_hot(iota((NEAR, LANES), 0) == iota((NEAR, LANES), 1))
    shape = (GAP, TOKENS_HERE + LANES)
    block_row, place = iota(shape, 0), iota(shape, 1)
    here = place < TOKENS_HERE
    from_partner, from_here = block_row < 2, (block_row >= 2) & (block_row < 4)
    for head in range(heads):
        offset = told_offset(near_ref, head)
        rows = slice(head * HEAD_DIM, (head + 1) * HEAD_DIM)
        block = slice(head * GAP, (head + 1) * GAP)
        key, value = key_ref[rows], value_ref[rows]
        near = mm(near_ref[block], widen, 0, 0).astype(BF16)
        keys = jnp.concatenate([key, near[:HEAD_DIM]], axis=1)
        values = jnp.concatenate([value, near[HEAD_DIM:]], axis=1)
        keys = jnp.concatenate([keys, blank], axis=0)
        values = jnp.concatenate([blank, values], axis=0)
        from_partner_far = one_hot((row < 2) & (column == row + 2 * head))
        from_own_far = one_hot((row >= 2) & (row < 4) & (column == row - 2 + 2 * head))
        chosen = mm(from_partner_far, partner_ref[first_far:], 1, 0)
        chosen = (chosen + mm(from_own_far, own_ref[first_far:], 1, 0)).astype(BF16)
        in_near = here & same_class(place, offset, RC)
        extra = jnp.where(here & same_class(place, offset, RB), 1.0, 0.0)
        extra = extra + jnp.where(in_near, 1.0, 0.0)
        mask_here = jnp.where(place < TOKENS_HERE + NEAR, jnp.log(1.0 + extra), ABSENT)
        mask = jnp.where(from_here, mask_here, ABSENT)
        mask = jnp.where(from_partner & in_near, 0.0, mask)
        rows_ref[block] = chosen
        scores_ref[block] = mm(chosen, keys, 1, 0) * SCORE_SCALE + mask
        grad_probs_ref[block] = mm(chosen, values, 1, 0)
        keys_ref[head] = keys
        for pair in range(3):
            chooser_ref[head, pair] = far_chooser(offset, pair)
        spread = mm(partner_ref[block], near_chooser(offset), 0, 0)
        grad_key_ref[rows] = local_key_ref[rows] + spread[:HEAD_DIM]
        grad_value_ref[rows] = local_value_ref[rows] + spread[HEAD_DIM:]


def final_kernel(
    rows_ref,
    scores_ref,
    grad_probs_ref,
    keys_ref,
    chooser_ref,
    local_query_ref,
    local_key_ref,
    local_value_ref,
    slots_ref,
    grad_query_ref,
    grad_key_ref,
    grad_value_ref,
    grad_weight_ref,
):
    heads = local_query_ref.shape[0] // HEAD_DIM
    half = grad_weight_ref.shape[1] // 2
    chunks = pl.cdiv(half, CHUNK)
    eye = one_hot(iota((LANES, LANES), 0) == iota((LANES, LANES), 1))
    for head in range(heads):
        rows = slice(head * HEAD_DIM, (head + 1) * HEAD_DIM)
        block = slice(head * GAP, (head + 1) * GAP)
        pieces = [slots_ref[head * chunks + chunk].astype(F32) for chunk in range(chunks)]
        folded = jnp.concatenate([piece[:CHUNK] for piece in pieces], axis=0)[:half]
        unfolded = mm(eye, folded.astype(BF16), 1, 1)
        grad_weight_ref[rows, :half] = unfolded[:HEAD_DIM]
        grad_weight_ref[rows, half:] = unfolded[HEAD_DIM:]

        returned = jnp.concatenate(
            [pieces[0][CHUNK:], jnp.zeros((GAP - SMALL, LANES), F32)], axis=0
        )
        chosen = rows_ref[block]
        start = jnp.where(iota(returned.shape, 0) < 2, 0, HEAD_DIM)
        normalizer, delta = (take_stat(returned, start, index) for index in range(2))
        probs = jnp.exp(scores_ref[block] - normalizer)
        grad_scores = (probs * (grad_probs_ref[block] - delta)).astype(BF16)
        probs_low = probs[:, :TOKENS_HERE].astype(BF16)
        far_query = (returned + mm(grad_scores, keys_ref[head], 1, 1)).astype(BF16)
        returned = returned.astype(BF16)
        grad_query = mm(far_query, chooser_ref[head, 1], 0, 0)[:HEAD_DIM]
        grad_key = mm(returned, chooser_ref[head, 2], 0, 0)[:HEAD_DIM]
        grad_key = grad_key + mm(chosen, grad_scores[:, :TOKENS_HERE], 0, 0)[:HEAD_DIM]
        grad_value = mm(returned, chooser_ref[head, 0], 0, 0)[HEAD_DIM:]
        grad_value = grad_value + mm(chosen, probs_low, 0, 0)[HEAD_DIM:]
        grad_query = (local_query_ref[rows] + grad_query) * SCORE_SCALE
        grad_key = (local_key_ref[rows] + grad_key) * SCORE_SCALE
        grad_query_ref[rows] = grad_query.astype(BF16)
        grad_key_ref[rows] = grad_key.astype(BF16)
        grad_value_ref[rows] = (local_value_ref[rows] + grad_value).astype(BF16)


def call(kernel, outs, arrays, scalars=0, scratch=(), space=pltpu.VMEM, limit=40 << 20):
    specs = [pl.BlockSpec(memory_space=pltpu.SMEM)] * scalars
    specs = specs + [pl.BlockSpec(memory_space=space)] * (len(arrays) - scalars)
    shapes = [jax.ShapeDtypeStruct(shape, dtype) for shape, dtype in outs]
    return pl.pallas_call(
        kernel,
        out_shape=shapes,
        in_specs=specs,
        out_specs=[pl.BlockSpec(memory_space=pltpu.VMEM)] * len(shapes),
        scratch_shapes=list(scratch),
        compiler_params=pltpu.CompilerParams(vmem_limit_bytes=limit),
        name=kernel.__name__,
    )(*arrays)


def local(queries, keys, values, grad_out, out_weight, offsets):
    features = queries.shape[0]
    model = out_weight.shape[1]
    heads = offsets.shape[0]
    sources = lax.axis_size("xz")
    near_shape = ((heads * NEAR + GAP, LANES), BF16)
    back_shape = ((heads * NEAR + GAP, LANES), BF16)
    slots_shape = ((sources, SLOT, LANES), BF16)
    merged_shape = ((PLANES, SLOT + sources * SMALL, LANES), BF16)
    wide_shape = ((features, TOKENS_HERE), F32)
    grad_shape = ((features, TOKENS_HERE), BF16)
    block_shape = ((heads * GAP, TOKENS_HERE + LANES), F32)
    other = [(i, i ^ 1) for i in range(PLANES)]

    scratch = [
        pltpu.SMEM(offsets.shape, offsets.dtype),
        pltpu.VMEM(keys.shape, keys.dtype),
        pltpu.VMEM(values.shape, values.dtype),
        pltpu.SemaphoreType.DMA((3,)),
    ]
    other_grad = lax.ppermute(grad_out, "chip", [(0, 1), (1, 0)])
    (near,) = call(
        near_kernel,
        [near_shape],
        (offsets, keys, values),
        scratch=scratch,
        space=pltpu.HBM,
        limit=LIMIT,
    )
    near = lax.ppermute(near, "yh", other)
    pair_grads = lax.all_gather(jnp.stack([grad_out, other_grad]), "core", axis=0, tiled=True)
    side = lax.axis_index("chip").reshape(1)
    slots, dout, stats = call(
        local_kernel,
        [slots_shape, grad_shape, ((heads * SMALL, TOKENS_HERE), F32)],
        (side, queries, keys, values, pair_grads, out_weight, near),
        scalars=1,
    )
    slots = lax.all_to_all(slots, "xz", 0, 0, tiled=True)
    own, local_query, local_key, local_value = call(
        local_grad_kernel,
        [back_shape, wide_shape, wide_shape, wide_shape],
        (queries, keys, values, dout, stats, near),
    )
    partner = lax.ppermute(own, "yh", other)
    prepared = call(
        prepare_kernel,
        [
            ((heads * GAP, LANES), BF16),
            block_shape,
            block_shape,
            ((heads, LANES, TOKENS_HERE + LANES), BF16),
            ((heads, 3, GAP, TOKENS_HERE), BF16),
            wide_shape,
            wide_shape,
        ],
        (keys, values, near, own, partner, local_key, local_value),
    )
    plane = lax.axis_index("yh").reshape(1)
    slots, prepared, local_query, plane = lax.optimization_barrier(
        (slots, prepared, local_query, plane)
    )
    rows, scores, grad_probs, wide_keys, chooser, local_key, local_value = prepared
    (merged,) = call(
        merge_kernel,
        [merged_shape],
        (slots,),
        scratch=[pltpu.VMEM((sources * SMALL, LANES), F32)],
    )
    merged = lax.all_to_all(merged, "yh", 0, 0, tiled=True)
    (slots,) = call(
        far_kernel,
        [slots_shape],
        (plane, merged),
        scalars=1,
        scratch=[pltpu.VMEM((3, PLANES * sources * 2, LANES), F32)],
    )
    slots = lax.all_to_all(slots, "xz", 0, 0, tiled=True)
    return tuple(
        call(
            final_kernel,
            [grad_shape, grad_shape, grad_shape, ((features, model), F32)],
            (
                rows,
                scores,
                grad_probs,
                wide_keys,
                chooser,
                local_query,
                local_key,
                local_value,
                slots,
            ),
        )
    )


def solution(mesh):
    devices = mesh.devices.reshape(-1, PLANES, 2, mesh.devices.shape[1] // 2)
    split_mesh = Mesh(devices, ("xz", "yh", "chip", "core"))
    parts = ("chip", "core")
    wide = P(parts, ("xz", "yh"))
    return jax.shard_map(
        local,
        mesh=split_mesh,
        in_specs=(wide, wide, wide, wide, P(parts, None), P(parts)),
        out_specs=(wide, wide, wide, P(parts, None)),
        check_vma=False,
    )
```

```python
import jax
import jax.numpy as jnp
from jax import lax
from jax.experimental import pallas as pl
from jax.experimental.pallas import tpu as pltpu
from jax.sharding import Mesh
from jax.sharding import PartitionSpec as P

HEAD_DIM = 64
TOKENS_HERE = 256
RB = 2
RC = 16
RE = 128
NEAR = TOKENS_HERE // RC
SCORE_SCALE = HEAD_DIM ** (-0.5)
WEIGHT_SCALE = 0.03125

PLANES = 4
LANES = 128
GAP = 16
SMALL = 8
CHUNK = 40
SLOT = CHUNK + SMALL
ABSENT = -1e30
LIMIT = 40 << 20

F32 = jnp.float32
BF16 = jnp.bfloat16


def mm(left, right, left_dim, right_dim):
    return lax.dot_general(
        left, right, (((left_dim,), (right_dim,)), ((), ())), preferred_element_type=F32
    )


def iota(shape, dim):
    return lax.broadcasted_iota(jnp.int32, shape, dim)


def one_hot(condition):
    return jnp.where(condition, 1.0, 0.0).astype(BF16)


def same_class(position, offset, stride):
    return (position & (stride - 1)) == (offset & (stride - 1))


def near_chooser(offset):
    shape = (NEAR, TOKENS_HERE)
    return one_hot(iota(shape, 1) == RC * iota(shape, 0) + (offset & (RC - 1)))


def far_chooser(offset, pair):
    shape = (GAP, TOKENS_HERE)
    row = iota(shape, 0)
    hit = iota(shape, 1) == RE * (row & 1) + offset
    return one_hot(hit & ((row >> 1) == pair))


def split3(value):
    high = value.astype(BF16).astype(F32)
    rest = value - high
    middle = rest.astype(BF16).astype(F32)
    return high, middle, rest - middle


def lay_stats(shape, dim, start, values):
    place = iota(shape, dim) - start
    out = jnp.zeros(shape, F32)
    for index, value in enumerate(values):
        for part_index, part in enumerate(split3(value)):
            out = jnp.where(place == 3 * index + part_index, part, out)
    return out


def take_stat(rows, start, index):
    place = iota(rows.shape, 1) - start - 3 * index
    return jnp.sum(jnp.where((place >= 0) & (place < 3), rows, 0.0), axis=1, keepdims=True)


def chunk_rows(folded, chunk):
    rows = folded[chunk * CHUNK : (chunk + 1) * CHUNK]
    short = CHUNK - rows.shape[0]
    if short:
        rows = jnp.concatenate([rows, jnp.zeros((short,) + rows.shape[1:], rows.dtype)], axis=0)
    return rows


def near_kernel(
    offset_hbm, key_hbm, value_hbm, near_ref, offset_ref, key_ref, value_ref, semaphores
):
    pairs = ((offset_hbm, offset_ref), (key_hbm, key_ref), (value_hbm, value_ref))
    copies = [
        pltpu.make_async_copy(source, target, semaphores.at[index])
        for index, (source, target) in enumerate(pairs)
    ]
    for copy in copies:
        copy.start()
    for copy in copies:
        copy.wait()
    for head in range(key_ref.shape[0] // HEAD_DIM):
        rows = slice(head * HEAD_DIM, (head + 1) * HEAD_DIM)
        both = jnp.concatenate([key_ref[rows], value_ref[rows]], axis=0)
        picked = mm(near_chooser(offset_ref[head]), both, 1, 1)
        near_ref[head * NEAR : (head + 1) * NEAR, :] = picked.astype(BF16)
    heads = near_ref.shape[0] // NEAR - 1
    row = iota((GAP, LANES), 0)
    told = jnp.zeros((GAP, LANES), F32)
    for head in range(heads):
        told = jnp.where(row == head, offset_ref[head].astype(F32), told)
    near_ref[heads * NEAR :] = told.astype(BF16)


def told_offset(near_ref, head):
    told = near_ref[near_ref.shape[0] - GAP :].astype(F32)
    return told[head : head + 1, :1].astype(jnp.int32)


def pair_count(key_pos, query_pos, offset):
    count = 1.0
    for stride in (RB, RC):
        keys = jnp.where(same_class(key_pos, offset, stride), 1.0, 0.0)
        count = count + keys * jnp.where(same_class(query_pos, offset, stride), 1.0, 0.0)
    return count


def local_kernel(
    side_ref,
    query_ref,
    key_ref,
    value_ref,
    grad_ref,
    weight_ref,
    near_ref,
    slots_ref,
    dout_ref,
    stats_ref,
):
    heads = query_ref.shape[0] // HEAD_DIM
    side = side_ref[0]
    blocks = [grad_ref[2 * core + (chip ^ side)] for chip in range(2) for core in range(2)]
    grad = jnp.concatenate(blocks, axis=0)
    half = grad.shape[0] // 2
    chunks = pl.cdiv(half, CHUNK)
    dout = mm(weight_ref[...], grad, 1, 0).astype(BF16)
    dout_ref[...] = dout
    offsets = [told_offset(near_ref, head) for head in range(heads)]
    choosers = [far_chooser(offsets[head], 3) for head in range(heads)]
    choosers = jnp.concatenate(choosers, axis=0)
    wide = grad.astype(F32)
    filler = jnp.zeros((LANES - 2 * CHUNK, TOKENS_HERE), F32)
    far_grads = []
    for chunk in range(chunks):
        both = [chunk_rows(wide[:half], chunk), chunk_rows(wide[half:], chunk), filler]
        far_grads.append(mm(choosers, jnp.concatenate(both, axis=0).astype(BF16), 1, 1))
    blank = jnp.zeros((HEAD_DIM, TOKENS_HERE), BF16)
    key_pos = iota((TOKENS_HERE, 1), 0)
    query_row = iota((1, TOKENS_HERE), 1)
    query_pos = query_row
    heads = range(heads)
    rows = [slice(head * HEAD_DIM, (head + 1) * HEAD_DIM) for head in heads]
    near = [near_ref[head * NEAR : (head + 1) * NEAR] for head in heads]
    in_near = [same_class(query_row, offset, RC) for offset in offsets]
    in_far = [same_class(query_row, offset, RE) for offset in offsets]
    scores = [mm(key_ref[rows[h]], query_ref[rows[h]], 0, 0) * SCORE_SCALE for h in heads]
    near_scores = [
        mm(near[h], jnp.concatenate([query_ref[rows[h]], blank], axis=0), 1, 0) * SCORE_SCALE
        for h in heads
    ]
    peak = [jnp.max(scores[h], axis=0, keepdims=True) for h in heads]
    near_max = [jnp.max(near_scores[h], axis=0, keepdims=True) for h in heads]
    peak = [jnp.where(in_near[h], jnp.maximum(peak[h], near_max[h]), peak[h]) for h in heads]
    mass = [
        pair_count(key_pos, query_pos, offsets[h]) * jnp.exp(scores[h] - peak[h]) for h in heads
    ]
    near_mass = [jnp.where(in_near[h], jnp.exp(near_scores[h] - peak[h]), 0.0) for h in heads]
    total = [
        jnp.sum(mass[h], axis=0, keepdims=True) + jnp.sum(near_mass[h], axis=0, keepdims=True)
        for h in heads
    ]
    log_mass = [peak[h] + jnp.log(total[h]) for h in heads]
    inverse = [1.0 / total[h] for h in heads]
    probs_low = [(mass[h] * inverse[h]).astype(BF16) for h in heads]
    near_low = [(near_mass[h] * inverse[h]).astype(BF16) for h in heads]
    attended = [
        mm(value_ref[rows[h]], probs_low[h], 1, 0) + mm(near[h], near_low[h], 0, 0)[HEAD_DIM:]
        for h in heads
    ]
    kept = [jnp.where(in_far[h], 0.0, attended[h]).astype(BF16) for h in heads]
    over = [jnp.concatenate([kept[h], blank], axis=0) for h in heads]
    under = [jnp.concatenate([blank, kept[h]], axis=0) for h in heads]
    weight_part = [
        (mm(grad[:half], over[h], 1, 1) + mm(grad[half:], under[h], 1, 1)) * WEIGHT_SCALE
        for h in heads
    ]
    delta = [
        jnp.sum(dout[rows[h]].astype(F32) * attended[h], axis=0, keepdims=True) for h in heads
    ]
    place = iota((SMALL, TOKENS_HERE), 0)
    for h in heads:
        query_dout = jnp.concatenate([query_ref[rows[h]], dout[rows[h]]], axis=0)
        key_value = jnp.concatenate([key_ref[rows[h]], value_ref[rows[h]]], axis=0)
        stats = lay_stats((HEAD_DIM, TOKENS_HERE), 0, 0, (log_mass[h], delta[h]))
        stats_attended = jnp.concatenate([stats.astype(BF16), attended[h].astype(BF16)], axis=0)
        mine = mm(far_chooser(offsets[h], 0), query_dout, 1, 1)
        mine = mine + mm(far_chooser(offsets[h], 1), key_value, 1, 1)
        mine = mine + mm(far_chooser(offsets[h], 2), stats_attended, 1, 1)
        stats_ref[h * SMALL : (h + 1) * SMALL] = jnp.where(place == 0, log_mass[h], delta[h])
        for chunk in range(chunks):
            far_grad = far_grads[chunk][h * GAP : h * GAP + SMALL]
            parts = [chunk_rows(weight_part[h], chunk), mine[:SMALL] + far_grad]
            slots_ref[h * chunks + chunk] = jnp.concatenate(parts, axis=0).astype(BF16)
    heads = len(heads)
    rest = slots_ref.shape[0] - heads * chunks
    slots_ref[heads * chunks :] = jnp.zeros((rest,) + slots_ref.shape[1:], BF16)


def local_grad_kernel(
    query_ref,
    key_ref,
    value_ref,
    dout_ref,
    stats_ref,
    near_ref,
    back_ref,
    grad_query_ref,
    grad_key_ref,
    grad_value_ref,
):
    heads = query_ref.shape[0] // HEAD_DIM
    blank = jnp.zeros((HEAD_DIM, TOKENS_HERE), BF16)
    key_pos = iota((TOKENS_HERE, 1), 0)
    query_row = iota((1, TOKENS_HERE), 1)
    query_pos = query_row
    far_rows = jnp.zeros((GAP, LANES), F32)
    for head in range(heads):
        offset = told_offset(near_ref, head)
        rows = slice(head * HEAD_DIM, (head + 1) * HEAD_DIM)
        near_rows = slice(head * NEAR, (head + 1) * NEAR)
        query, key, value = query_ref[rows], key_ref[rows], value_ref[rows]
        near = near_ref[near_rows]
        dout_head = dout_ref[rows]
        log_mass = stats_ref[head * SMALL : head * SMALL + 1]
        delta = stats_ref[head * SMALL + 1 : head * SMALL + 2]
        query_over = jnp.concatenate([query, blank], axis=0)
        dout_under = jnp.concatenate([blank, dout_head], axis=0)
        in_near = same_class(query_row, offset, RC)
        in_far = same_class(query_row, offset, RE)
        near_only = in_near & jnp.logical_not(in_far)

        scores = mm(key, query, 0, 0) * SCORE_SCALE
        near_scores = mm(near, query_over, 1, 0) * SCORE_SCALE
        probs = pair_count(key_pos, query_pos, offset) * jnp.exp(scores - log_mass)
        probs = jnp.where(in_far, 0.0, probs)
        near_probs = jnp.where(near_only, jnp.exp(near_scores - log_mass), 0.0)
        grad_scores = (probs * (mm(value, dout_head, 0, 0) - delta)).astype(BF16)
        near_grad_scores = (near_probs * (mm(near, dout_under, 1, 0) - delta)).astype(BF16)
        grad_query_ref[rows] = (
            mm(key, grad_scores, 1, 0) + mm(near, near_grad_scores, 0, 0)[:HEAD_DIM]
        )
        grad_key_ref[rows] = mm(query, grad_scores, 1, 1)
        grad_value_ref[rows] = mm(dout_head, probs.astype(BF16), 1, 1)
        back = mm(near_grad_scores, query_over, 1, 1)
        back = back + mm(near_probs.astype(BF16), dout_under, 1, 1)
        back_ref[near_rows] = back.astype(BF16)
        query_dout = jnp.concatenate([query, dout_head], axis=0)
        far_rows = far_rows + mm(far_chooser(offset, head), query_dout, 1, 1)
    back_ref[heads * NEAR :] = far_rows.astype(BF16)


def merge_kernel(slots_ref, merged_ref, far_ref):
    sources = slots_ref.shape[0]
    total = jnp.zeros((SLOT, LANES), F32)
    for source in range(sources):
        block = slots_ref[source].astype(F32)
        total = total + block
        far_ref[source * SMALL : (source + 1) * SMALL] = block[CHUNK:]
    pieces = [far_ref[pl.ds(kind, sources, stride=SMALL), :] for kind in range(SMALL)]
    full = jnp.concatenate([total] + pieces, axis=0).astype(BF16)
    for plane in range(PLANES):
        merged_ref[plane] = full


def far_kernel(plane_ref, merged_ref, slots_ref, returned_ref):
    sources = slots_ref.shape[0]
    width = 2 * sources
    count = PLANES * width

    def kind(index):
        start = SLOT + index * width
        return merged_ref[:, start : start + width, :].reshape(count, LANES)

    query_dout, key_value, stats_attended, far_grad = (kind(index) for index in range(4))
    left = iota((count, LANES), 1) < HEAD_DIM
    shape = (LANES, LANES)
    swap = one_hot(iota(shape, 0) == (iota(shape, 1) ^ HEAD_DIM))
    value_key = mm(key_value, swap, 1, 0).astype(BF16)
    stats = stats_attended.astype(F32)
    attended_stats = mm(stats_attended, swap, 1, 0)
    wide = query_dout.astype(F32)
    query = jnp.where(left, wide, 0.0).astype(BF16)
    dout_wide = jnp.where(left, 0.0, wide)
    local_mass = take_stat(stats, 0, 0)

    scores = mm(query, key_value, 1, 1) * SCORE_SCALE
    grad_probs = mm(dout_wide.astype(BF16), key_value, 1, 1)
    peak = jnp.maximum(jnp.max(scores, axis=1, keepdims=True), local_mass)
    mass = jnp.exp(scores - peak)
    local_part = jnp.exp(local_mass - peak)
    total = jnp.sum(mass, axis=1, keepdims=True) + local_part
    normalizer = peak + jnp.log(total)
    inverse = 1.0 / total
    local_part = local_part * inverse
    probs = mass * inverse
    probs_low = probs.astype(BF16)
    under = local_part * stats + mm(probs_low, key_value, 1, 0)
    delta = jnp.sum(dout_wide * under, axis=1, keepdims=True)
    over = local_part * attended_stats + mm(probs_low, value_key, 1, 0)
    over = jnp.where(left, over, 0.0).astype(BF16)
    under = jnp.where(left, 0.0, under).astype(BF16)
    grad_scores = (probs * (grad_probs - delta)).astype(BF16)

    def other_plane(column):
        blocks = [column[(p ^ 1) * width : ((p ^ 1) + 1) * width] for p in range(PLANES)]
        return jnp.concatenate(blocks, axis=0)

    weight_part = mm(far_grad, over, 0, 0)[:CHUNK] + mm(far_grad, under, 0, 0)[CHUNK : 2 * CHUNK]
    weight_part = weight_part * WEIGHT_SCALE
    for plane in range(PLANES):
        weight_part = weight_part + merged_ref[plane, :SLOT].astype(F32)[:CHUNK]
    own_stats = lay_stats((count, LANES), 1, HEAD_DIM, (normalizer, delta))
    other_stats = lay_stats((count, LANES), 1, 0, (other_plane(normalizer), other_plane(delta)))
    returned_ref[0] = jnp.where(left, other_stats, mm(probs_low, query_dout, 0, 0))
    returned_ref[1] = jnp.where(left, mm(grad_scores, key_value, 1, 0), own_stats)
    returned_ref[2] = jnp.where(left, mm(grad_scores, query_dout, 0, 0), 0.0)
    own = pl.ds(pl.multiple_of(plane_ref[0] * width, width), width)
    shape = (sources * SMALL, width)
    row, column = iota(shape, 0), iota(shape, 1)
    same = (row // SMALL) == (column % sources)
    slot_row, pair = row % SMALL, column // sources
    placed = jnp.zeros((sources * SMALL, LANES), F32)
    for index in range(returned_ref.shape[0]):
        chosen = one_hot(same & (slot_row == pair + 2 * index))
        placed = placed + mm(chosen, returned_ref[index, own, :].astype(BF16), 1, 0)
    for source in range(sources):
        parts = [weight_part, placed[source * SMALL : (source + 1) * SMALL]]
        slots_ref[source] = jnp.concatenate(parts, axis=0).astype(BF16)


def prepare_kernel(
    key_ref,
    value_ref,
    near_ref,
    own_ref,
    partner_ref,
    local_key_ref,
    local_value_ref,
    rows_ref,
    scores_ref,
    grad_probs_ref,
    keys_ref,
    chooser_ref,
    grad_key_ref,
    grad_value_ref,
):
    heads = key_ref.shape[0] // HEAD_DIM
    first_far = heads * NEAR
    blank = jnp.zeros((HEAD_DIM, TOKENS_HERE + LANES), BF16)
    shape = (GAP, GAP)
    row, column = iota(shape, 0), iota(shape, 1)
    widen = one_hot(iota((NEAR, LANES), 0) == iota((NEAR, LANES), 1))
    shape = (GAP, TOKENS_HERE + LANES)
    block_row, place = iota(shape, 0), iota(shape, 1)
    here = place < TOKENS_HERE
    from_partner, from_here = block_row < 2, (block_row >= 2) & (block_row < 4)
    for head in range(heads):
        offset = told_offset(near_ref, head)
        rows = slice(head * HEAD_DIM, (head + 1) * HEAD_DIM)
        block = slice(head * GAP, (head + 1) * GAP)
        key, value = key_ref[rows], value_ref[rows]
        near = mm(near_ref[block], widen, 0, 0).astype(BF16)
        keys = jnp.concatenate([key, near[:HEAD_DIM]], axis=1)
        values = jnp.concatenate([value, near[HEAD_DIM:]], axis=1)
        keys = jnp.concatenate([keys, blank], axis=0)
        values = jnp.concatenate([blank, values], axis=0)
        from_partner_far = one_hot((row < 2) & (column == row + 2 * head))
        from_own_far = one_hot((row >= 2) & (row < 4) & (column == row - 2 + 2 * head))
        chosen = mm(from_partner_far, partner_ref[first_far:], 1, 0)
        chosen = (chosen + mm(from_own_far, own_ref[first_far:], 1, 0)).astype(BF16)
        in_near = here & same_class(place, offset, RC)
        extra = jnp.where(here & same_class(place, offset, RB), 1.0, 0.0)
        extra = extra + jnp.where(in_near, 1.0, 0.0)
        mask_here = jnp.where(place < TOKENS_HERE + NEAR, jnp.log(1.0 + extra), ABSENT)
        mask = jnp.where(from_here, mask_here, ABSENT)
        mask = jnp.where(from_partner & in_near, 0.0, mask)
        rows_ref[block] = chosen
        scores_ref[block] = mm(chosen, keys, 1, 0) * SCORE_SCALE + mask
        grad_probs_ref[block] = mm(chosen, values, 1, 0)
        keys_ref[head] = keys
        for pair in range(3):
            chooser_ref[head, pair] = far_chooser(offset, pair)
        spread = mm(partner_ref[block], near_chooser(offset), 0, 0)
        grad_key_ref[rows] = local_key_ref[rows] + spread[:HEAD_DIM]
        grad_value_ref[rows] = local_value_ref[rows] + spread[HEAD_DIM:]


def final_kernel(
    rows_ref,
    scores_ref,
    grad_probs_ref,
    keys_ref,
    chooser_ref,
    local_query_ref,
    local_key_ref,
    local_value_ref,
    slots_ref,
    grad_query_ref,
    grad_key_ref,
    grad_value_ref,
    grad_weight_ref,
):
    heads = local_query_ref.shape[0] // HEAD_DIM
    half = grad_weight_ref.shape[1] // 2
    chunks = pl.cdiv(half, CHUNK)
    eye = one_hot(iota((LANES, LANES), 0) == iota((LANES, LANES), 1))
    for head in range(heads):
        rows = slice(head * HEAD_DIM, (head + 1) * HEAD_DIM)
        block = slice(head * GAP, (head + 1) * GAP)
        pieces = [slots_ref[head * chunks + chunk].astype(F32) for chunk in range(chunks)]
        folded = jnp.concatenate([piece[:CHUNK] for piece in pieces], axis=0)[:half]
        unfolded = mm(eye, folded.astype(BF16), 1, 1)
        grad_weight_ref[rows, :half] = unfolded[:HEAD_DIM]
        grad_weight_ref[rows, half:] = unfolded[HEAD_DIM:]

        returned = jnp.concatenate(
            [pieces[0][CHUNK:], jnp.zeros((GAP - SMALL, LANES), F32)], axis=0
        )
        chosen = rows_ref[block]
        start = jnp.where(iota(returned.shape, 0) < 2, 0, HEAD_DIM)
        normalizer, delta = (take_stat(returned, start, index) for index in range(2))
        probs = jnp.exp(scores_ref[block] - normalizer)
        grad_scores = (probs * (grad_probs_ref[block] - delta)).astype(BF16)
        probs_low = probs[:, :TOKENS_HERE].astype(BF16)
        far_query = (returned + mm(grad_scores, keys_ref[head], 1, 1)).astype(BF16)
        returned = returned.astype(BF16)
        grad_query = mm(far_query, chooser_ref[head, 1], 0, 0)[:HEAD_DIM]
        grad_key = mm(returned, chooser_ref[head, 2], 0, 0)[:HEAD_DIM]
        grad_key = grad_key + mm(chosen, grad_scores[:, :TOKENS_HERE], 0, 0)[:HEAD_DIM]
        grad_value = mm(returned, chooser_ref[head, 0], 0, 0)[HEAD_DIM:]
        grad_value = grad_value + mm(chosen, probs_low, 0, 0)[HEAD_DIM:]
        grad_query = (local_query_ref[rows] + grad_query) * SCORE_SCALE
        grad_key = (local_key_ref[rows] + grad_key) * SCORE_SCALE
        grad_query_ref[rows] = grad_query.astype(BF16)
        grad_key_ref[rows] = grad_key.astype(BF16)
        grad_value_ref[rows] = (local_value_ref[rows] + grad_value).astype(BF16)


def call(kernel, outs, arrays, scalars=0, scratch=(), space=pltpu.VMEM, limit=40 << 20):
    specs = [pl.BlockSpec(memory_space=pltpu.SMEM)] * scalars
    specs = specs + [pl.BlockSpec(memory_space=space)] * (len(arrays) - scalars)
    shapes = [jax.ShapeDtypeStruct(shape, dtype) for shape, dtype in outs]
    return pl.pallas_call(
        kernel,
        out_shape=shapes,
        in_specs=specs,
        out_specs=[pl.BlockSpec(memory_space=pltpu.VMEM)] * len(shapes),
        scratch_shapes=list(scratch),
        compiler_params=pltpu.CompilerParams(vmem_limit_bytes=limit),
        name=kernel.__name__,
    )(*arrays)


def local(queries, keys, values, grad_out, out_weight, offsets):
    features = queries.shape[0]
    model = out_weight.shape[1]
    heads = offsets.shape[0]
    sources = lax.axis_size("xz")
    near_shape = ((heads * NEAR + GAP, LANES), BF16)
    back_shape = ((heads * NEAR + GAP, LANES), BF16)
    slots_shape = ((sources, SLOT, LANES), BF16)
    merged_shape = ((PLANES, SLOT + sources * SMALL, LANES), BF16)
    wide_shape = ((features, TOKENS_HERE), F32)
    grad_shape = ((features, TOKENS_HERE), BF16)
    block_shape = ((heads * GAP, TOKENS_HERE + LANES), F32)
    other = [(i, i ^ 1) for i in range(PLANES)]

    scratch = [
        pltpu.SMEM(offsets.shape, offsets.dtype),
        pltpu.VMEM(keys.shape, keys.dtype),
        pltpu.VMEM(values.shape, values.dtype),
        pltpu.SemaphoreType.DMA((3,)),
    ]
    other_grad = lax.ppermute(grad_out, "chip", [(0, 1), (1, 0)])
    (near,) = call(
        near_kernel,
        [near_shape],
        tuple(pltpu.with_memory_space_constraint(x, pltpu.HBM) for x in (offsets, keys, values)),
        scratch=scratch,
        space=pltpu.HBM,
        limit=LIMIT,
    )
    near = lax.ppermute(near, "yh", other)
    pair_grads = lax.all_gather(jnp.stack([grad_out, other_grad]), "core", axis=0, tiled=True)
    side = lax.axis_index("chip").reshape(1)
    slots, dout, stats = call(
        local_kernel,
        [slots_shape, grad_shape, ((heads * SMALL, TOKENS_HERE), F32)],
        (side, queries, keys, values, pair_grads, out_weight, near),
        scalars=1,
    )
    slots = lax.all_to_all(slots, "xz", 0, 0, tiled=True)
    own, local_query, local_key, local_value = call(
        local_grad_kernel,
        [back_shape, wide_shape, wide_shape, wide_shape],
        (queries, keys, values, dout, stats, near),
    )
    partner = lax.ppermute(own, "yh", other)
    prepared = call(
        prepare_kernel,
        [
            ((heads * GAP, LANES), BF16),
            block_shape,
            block_shape,
            ((heads, LANES, TOKENS_HERE + LANES), BF16),
            ((heads, 3, GAP, TOKENS_HERE), BF16),
            wide_shape,
            wide_shape,
        ],
        (keys, values, near, own, partner, local_key, local_value),
    )
    plane = lax.axis_index("yh").reshape(1)
    slots, prepared, local_query, plane = lax.optimization_barrier(
        (slots, prepared, local_query, plane)
    )
    rows, scores, grad_probs, wide_keys, chooser, local_key, local_value = prepared
    (merged,) = call(
        merge_kernel,
        [merged_shape],
        (slots,),
        scratch=[pltpu.VMEM((sources * SMALL, LANES), F32)],
    )
    merged = lax.all_to_all(merged, "yh", 0, 0, tiled=True)
    (slots,) = call(
        far_kernel,
        [slots_shape],
        (plane, merged),
        scalars=1,
        scratch=[pltpu.VMEM((3, PLANES * sources * 2, LANES), F32)],
    )
    slots = lax.all_to_all(slots, "xz", 0, 0, tiled=True)
    return tuple(
        call(
            final_kernel,
            [grad_shape, grad_shape, grad_shape, ((features, model), F32)],
            (
                rows,
                scores,
                grad_probs,
                wide_keys,
                chooser,
                local_query,
                local_key,
                local_value,
                slots,
            ),
        )
    )


def solution(mesh):
    devices = mesh.devices.reshape(-1, PLANES, 2, mesh.devices.shape[1] // 2)
    split_mesh = Mesh(devices, ("xz", "yh", "chip", "core"))
    parts = ("chip", "core")
    wide = P(parts, ("xz", "yh"))
    return jax.shard_map(
        local,
        mesh=split_mesh,
        in_specs=(wide, wide, wide, wide, P(parts, None), P(parts)),
        out_specs=(wide, wide, wide, P(parts, None)),
        check_vma=False,
    )
```

```python
import jax
import jax.numpy as jnp
from jax import lax
from jax.experimental import pallas as pl
from jax.experimental.pallas import tpu as pltpu
from jax.sharding import Mesh
from jax.sharding import PartitionSpec as P

HEAD_DIM = 64
TOKENS_HERE = 256
RB = 2
RC = 16
RE = 128
NEAR = TOKENS_HERE // RC
SCORE_SCALE = HEAD_DIM ** (-0.5)
WEIGHT_SCALE = 0.03125

PLANES = 4
LANES = 128
GAP = 16
SMALL = 8
CHUNK = 40
SLOT = CHUNK + SMALL
ABSENT = -1e30
LIMIT = 40 << 20

F32 = jnp.float32
BF16 = jnp.bfloat16


def mm(left, right, left_dim, right_dim):
    return lax.dot_general(
        left, right, (((left_dim,), (right_dim,)), ((), ())), preferred_element_type=F32
    )


def iota(shape, dim):
    return lax.broadcasted_iota(jnp.int32, shape, dim)


def one_hot(condition):
    return jnp.where(condition, 1.0, 0.0).astype(BF16)


def same_class(position, offset, stride):
    return (position & (stride - 1)) == (offset & (stride - 1))


def near_chooser(offset):
    shape = (NEAR, TOKENS_HERE)
    return one_hot(iota(shape, 1) == RC * iota(shape, 0) + (offset & (RC - 1)))


def far_chooser(offset, pair):
    shape = (GAP, TOKENS_HERE)
    row = iota(shape, 0)
    hit = iota(shape, 1) == RE * (row & 1) + offset
    return one_hot(hit & ((row >> 1) == pair))


def split3(value):
    high = value.astype(BF16).astype(F32)
    rest = value - high
    middle = rest.astype(BF16).astype(F32)
    return high, middle, rest - middle


def lay_stats(shape, dim, start, values):
    place = iota(shape, dim) - start
    out = jnp.zeros(shape, F32)
    for index, value in enumerate(values):
        for part_index, part in enumerate(split3(value)):
            out = jnp.where(place == 3 * index + part_index, part, out)
    return out


def take_stat(rows, start, index):
    place = iota(rows.shape, 1) - start - 3 * index
    return jnp.sum(jnp.where((place >= 0) & (place < 3), rows, 0.0), axis=1, keepdims=True)


def chunk_rows(folded, chunk):
    rows = folded[chunk * CHUNK : (chunk + 1) * CHUNK]
    short = CHUNK - rows.shape[0]
    if short:
        rows = jnp.concatenate([rows, jnp.zeros((short,) + rows.shape[1:], rows.dtype)], axis=0)
    return rows


def near_kernel(
    offset_hbm, key_hbm, value_hbm, near_ref, offset_ref, key_ref, value_ref, semaphores
):
    pairs = ((offset_hbm, offset_ref), (key_hbm, key_ref), (value_hbm, value_ref))
    copies = [
        pltpu.make_async_copy(source, target, semaphores.at[index])
        for index, (source, target) in enumerate(pairs)
    ]
    for copy in copies:
        copy.start()
    for copy in copies:
        copy.wait()
    for head in range(key_ref.shape[0] // HEAD_DIM):
        rows = slice(head * HEAD_DIM, (head + 1) * HEAD_DIM)
        both = jnp.concatenate([key_ref[rows], value_ref[rows]], axis=0)
        picked = mm(near_chooser(offset_ref[head]), both, 1, 1)
        near_ref[head * NEAR : (head + 1) * NEAR, :] = picked.astype(BF16)
    heads = near_ref.shape[0] // NEAR - 1
    row = iota((GAP, LANES), 0)
    told = jnp.zeros((GAP, LANES), F32)
    for head in range(heads):
        told = jnp.where(row == head, offset_ref[head].astype(F32), told)
    near_ref[heads * NEAR :] = told.astype(BF16)


def told_offset(near_ref, head):
    told = near_ref[near_ref.shape[0] - GAP :].astype(F32)
    return told[head : head + 1, :1].astype(jnp.int32)


def pair_count(key_pos, query_pos, offset):
    count = 1.0
    for stride in (RB, RC):
        keys = jnp.where(same_class(key_pos, offset, stride), 1.0, 0.0)
        count = count + keys * jnp.where(same_class(query_pos, offset, stride), 1.0, 0.0)
    return count


def local_kernel(
    side_ref,
    query_ref,
    key_ref,
    value_ref,
    grad_ref,
    weight_ref,
    near_ref,
    slots_ref,
    dout_ref,
    stats_ref,
):
    heads = query_ref.shape[0] // HEAD_DIM
    side = side_ref[0]
    blocks = [grad_ref[2 * core + (chip ^ side)] for chip in range(2) for core in range(2)]
    grad = jnp.concatenate(blocks, axis=0)
    half = grad.shape[0] // 2
    chunks = pl.cdiv(half, CHUNK)
    dout = mm(weight_ref[...], grad, 1, 0).astype(BF16)
    dout_ref[...] = dout
    offsets = [told_offset(near_ref, head) for head in range(heads)]
    choosers = [far_chooser(offsets[head], 3) for head in range(heads)]
    choosers = jnp.concatenate(choosers, axis=0)
    wide = grad.astype(F32)
    filler = jnp.zeros((LANES - 2 * CHUNK, TOKENS_HERE), F32)
    far_grads = []
    for chunk in range(chunks):
        both = [chunk_rows(wide[:half], chunk), chunk_rows(wide[half:], chunk), filler]
        far_grads.append(mm(choosers, jnp.concatenate(both, axis=0).astype(BF16), 1, 1))
    blank = jnp.zeros((HEAD_DIM, TOKENS_HERE), BF16)
    key_pos = iota((TOKENS_HERE, 1), 0)
    query_row = iota((1, TOKENS_HERE), 1)
    query_pos = query_row
    heads = range(heads)
    rows = [slice(head * HEAD_DIM, (head + 1) * HEAD_DIM) for head in heads]
    near = [near_ref[head * NEAR : (head + 1) * NEAR] for head in heads]
    in_near = [same_class(query_row, offset, RC) for offset in offsets]
    in_far = [same_class(query_row, offset, RE) for offset in offsets]
    scores = [mm(key_ref[rows[h]], query_ref[rows[h]], 0, 0) * SCORE_SCALE for h in heads]
    near_scores = [
        mm(near[h], jnp.concatenate([query_ref[rows[h]], blank], axis=0), 1, 0) * SCORE_SCALE
        for h in heads
    ]
    peak = [jnp.max(scores[h], axis=0, keepdims=True) for h in heads]
    near_max = [jnp.max(near_scores[h], axis=0, keepdims=True) for h in heads]
    peak = [jnp.where(in_near[h], jnp.maximum(peak[h], near_max[h]), peak[h]) for h in heads]
    mass = [
        pair_count(key_pos, query_pos, offsets[h]) * jnp.exp(scores[h] - peak[h]) for h in heads
    ]
    near_mass = [jnp.where(in_near[h], jnp.exp(near_scores[h] - peak[h]), 0.0) for h in heads]
    total = [
        jnp.sum(mass[h], axis=0, keepdims=True) + jnp.sum(near_mass[h], axis=0, keepdims=True)
        for h in heads
    ]
    log_mass = [peak[h] + jnp.log(total[h]) for h in heads]
    inverse = [1.0 / total[h] for h in heads]
    attended = [
        mm(value_ref[rows[h]], mass[h].astype(BF16), 1, 0)
        + mm(near[h], near_mass[h].astype(BF16), 0, 0)[HEAD_DIM:]
        for h in heads
    ]
    attended = [attended[h] * inverse[h] for h in heads]
    kept = [jnp.where(in_far[h], 0.0, attended[h]).astype(BF16) * WEIGHT_SCALE for h in heads]
    over = [jnp.concatenate([kept[h], blank], axis=0) for h in heads]
    under = [jnp.concatenate([blank, kept[h]], axis=0) for h in heads]
    weight_part = [
        mm(grad[:half], over[h], 1, 1) + mm(grad[half:], under[h], 1, 1)
        for h in heads
    ]
    delta = [
        jnp.sum(dout[rows[h]].astype(F32) * attended[h], axis=0, keepdims=True) for h in heads
    ]
    place = iota((SMALL, TOKENS_HERE), 0)
    for h in heads:
        query_dout = jnp.concatenate([query_ref[rows[h]], dout[rows[h]]], axis=0)
        key_value = jnp.concatenate([key_ref[rows[h]], value_ref[rows[h]]], axis=0)
        stats = lay_stats((HEAD_DIM, TOKENS_HERE), 0, 0, (log_mass[h], delta[h]))
        stats_attended = jnp.concatenate([stats.astype(BF16), attended[h].astype(BF16)], axis=0)
        mine = mm(far_chooser(offsets[h], 0), query_dout, 1, 1)
        mine = mine + mm(far_chooser(offsets[h], 1), key_value, 1, 1)
        mine = mine + mm(far_chooser(offsets[h], 2), stats_attended, 1, 1)
        stats_ref[h * SMALL : (h + 1) * SMALL] = jnp.where(place == 0, log_mass[h], delta[h])
        for chunk in range(chunks):
            far_grad = far_grads[chunk][h * GAP : h * GAP + SMALL]
            parts = [chunk_rows(weight_part[h], chunk), mine[:SMALL] + far_grad]
            slots_ref[h * chunks + chunk] = jnp.concatenate(parts, axis=0).astype(BF16)
    heads = len(heads)
    rest = slots_ref.shape[0] - heads * chunks
    slots_ref[heads * chunks :] = jnp.zeros((rest,) + slots_ref.shape[1:], BF16)


def local_grad_kernel(
    query_ref,
    key_ref,
    value_ref,
    dout_ref,
    stats_ref,
    near_ref,
    back_ref,
    grad_query_ref,
    grad_key_ref,
    grad_value_ref,
):
    heads = query_ref.shape[0] // HEAD_DIM
    blank = jnp.zeros((HEAD_DIM, TOKENS_HERE), BF16)
    key_pos = iota((TOKENS_HERE, 1), 0)
    query_row = iota((1, TOKENS_HERE), 1)
    query_pos = query_row
    far_rows = jnp.zeros((GAP, LANES), F32)
    for head in range(heads):
        offset = told_offset(near_ref, head)
        rows = slice(head * HEAD_DIM, (head + 1) * HEAD_DIM)
        near_rows = slice(head * NEAR, (head + 1) * NEAR)
        query, key, value = query_ref[rows], key_ref[rows], value_ref[rows]
        near = near_ref[near_rows]
        dout_head = dout_ref[rows]
        log_mass = stats_ref[head * SMALL : head * SMALL + 1]
        delta = stats_ref[head * SMALL + 1 : head * SMALL + 2]
        query_over = jnp.concatenate([query, blank], axis=0)
        dout_under = jnp.concatenate([blank, dout_head], axis=0)
        in_near = same_class(query_row, offset, RC)
        in_far = same_class(query_row, offset, RE)
        near_only = in_near & jnp.logical_not(in_far)

        scores = mm(key, query, 0, 0) * SCORE_SCALE
        near_scores = mm(near, query_over, 1, 0) * SCORE_SCALE
        probs = pair_count(key_pos, query_pos, offset) * jnp.exp(scores - log_mass)
        probs = jnp.where(in_far, 0.0, probs)
        near_probs = jnp.where(near_only, jnp.exp(near_scores - log_mass), 0.0)
        grad_scores = (probs * (mm(value, dout_head, 0, 0) - delta)).astype(BF16)
        near_grad_scores = (near_probs * (mm(near, dout_under, 1, 0) - delta)).astype(BF16)
        grad_query_ref[rows] = (
            mm(key, grad_scores, 1, 0) + mm(near, near_grad_scores, 0, 0)[:HEAD_DIM]
        )
        grad_key_ref[rows] = mm(query, grad_scores, 1, 1)
        grad_value_ref[rows] = mm(dout_head, probs.astype(BF16), 1, 1)
        back = mm(near_grad_scores, query_over, 1, 1)
        back = back + mm(near_probs.astype(BF16), dout_under, 1, 1)
        back_ref[near_rows] = back.astype(BF16)
        query_dout = jnp.concatenate([query, dout_head], axis=0)
        far_rows = far_rows + mm(far_chooser(offset, head), query_dout, 1, 1)
    back_ref[heads * NEAR :] = far_rows.astype(BF16)


def merge_kernel(slots_ref, merged_ref, far_ref):
    sources = slots_ref.shape[0]
    total = jnp.zeros((SLOT, LANES), F32)
    for source in range(sources):
        block = slots_ref[source].astype(F32)
        total = total + block
        far_ref[source * SMALL : (source + 1) * SMALL] = block[CHUNK:]
    pieces = [far_ref[pl.ds(kind, sources, stride=SMALL), :] for kind in range(SMALL)]
    full = jnp.concatenate([total] + pieces, axis=0).astype(BF16)
    for plane in range(PLANES):
        merged_ref[plane] = full


def far_kernel(plane_ref, merged_ref, slots_ref, returned_ref):
    sources = slots_ref.shape[0]
    width = 2 * sources
    count = PLANES * width

    def kind(index):
        start = SLOT + index * width
        return merged_ref[:, start : start + width, :].reshape(count, LANES)

    query_dout, key_value, stats_attended, far_grad = (kind(index) for index in range(4))
    left = iota((count, LANES), 1) < HEAD_DIM
    shape = (LANES, LANES)
    swap = one_hot(iota(shape, 0) == (iota(shape, 1) ^ HEAD_DIM))
    value_key = mm(key_value, swap, 1, 0).astype(BF16)
    stats = stats_attended.astype(F32)
    attended_stats = mm(stats_attended, swap, 1, 0)
    wide = query_dout.astype(F32)
    query = jnp.where(left, wide, 0.0).astype(BF16)
    dout_wide = jnp.where(left, 0.0, wide)
    local_mass = take_stat(stats, 0, 0)

    scores = mm(query, key_value, 1, 1) * SCORE_SCALE
    grad_probs = mm(dout_wide.astype(BF16), key_value, 1, 1)
    peak = jnp.maximum(jnp.max(scores, axis=1, keepdims=True), local_mass)
    mass = jnp.exp(scores - peak)
    local_part = jnp.exp(local_mass - peak)
    total = jnp.sum(mass, axis=1, keepdims=True) + local_part
    normalizer = peak + jnp.log(total)
    inverse = 1.0 / total
    local_part = local_part * inverse
    probs = mass * inverse
    probs_low = probs.astype(BF16)
    mass_low = mass.astype(BF16)
    under = local_part * stats + mm(mass_low, key_value, 1, 0) * inverse
    delta = jnp.sum(dout_wide * under, axis=1, keepdims=True)
    over = local_part * attended_stats + mm(mass_low, value_key, 1, 0) * inverse
    over = jnp.where(left, over, 0.0).astype(BF16)
    under = jnp.where(left, 0.0, under).astype(BF16)
    grad_scores = (probs * (grad_probs - delta)).astype(BF16)

    def other_plane(column):
        blocks = [column[(p ^ 1) * width : ((p ^ 1) + 1) * width] for p in range(PLANES)]
        return jnp.concatenate(blocks, axis=0)

    weight_part = mm(far_grad, over, 0, 0)[:CHUNK] + mm(far_grad, under, 0, 0)[CHUNK : 2 * CHUNK]
    weight_part = weight_part * WEIGHT_SCALE
    for plane in range(PLANES):
        weight_part = weight_part + merged_ref[plane, :SLOT].astype(F32)[:CHUNK]
    own_stats = lay_stats((count, LANES), 1, HEAD_DIM, (normalizer, delta))
    other_stats = lay_stats((count, LANES), 1, 0, (other_plane(normalizer), other_plane(delta)))
    returned_ref[0] = jnp.where(left, other_stats, mm(probs_low, query_dout, 0, 0))
    returned_ref[1] = jnp.where(left, mm(grad_scores, key_value, 1, 0), own_stats)
    returned_ref[2] = jnp.where(left, mm(grad_scores, query_dout, 0, 0), 0.0)
    own = pl.ds(pl.multiple_of(plane_ref[0] * width, width), width)
    shape = (sources * SMALL, width)
    row, column = iota(shape, 0), iota(shape, 1)
    same = (row // SMALL) == (column % sources)
    slot_row, pair = row % SMALL, column // sources
    placed = jnp.zeros((sources * SMALL, LANES), F32)
    for index in range(returned_ref.shape[0]):
        chosen = one_hot(same & (slot_row == pair + 2 * index))
        placed = placed + mm(chosen, returned_ref[index, own, :].astype(BF16), 1, 0)
    for source in range(sources):
        parts = [weight_part, placed[source * SMALL : (source + 1) * SMALL]]
        slots_ref[source] = jnp.concatenate(parts, axis=0).astype(BF16)


def prepare_kernel(
    key_ref,
    value_ref,
    near_ref,
    own_ref,
    partner_ref,
    local_key_ref,
    local_value_ref,
    rows_ref,
    scores_ref,
    grad_probs_ref,
    keys_ref,
    chooser_ref,
    grad_key_ref,
    grad_value_ref,
):
    heads = key_ref.shape[0] // HEAD_DIM
    first_far = heads * NEAR
    blank = jnp.zeros((HEAD_DIM, TOKENS_HERE + LANES), BF16)
    shape = (GAP, GAP)
    row, column = iota(shape, 0), iota(shape, 1)
    widen = one_hot(iota((NEAR, LANES), 0) == iota((NEAR, LANES), 1))
    shape = (GAP, TOKENS_HERE + LANES)
    block_row, place = iota(shape, 0), iota(shape, 1)
    here = place < TOKENS_HERE
    from_partner, from_here = block_row < 2, (block_row >= 2) & (block_row < 4)
    for head in range(heads):
        offset = told_offset(near_ref, head)
        rows = slice(head * HEAD_DIM, (head + 1) * HEAD_DIM)
        block = slice(head * GAP, (head + 1) * GAP)
        key, value = key_ref[rows], value_ref[rows]
        near = mm(near_ref[block], widen, 0, 0).astype(BF16)
        keys = jnp.concatenate([key, near[:HEAD_DIM]], axis=1)
        values = jnp.concatenate([value, near[HEAD_DIM:]], axis=1)
        keys = jnp.concatenate([keys, blank], axis=0)
        values = jnp.concatenate([blank, values], axis=0)
        from_partner_far = one_hot((row < 2) & (column == row + 2 * head))
        from_own_far = one_hot((row >= 2) & (row < 4) & (column == row - 2 + 2 * head))
        chosen = mm(from_partner_far, partner_ref[first_far:], 1, 0)
        chosen = (chosen + mm(from_own_far, own_ref[first_far:], 1, 0)).astype(BF16)
        in_near = here & same_class(place, offset, RC)
        extra = jnp.where(here & same_class(place, offset, RB), 1.0, 0.0)
        extra = extra + jnp.where(in_near, 1.0, 0.0)
        mask_here = jnp.where(place < TOKENS_HERE + NEAR, jnp.log(1.0 + extra), ABSENT)
        mask = jnp.where(from_here, mask_here, ABSENT)
        mask = jnp.where(from_partner & in_near, 0.0, mask)
        rows_ref[block] = chosen
        scores_ref[block] = mm(chosen, keys, 1, 0) * SCORE_SCALE + mask
        grad_probs_ref[block] = mm(chosen, values, 1, 0)
        keys_ref[head] = keys
        for pair in range(3):
            chooser_ref[head, pair] = far_chooser(offset, pair)
        spread = mm(partner_ref[block], near_chooser(offset), 0, 0)
        grad_key_ref[rows] = local_key_ref[rows] + spread[:HEAD_DIM]
        grad_value_ref[rows] = local_value_ref[rows] + spread[HEAD_DIM:]


def final_kernel(
    rows_ref,
    scores_ref,
    grad_probs_ref,
    keys_ref,
    chooser_ref,
    local_query_ref,
    local_key_ref,
    local_value_ref,
    slots_ref,
    grad_query_ref,
    grad_key_ref,
    grad_value_ref,
    grad_weight_ref,
):
    heads = local_query_ref.shape[0] // HEAD_DIM
    half = grad_weight_ref.shape[1] // 2
    chunks = pl.cdiv(half, CHUNK)
    eye = one_hot(iota((LANES, LANES), 0) == iota((LANES, LANES), 1))
    for head in range(heads):
        rows = slice(head * HEAD_DIM, (head + 1) * HEAD_DIM)
        block = slice(head * GAP, (head + 1) * GAP)
        pieces = [slots_ref[head * chunks + chunk].astype(F32) for chunk in range(chunks)]
        folded = jnp.concatenate([piece[:CHUNK] for piece in pieces], axis=0)[:half]
        unfolded = mm(eye, folded.astype(BF16), 1, 1)
        grad_weight_ref[rows, :half] = unfolded[:HEAD_DIM]
        grad_weight_ref[rows, half:] = unfolded[HEAD_DIM:]

        returned = jnp.concatenate(
            [pieces[0][CHUNK:], jnp.zeros((GAP - SMALL, LANES), F32)], axis=0
        )
        chosen = rows_ref[block]
        start = jnp.where(iota(returned.shape, 0) < 2, 0, HEAD_DIM)
        normalizer, delta = (take_stat(returned, start, index) for index in range(2))
        probs = jnp.exp(scores_ref[block] - normalizer)
        grad_scores = (probs * (grad_probs_ref[block] - delta)).astype(BF16)
        probs_low = probs[:, :TOKENS_HERE].astype(BF16)
        far_query = (returned + mm(grad_scores, keys_ref[head], 1, 1)).astype(BF16)
        returned = returned.astype(BF16)
        grad_query = mm(far_query, chooser_ref[head, 1], 0, 0)[:HEAD_DIM]
        grad_key = mm(returned, chooser_ref[head, 2], 0, 0)[:HEAD_DIM]
        grad_key = grad_key + mm(chosen, grad_scores[:, :TOKENS_HERE], 0, 0)[:HEAD_DIM]
        grad_value = mm(returned, chooser_ref[head, 0], 0, 0)[HEAD_DIM:]
        grad_value = grad_value + mm(chosen, probs_low, 0, 0)[HEAD_DIM:]
        grad_query = (local_query_ref[rows] + grad_query) * SCORE_SCALE
        grad_key = (local_key_ref[rows] + grad_key) * SCORE_SCALE
        grad_query_ref[rows] = grad_query.astype(BF16)
        grad_key_ref[rows] = grad_key.astype(BF16)
        grad_value_ref[rows] = (local_value_ref[rows] + grad_value).astype(BF16)


def call(kernel, outs, arrays, scalars=0, scratch=(), space=pltpu.VMEM, limit=40 << 20):
    specs = [pl.BlockSpec(memory_space=pltpu.SMEM)] * scalars
    specs = specs + [pl.BlockSpec(memory_space=space)] * (len(arrays) - scalars)
    shapes = [jax.ShapeDtypeStruct(shape, dtype) for shape, dtype in outs]
    return pl.pallas_call(
        kernel,
        out_shape=shapes,
        in_specs=specs,
        out_specs=[pl.BlockSpec(memory_space=pltpu.VMEM)] * len(shapes),
        scratch_shapes=list(scratch),
        compiler_params=pltpu.CompilerParams(vmem_limit_bytes=limit),
        name=kernel.__name__,
    )(*arrays)


def local(queries, keys, values, grad_out, out_weight, offsets):
    features = queries.shape[0]
    model = out_weight.shape[1]
    heads = offsets.shape[0]
    sources = lax.axis_size("xz")
    near_shape = ((heads * NEAR + GAP, LANES), BF16)
    back_shape = ((heads * NEAR + GAP, LANES), BF16)
    slots_shape = ((sources, SLOT, LANES), BF16)
    merged_shape = ((PLANES, SLOT + sources * SMALL, LANES), BF16)
    wide_shape = ((features, TOKENS_HERE), F32)
    grad_shape = ((features, TOKENS_HERE), BF16)
    block_shape = ((heads * GAP, TOKENS_HERE + LANES), F32)
    other = [(i, i ^ 1) for i in range(PLANES)]

    scratch = [
        pltpu.SMEM(offsets.shape, offsets.dtype),
        pltpu.VMEM(keys.shape, keys.dtype),
        pltpu.VMEM(values.shape, values.dtype),
        pltpu.SemaphoreType.DMA((3,)),
    ]
    other_grad = lax.ppermute(grad_out, "chip", [(0, 1), (1, 0)])
    (near,) = call(
        near_kernel,
        [near_shape],
        tuple(pltpu.with_memory_space_constraint(x, pltpu.HBM) for x in (offsets, keys, values)),
        scratch=scratch,
        space=pltpu.HBM,
        limit=LIMIT,
    )
    near = lax.ppermute(near, "yh", other)
    pair_grads = lax.all_gather(jnp.stack([grad_out, other_grad]), "core", axis=0, tiled=True)
    side = lax.axis_index("chip").reshape(1)
    slots, dout, stats = call(
        local_kernel,
        [slots_shape, grad_shape, ((heads * SMALL, TOKENS_HERE), F32)],
        (side, queries, keys, values, pair_grads, out_weight, near),
        scalars=1,
    )
    slots = lax.all_to_all(slots, "xz", 0, 0, tiled=True)
    own, local_query, local_key, local_value = call(
        local_grad_kernel,
        [back_shape, wide_shape, wide_shape, wide_shape],
        (queries, keys, values, dout, stats, near),
    )
    partner = lax.ppermute(own, "yh", other)
    prepared = call(
        prepare_kernel,
        [
            ((heads * GAP, LANES), BF16),
            block_shape,
            block_shape,
            ((heads, LANES, TOKENS_HERE + LANES), BF16),
            ((heads, 3, GAP, TOKENS_HERE), BF16),
            wide_shape,
            wide_shape,
        ],
        (keys, values, near, own, partner, local_key, local_value),
    )
    plane = lax.axis_index("yh").reshape(1)
    slots, prepared, local_query, plane = lax.optimization_barrier(
        (slots, prepared, local_query, plane)
    )
    rows, scores, grad_probs, wide_keys, chooser, local_key, local_value = prepared
    (merged,) = call(
        merge_kernel,
        [merged_shape],
        (slots,),
        scratch=[pltpu.VMEM((sources * SMALL, LANES), F32)],
    )
    merged = lax.all_to_all(merged, "yh", 0, 0, tiled=True)
    (slots,) = call(
        far_kernel,
        [slots_shape],
        (plane, merged),
        scalars=1,
        scratch=[pltpu.VMEM((3, PLANES * sources * 2, LANES), F32)],
    )
    slots = lax.all_to_all(slots, "xz", 0, 0, tiled=True)
    return tuple(
        call(
            final_kernel,
            [grad_shape, grad_shape, grad_shape, ((features, model), F32)],
            (
                rows,
                scores,
                grad_probs,
                wide_keys,
                chooser,
                local_query,
                local_key,
                local_value,
                slots,
            ),
        )
    )


def solution(mesh):
    devices = mesh.devices.reshape(-1, PLANES, 2, mesh.devices.shape[1] // 2)
    split_mesh = Mesh(devices, ("xz", "yh", "chip", "core"))
    parts = ("chip", "core")
    wide = P(parts, ("xz", "yh"))
    return jax.shard_map(
        local,
        mesh=split_mesh,
        in_specs=(wide, wide, wide, wide, P(parts, None), P(parts)),
        out_specs=(wide, wide, wide, P(parts, None)),
        check_vma=False,
    )
```

```python
import jax
import jax.numpy as jnp
from jax import lax
from jax.experimental import pallas as pl
from jax.experimental.pallas import tpu as pltpu
from jax.sharding import Mesh
from jax.sharding import PartitionSpec as P

HEAD_DIM = 64
TOKENS_HERE = 256
RB = 2
RC = 16
RE = 128
NEAR = TOKENS_HERE // RC
SCORE_SCALE = HEAD_DIM ** (-0.5)
WEIGHT_SCALE = 0.03125

PLANES = 4
LANES = 128
GAP = 16
SMALL = 8
CHUNK = 40
SLOT = CHUNK + SMALL
ABSENT = -1e30
LIMIT = 40 << 20

F32 = jnp.float32
BF16 = jnp.bfloat16


def mm(left, right, left_dim, right_dim):
    return lax.dot_general(
        left, right, (((left_dim,), (right_dim,)), ((), ())), preferred_element_type=F32
    )


def iota(shape, dim):
    return lax.broadcasted_iota(jnp.int32, shape, dim)


def one_hot(condition):
    return jnp.where(condition, 1.0, 0.0).astype(BF16)


def same_class(position, offset, stride):
    return (position & (stride - 1)) == (offset & (stride - 1))


def near_chooser(offset):
    shape = (NEAR, TOKENS_HERE)
    return one_hot(iota(shape, 1) == RC * iota(shape, 0) + (offset & (RC - 1)))


def far_chooser(offset, pair):
    shape = (GAP, TOKENS_HERE)
    row = iota(shape, 0)
    hit = iota(shape, 1) == RE * (row & 1) + offset
    return one_hot(hit & ((row >> 1) == pair))


def split3(value):
    high = value.astype(BF16).astype(F32)
    rest = value - high
    middle = rest.astype(BF16).astype(F32)
    return high, middle, rest - middle


def lay_stats(shape, dim, start, values):
    place = iota(shape, dim) - start
    out = jnp.zeros(shape, F32)
    for index, value in enumerate(values):
        for part_index, part in enumerate(split3(value)):
            out = jnp.where(place == 3 * index + part_index, part, out)
    return out


def take_stat(rows, start, index):
    place = iota(rows.shape, 1) - start - 3 * index
    return jnp.sum(jnp.where((place >= 0) & (place < 3), rows, 0.0), axis=1, keepdims=True)


def chunk_rows(folded, chunk):
    rows = folded[chunk * CHUNK : (chunk + 1) * CHUNK]
    short = CHUNK - rows.shape[0]
    if short:
        rows = jnp.concatenate([rows, jnp.zeros((short,) + rows.shape[1:], rows.dtype)], axis=0)
    return rows


def near_kernel(
    offset_hbm, key_hbm, value_hbm, near_ref, offset_ref, key_ref, value_ref, semaphores
):
    pairs = ((offset_hbm, offset_ref), (key_hbm, key_ref), (value_hbm, value_ref))
    copies = [
        pltpu.make_async_copy(source, target, semaphores.at[index])
        for index, (source, target) in enumerate(pairs)
    ]
    for copy in copies:
        copy.start()
    for copy in copies:
        copy.wait()
    for head in range(key_ref.shape[0] // HEAD_DIM):
        rows = slice(head * HEAD_DIM, (head + 1) * HEAD_DIM)
        both = jnp.concatenate([key_ref[rows], value_ref[rows]], axis=0)
        picked = mm(near_chooser(offset_ref[head]), both, 1, 1)
        near_ref[head * NEAR : (head + 1) * NEAR, :] = picked.astype(BF16)
    heads = near_ref.shape[0] // NEAR - 1
    row = iota((GAP, LANES), 0)
    told = jnp.zeros((GAP, LANES), F32)
    for head in range(heads):
        told = jnp.where(row == head, offset_ref[head].astype(F32), told)
    near_ref[heads * NEAR :] = told.astype(BF16)


def told_offset(near_ref, head):
    told = near_ref[near_ref.shape[0] - GAP :].astype(F32)
    return told[head : head + 1, :1].astype(jnp.int32)


def pair_count(key_pos, query_pos, offset):
    count = 1.0
    for stride in (RB, RC):
        keys = jnp.where(same_class(key_pos, offset, stride), 1.0, 0.0)
        count = count + keys * jnp.where(same_class(query_pos, offset, stride), 1.0, 0.0)
    return count


def local_kernel(
    side_ref,
    query_ref,
    key_ref,
    value_ref,
    grad_ref,
    weight_ref,
    near_ref,
    slots_ref,
    dout_ref,
    stats_ref,
):
    heads = query_ref.shape[0] // HEAD_DIM
    side = side_ref[0]
    blocks = [grad_ref[2 * core + (chip ^ side)] for chip in range(2) for core in range(2)]
    grad = jnp.concatenate(blocks, axis=0)
    half = grad.shape[0] // 2
    chunks = pl.cdiv(half, CHUNK)
    dout = mm(weight_ref[...], grad, 1, 0).astype(BF16)
    dout_ref[...] = dout
    offsets = [told_offset(near_ref, head) for head in range(heads)]
    choosers = [far_chooser(offsets[head], 3) for head in range(heads)]
    choosers = jnp.concatenate(choosers, axis=0)
    wide = grad.astype(F32)
    filler = jnp.zeros((LANES - 2 * CHUNK, TOKENS_HERE), F32)
    far_grads = []
    for chunk in range(chunks):
        both = [chunk_rows(wide[:half], chunk), chunk_rows(wide[half:], chunk), filler]
        far_grads.append(mm(choosers, jnp.concatenate(both, axis=0).astype(BF16), 1, 1))
    blank = jnp.zeros((HEAD_DIM, TOKENS_HERE), BF16)
    key_pos = iota((TOKENS_HERE, 1), 0)
    query_row = iota((1, TOKENS_HERE), 1)
    query_pos = query_row
    heads = range(heads)
    rows = [slice(head * HEAD_DIM, (head + 1) * HEAD_DIM) for head in heads]
    near = [near_ref[head * NEAR : (head + 1) * NEAR] for head in heads]
    in_near = [same_class(query_row, offset, RC) for offset in offsets]
    in_far = [same_class(query_row, offset, RE) for offset in offsets]
    scaled = [query_ref[rows[h]] * SCORE_SCALE for h in heads]
    scores = [mm(key_ref[rows[h]], scaled[h], 0, 0) for h in heads]
    near_scores = [
        mm(near[h], jnp.concatenate([scaled[h], blank], axis=0), 1, 0) for h in heads
    ]
    peak = [jnp.max(scores[h], axis=0, keepdims=True) for h in heads]
    near_max = [jnp.max(near_scores[h], axis=0, keepdims=True) for h in heads]
    peak = [jnp.where(in_near[h], jnp.maximum(peak[h], near_max[h]), peak[h]) for h in heads]
    mass = [
        pair_count(key_pos, query_pos, offsets[h]) * jnp.exp(scores[h] - peak[h]) for h in heads
    ]
    near_mass = [jnp.where(in_near[h], jnp.exp(near_scores[h] - peak[h]), 0.0) for h in heads]
    total = [
        jnp.sum(mass[h], axis=0, keepdims=True) + jnp.sum(near_mass[h], axis=0, keepdims=True)
        for h in heads
    ]
    log_mass = [peak[h] + jnp.log(total[h]) for h in heads]
    inverse = [1.0 / total[h] for h in heads]
    attended = [
        mm(value_ref[rows[h]], mass[h].astype(BF16), 1, 0)
        + mm(near[h], near_mass[h].astype(BF16), 0, 0)[HEAD_DIM:]
        for h in heads
    ]
    attended = [attended[h] * inverse[h] for h in heads]
    kept = [jnp.where(in_far[h], 0.0, attended[h]).astype(BF16) * WEIGHT_SCALE for h in heads]
    over = [jnp.concatenate([kept[h], blank], axis=0) for h in heads]
    under = [jnp.concatenate([blank, kept[h]], axis=0) for h in heads]
    weight_part = [
        mm(grad[:half], over[h], 1, 1) + mm(grad[half:], under[h], 1, 1)
        for h in heads
    ]
    delta = [
        jnp.sum(dout[rows[h]].astype(F32) * attended[h], axis=0, keepdims=True) for h in heads
    ]
    place = iota((SMALL, TOKENS_HERE), 0)
    for h in heads:
        query_dout = jnp.concatenate([query_ref[rows[h]], dout[rows[h]]], axis=0)
        key_value = jnp.concatenate([key_ref[rows[h]], value_ref[rows[h]]], axis=0)
        stats = lay_stats((HEAD_DIM, TOKENS_HERE), 0, 0, (log_mass[h], delta[h]))
        stats_attended = jnp.concatenate([stats.astype(BF16), attended[h].astype(BF16)], axis=0)
        mine = mm(far_chooser(offsets[h], 0), query_dout, 1, 1)
        mine = mine + mm(far_chooser(offsets[h], 1), key_value, 1, 1)
        mine = mine + mm(far_chooser(offsets[h], 2), stats_attended, 1, 1)
        stats_ref[h * SMALL : (h + 1) * SMALL] = jnp.where(place == 0, log_mass[h], delta[h])
        for chunk in range(chunks):
            far_grad = far_grads[chunk][h * GAP : h * GAP + SMALL]
            parts = [chunk_rows(weight_part[h], chunk), mine[:SMALL] + far_grad]
            slots_ref[h * chunks + chunk] = jnp.concatenate(parts, axis=0).astype(BF16)
    heads = len(heads)
    rest = slots_ref.shape[0] - heads * chunks
    slots_ref[heads * chunks :] = jnp.zeros((rest,) + slots_ref.shape[1:], BF16)


def local_grad_kernel(
    query_ref,
    key_ref,
    value_ref,
    dout_ref,
    stats_ref,
    near_ref,
    back_ref,
    grad_query_ref,
    grad_key_ref,
    grad_value_ref,
):
    heads = query_ref.shape[0] // HEAD_DIM
    blank = jnp.zeros((HEAD_DIM, TOKENS_HERE), BF16)
    key_pos = iota((TOKENS_HERE, 1), 0)
    query_row = iota((1, TOKENS_HERE), 1)
    query_pos = query_row
    far_rows = jnp.zeros((GAP, LANES), F32)
    for head in range(heads):
        offset = told_offset(near_ref, head)
        rows = slice(head * HEAD_DIM, (head + 1) * HEAD_DIM)
        near_rows = slice(head * NEAR, (head + 1) * NEAR)
        query, key, value = query_ref[rows], key_ref[rows], value_ref[rows]
        near = near_ref[near_rows]
        dout_head = dout_ref[rows]
        log_mass = stats_ref[head * SMALL : head * SMALL + 1]
        delta = stats_ref[head * SMALL + 1 : head * SMALL + 2]
        query_over = jnp.concatenate([query, blank], axis=0)
        dout_under = jnp.concatenate([blank, dout_head], axis=0)
        in_near = same_class(query_row, offset, RC)
        in_far = same_class(query_row, offset, RE)
        near_only = in_near & jnp.logical_not(in_far)

        scores = mm(key, query, 0, 0) * SCORE_SCALE
        near_scores = mm(near, query_over, 1, 0) * SCORE_SCALE
        probs = pair_count(key_pos, query_pos, offset) * jnp.exp(scores - log_mass)
        probs = jnp.where(in_far, 0.0, probs)
        near_probs = jnp.where(near_only, jnp.exp(near_scores - log_mass), 0.0)
        grad_scores = (probs * (mm(value, dout_head, 0, 0) - delta)).astype(BF16)
        near_grad_scores = (near_probs * (mm(near, dout_under, 1, 0) - delta)).astype(BF16)
        grad_query_ref[rows] = (
            mm(key, grad_scores, 1, 0) + mm(near, near_grad_scores, 0, 0)[:HEAD_DIM]
        )
        grad_key_ref[rows] = mm(query, grad_scores, 1, 1)
        grad_value_ref[rows] = mm(dout_head, probs.astype(BF16), 1, 1)
        back = mm(near_grad_scores, query_over, 1, 1)
        back = back + mm(near_probs.astype(BF16), dout_under, 1, 1)
        back_ref[near_rows] = back.astype(BF16)
        query_dout = jnp.concatenate([query, dout_head], axis=0)
        far_rows = far_rows + mm(far_chooser(offset, head), query_dout, 1, 1)
    back_ref[heads * NEAR :] = far_rows.astype(BF16)


def merge_kernel(slots_ref, merged_ref, far_ref):
    sources = slots_ref.shape[0]
    total = jnp.zeros((SLOT, LANES), F32)
    for source in range(sources):
        block = slots_ref[source].astype(F32)
        total = total + block
        far_ref[source * SMALL : (source + 1) * SMALL] = block[CHUNK:]
    pieces = [far_ref[pl.ds(kind, sources, stride=SMALL), :] for kind in range(SMALL)]
    full = jnp.concatenate([total] + pieces, axis=0).astype(BF16)
    for plane in range(PLANES):
        merged_ref[plane] = full


def far_kernel(plane_ref, merged_ref, slots_ref, returned_ref):
    sources = slots_ref.shape[0]
    width = 2 * sources
    count = PLANES * width

    def kind(index):
        start = SLOT + index * width
        return merged_ref[:, start : start + width, :].reshape(count, LANES)

    query_dout, key_value, stats_attended, far_grad = (kind(index) for index in range(4))
    left = iota((count, LANES), 1) < HEAD_DIM
    shape = (LANES, LANES)
    swap = one_hot(iota(shape, 0) == (iota(shape, 1) ^ HEAD_DIM))
    value_key = mm(key_value, swap, 1, 0).astype(BF16)
    stats = stats_attended.astype(F32)
    attended_stats = mm(stats_attended, swap, 1, 0)
    wide = query_dout.astype(F32)
    query = jnp.where(left, wide * SCORE_SCALE, 0.0).astype(BF16)
    dout_wide = jnp.where(left, 0.0, wide)
    local_mass = take_stat(stats, 0, 0)

    scores = mm(query, key_value, 1, 1)
    grad_probs = mm(dout_wide.astype(BF16), key_value, 1, 1)
    peak = jnp.maximum(jnp.max(scores, axis=1, keepdims=True), local_mass)
    mass = jnp.exp(scores - peak)
    local_part = jnp.exp(local_mass - peak)
    total = jnp.sum(mass, axis=1, keepdims=True) + local_part
    normalizer = peak + jnp.log(total)
    inverse = 1.0 / total
    local_part = local_part * inverse
    probs = mass * inverse
    probs_low = probs.astype(BF16)
    mass_low = mass.astype(BF16)
    under = local_part * stats + mm(mass_low, key_value, 1, 0) * inverse
    delta = jnp.sum(dout_wide * under, axis=1, keepdims=True)
    over = local_part * attended_stats + mm(mass_low, value_key, 1, 0) * inverse
    over = jnp.where(left, over, 0.0).astype(BF16)
    under = jnp.where(left, 0.0, under).astype(BF16)
    grad_scores = (probs * (grad_probs - delta)).astype(BF16)

    def other_plane(column):
        blocks = [column[(p ^ 1) * width : ((p ^ 1) + 1) * width] for p in range(PLANES)]
        return jnp.concatenate(blocks, axis=0)

    weight_part = mm(far_grad, over, 0, 0)[:CHUNK] + mm(far_grad, under, 0, 0)[CHUNK : 2 * CHUNK]
    weight_part = weight_part * WEIGHT_SCALE
    for plane in range(PLANES):
        weight_part = weight_part + merged_ref[plane, :SLOT].astype(F32)[:CHUNK]
    own_stats = lay_stats((count, LANES), 1, HEAD_DIM, (normalizer, delta))
    other_stats = lay_stats((count, LANES), 1, 0, (other_plane(normalizer), other_plane(delta)))
    returned_ref[0] = jnp.where(left, other_stats, mm(probs_low, query_dout, 0, 0))
    returned_ref[1] = jnp.where(left, mm(grad_scores, key_value, 1, 0), own_stats)
    returned_ref[2] = jnp.where(left, mm(grad_scores, query_dout, 0, 0), 0.0)
    own = pl.ds(pl.multiple_of(plane_ref[0] * width, width), width)
    shape = (sources * SMALL, width)
    row, column = iota(shape, 0), iota(shape, 1)
    same = (row // SMALL) == (column % sources)
    slot_row, pair = row % SMALL, column // sources
    placed = jnp.zeros((sources * SMALL, LANES), F32)
    for index in range(returned_ref.shape[0]):
        chosen = one_hot(same & (slot_row == pair + 2 * index))
        placed = placed + mm(chosen, returned_ref[index, own, :].astype(BF16), 1, 0)
    for source in range(sources):
        parts = [weight_part, placed[source * SMALL : (source + 1) * SMALL]]
        slots_ref[source] = jnp.concatenate(parts, axis=0).astype(BF16)


def prepare_kernel(
    key_ref,
    value_ref,
    near_ref,
    own_ref,
    partner_ref,
    local_key_ref,
    local_value_ref,
    rows_ref,
    scores_ref,
    grad_probs_ref,
    keys_ref,
    chooser_ref,
    grad_key_ref,
    grad_value_ref,
):
    heads = key_ref.shape[0] // HEAD_DIM
    first_far = heads * NEAR
    blank = jnp.zeros((HEAD_DIM, TOKENS_HERE + LANES), BF16)
    shape = (GAP, GAP)
    row, column = iota(shape, 0), iota(shape, 1)
    widen = one_hot(iota((NEAR, LANES), 0) == iota((NEAR, LANES), 1))
    shape = (GAP, TOKENS_HERE + LANES)
    block_row, place = iota(shape, 0), iota(shape, 1)
    here = place < TOKENS_HERE
    from_partner, from_here = block_row < 2, (block_row >= 2) & (block_row < 4)
    for head in range(heads):
        offset = told_offset(near_ref, head)
        rows = slice(head * HEAD_DIM, (head + 1) * HEAD_DIM)
        block = slice(head * GAP, (head + 1) * GAP)
        key, value = key_ref[rows], value_ref[rows]
        near = mm(near_ref[block], widen, 0, 0).astype(BF16)
        keys = jnp.concatenate([key, near[:HEAD_DIM]], axis=1)
        values = jnp.concatenate([value, near[HEAD_DIM:]], axis=1)
        keys = jnp.concatenate([keys, blank], axis=0)
        values = jnp.concatenate([blank, values], axis=0)
        from_partner_far = one_hot((row < 2) & (column == row + 2 * head))
        from_own_far = one_hot((row >= 2) & (row < 4) & (column == row - 2 + 2 * head))
        chosen = mm(from_partner_far, partner_ref[first_far:], 1, 0)
        chosen = (chosen + mm(from_own_far, own_ref[first_far:], 1, 0)).astype(BF16)
        in_near = here & same_class(place, offset, RC)
        extra = jnp.where(here & same_class(place, offset, RB), 1.0, 0.0)
        extra = extra + jnp.where(in_near, 1.0, 0.0)
        mask_here = jnp.where(place < TOKENS_HERE + NEAR, jnp.log(1.0 + extra), ABSENT)
        mask = jnp.where(from_here, mask_here, ABSENT)
        mask = jnp.where(from_partner & in_near, 0.0, mask)
        rows_ref[block] = chosen
        scores_ref[block] = mm(chosen, keys, 1, 0) * SCORE_SCALE + mask
        grad_probs_ref[block] = mm(chosen, values, 1, 0)
        keys_ref[head] = keys
        for pair in range(3):
            chooser_ref[head, pair] = far_chooser(offset, pair)
        spread = mm(partner_ref[block], near_chooser(offset), 0, 0)
        grad_key_ref[rows] = local_key_ref[rows] + spread[:HEAD_DIM]
        grad_value_ref[rows] = local_value_ref[rows] + spread[HEAD_DIM:]


def final_kernel(
    rows_ref,
    scores_ref,
    grad_probs_ref,
    keys_ref,
    chooser_ref,
    local_query_ref,
    local_key_ref,
    local_value_ref,
    slots_ref,
    grad_query_ref,
    grad_key_ref,
    grad_value_ref,
    grad_weight_ref,
):
    heads = local_query_ref.shape[0] // HEAD_DIM
    half = grad_weight_ref.shape[1] // 2
    chunks = pl.cdiv(half, CHUNK)
    eye = one_hot(iota((LANES, LANES), 0) == iota((LANES, LANES), 1))
    for head in range(heads):
        rows = slice(head * HEAD_DIM, (head + 1) * HEAD_DIM)
        block = slice(head * GAP, (head + 1) * GAP)
        pieces = [slots_ref[head * chunks + chunk].astype(F32) for chunk in range(chunks)]
        folded = jnp.concatenate([piece[:CHUNK] for piece in pieces], axis=0)[:half]
        unfolded = mm(eye, folded.astype(BF16), 1, 1)
        grad_weight_ref[rows, :half] = unfolded[:HEAD_DIM]
        grad_weight_ref[rows, half:] = unfolded[HEAD_DIM:]

        returned = jnp.concatenate(
            [pieces[0][CHUNK:], jnp.zeros((GAP - SMALL, LANES), F32)], axis=0
        )
        chosen = rows_ref[block]
        start = jnp.where(iota(returned.shape, 0) < 2, 0, HEAD_DIM)
        normalizer, delta = (take_stat(returned, start, index) for index in range(2))
        probs = jnp.exp(scores_ref[block] - normalizer)
        grad_scores = (probs * (grad_probs_ref[block] - delta)).astype(BF16)
        probs_low = probs[:, :TOKENS_HERE].astype(BF16)
        far_query = (returned + mm(grad_scores, keys_ref[head], 1, 1)).astype(BF16)
        returned = returned.astype(BF16)
        grad_query = mm(far_query, chooser_ref[head, 1], 0, 0)[:HEAD_DIM]
        grad_key = mm(returned, chooser_ref[head, 2], 0, 0)[:HEAD_DIM]
        grad_key = grad_key + mm(chosen, grad_scores[:, :TOKENS_HERE], 0, 0)[:HEAD_DIM]
        grad_value = mm(returned, chooser_ref[head, 0], 0, 0)[HEAD_DIM:]
        grad_value = grad_value + mm(chosen, probs_low, 0, 0)[HEAD_DIM:]
        grad_query = (local_query_ref[rows] + grad_query) * SCORE_SCALE
        grad_key = (local_key_ref[rows] + grad_key) * SCORE_SCALE
        grad_query_ref[rows] = grad_query.astype(BF16)
        grad_key_ref[rows] = grad_key.astype(BF16)
        grad_value_ref[rows] = (local_value_ref[rows] + grad_value).astype(BF16)


def call(kernel, outs, arrays, scalars=0, scratch=(), space=pltpu.VMEM, limit=40 << 20):
    specs = [pl.BlockSpec(memory_space=pltpu.SMEM)] * scalars
    specs = specs + [pl.BlockSpec(memory_space=space)] * (len(arrays) - scalars)
    shapes = [jax.ShapeDtypeStruct(shape, dtype) for shape, dtype in outs]
    return pl.pallas_call(
        kernel,
        out_shape=shapes,
        in_specs=specs,
        out_specs=[pl.BlockSpec(memory_space=pltpu.VMEM)] * len(shapes),
        scratch_shapes=list(scratch),
        compiler_params=pltpu.CompilerParams(vmem_limit_bytes=limit),
        name=kernel.__name__,
    )(*arrays)


def local(queries, keys, values, grad_out, out_weight, offsets):
    features = queries.shape[0]
    model = out_weight.shape[1]
    heads = offsets.shape[0]
    sources = lax.axis_size("xz")
    near_shape = ((heads * NEAR + GAP, LANES), BF16)
    back_shape = ((heads * NEAR + GAP, LANES), BF16)
    slots_shape = ((sources, SLOT, LANES), BF16)
    merged_shape = ((PLANES, SLOT + sources * SMALL, LANES), BF16)
    wide_shape = ((features, TOKENS_HERE), F32)
    grad_shape = ((features, TOKENS_HERE), BF16)
    block_shape = ((heads * GAP, TOKENS_HERE + LANES), F32)
    other = [(i, i ^ 1) for i in range(PLANES)]

    scratch = [
        pltpu.SMEM(offsets.shape, offsets.dtype),
        pltpu.VMEM(keys.shape, keys.dtype),
        pltpu.VMEM(values.shape, values.dtype),
        pltpu.SemaphoreType.DMA((3,)),
    ]
    other_grad = lax.ppermute(grad_out, "chip", [(0, 1), (1, 0)])
    (near,) = call(
        near_kernel,
        [near_shape],
        tuple(pltpu.with_memory_space_constraint(x, pltpu.HBM) for x in (offsets, keys, values)),
        scratch=scratch,
        space=pltpu.HBM,
        limit=LIMIT,
    )
    near = lax.ppermute(near, "yh", other)
    pair_grads = lax.all_gather(jnp.stack([grad_out, other_grad]), "core", axis=0, tiled=True)
    side = lax.axis_index("chip").reshape(1)
    slots, dout, stats = call(
        local_kernel,
        [slots_shape, grad_shape, ((heads * SMALL, TOKENS_HERE), F32)],
        (side, queries, keys, values, pair_grads, out_weight, near),
        scalars=1,
    )
    slots = lax.all_to_all(slots, "xz", 0, 0, tiled=True)
    own, local_query, local_key, local_value = call(
        local_grad_kernel,
        [back_shape, wide_shape, wide_shape, wide_shape],
        (queries, keys, values, dout, stats, near),
    )
    partner = lax.ppermute(own, "yh", other)
    prepared = call(
        prepare_kernel,
        [
            ((heads * GAP, LANES), BF16),
            block_shape,
            block_shape,
            ((heads, LANES, TOKENS_HERE + LANES), BF16),
            ((heads, 3, GAP, TOKENS_HERE), BF16),
            wide_shape,
            wide_shape,
        ],
        (keys, values, near, own, partner, local_key, local_value),
    )
    plane = lax.axis_index("yh").reshape(1)
    slots, prepared, local_query, plane = lax.optimization_barrier(
        (slots, prepared, local_query, plane)
    )
    rows, scores, grad_probs, wide_keys, chooser, local_key, local_value = prepared
    (merged,) = call(
        merge_kernel,
        [merged_shape],
        (slots,),
        scratch=[pltpu.VMEM((sources * SMALL, LANES), F32)],
    )
    merged = lax.all_to_all(merged, "yh", 0, 0, tiled=True)
    (slots,) = call(
        far_kernel,
        [slots_shape],
        (plane, merged),
        scalars=1,
        scratch=[pltpu.VMEM((3, PLANES * sources * 2, LANES), F32)],
    )
    slots = lax.all_to_all(slots, "xz", 0, 0, tiled=True)
    return tuple(
        call(
            final_kernel,
            [grad_shape, grad_shape, grad_shape, ((features, model), F32)],
            (
                rows,
                scores,
                grad_probs,
                wide_keys,
                chooser,
                local_query,
                local_key,
                local_value,
                slots,
            ),
        )
    )


def solution(mesh):
    devices = mesh.devices.reshape(-1, PLANES, 2, mesh.devices.shape[1] // 2)
    split_mesh = Mesh(devices, ("xz", "yh", "chip", "core"))
    parts = ("chip", "core")
    wide = P(parts, ("xz", "yh"))
    return jax.shard_map(
        local,
        mesh=split_mesh,
        in_specs=(wide, wide, wide, wide, P(parts, None), P(parts)),
        out_specs=(wide, wide, wide, P(parts, None)),
        check_vma=False,
    )
```
